32 devices in a mesh: dp: 8 (over z, y), mp: 4 (over x, core).
Axes of the slice: x: 2, y: 2, z: 4, core: 2. Of those that a mesh axis runs over, the one named last changes fastest.
Arguments:
- patches: bfloat16 [8192, 1024], P('dp')
- cotangent: bfloat16 [8192, 512], P('dp')
- item_lengths: int32 [8, 8], P('dp'), may hold values from 0 to 784, as said below
- enc_master: float32 [1024, 12800], P('dp', 'mp')
- dec_master: float32 [512, 6144], P('dp', 'mp')
- enc_norms: float32 [4, 1024], P(None, 'dp')
- dec_norms: float32 [4, 512], P(None, 'dp')
- enc_moment: float32 [1024, 12800], P('dp', 'mp')
- dec_moment: float32 [512, 6144], P('dp', 'mp')
- enc_norm_moment: float32 [4, 1024], P(None, 'dp')
- dec_norm_moment: float32 [4, 512], P(None, 'dp')
Outputs:
- block_out: float32 [8192, 512], P('dp')
- input_grad: float32 [8192, 1024], P('dp')
- enc_grad: float32 [1024, 12800], P('dp', 'mp')
- dec_grad: float32 [512, 6144], P('dp', 'mp')
- enc_norm_grad: float32 [4, 1024], P(None, 'dp')
- dec_norm_grad: float32 [4, 512], P(None, 'dp')
- dec_shift_grad: float32 [512], P('dp')
- enc_moment_new: float32 [1024, 12800], P('dp', 'mp')
- dec_moment_new: float32 [512, 6144], P('dp', 'mp')
- enc_norm_moment_new: float32 [4, 1024], P(None, 'dp')
- dec_norm_moment_new: float32 [4, 512], P(None, 'dp')
- enc_master_new: float32 [1024, 12800], P('dp', 'mp')
- dec_master_new: float32 [512, 6144], P('dp', 'mp')
- enc_norms_new: float32 [4, 1024], P(None, 'dp')
- dec_norms_new: float32 [4, 512], P(None, 'dp')
- enc_copy: bfloat16 [1024, 12800], P('dp', 'mp')
- dec_copy: bfloat16 [512, 6144], P('dp', 'mp')
- enc_norms_copy: bfloat16 [4, 1024], P(None, 'dp')
- dec_norms_copy: bfloat16 [4, 512], P(None, 'dp')
- grad_norm: float32 [], replicated
The draws below stay inside these ranges and needn't reach their ends.
Inputs may be any that keep to these rules, and one draw needn't show every extreme that they name: `item_lengths`: row r lists the items placed on index r of dp: each entry is 64, 196, 784 or 0, the zeros after all nonzero entries, and a row sums to at most 1024; the last row always holds an item of 784 patches.
All inputs are finite; a program needn't handle non-finite values.
Results may differ from the reference program's by a relative error of at most 0.029.
Values may be sent and summed in bfloat16 or wider, within the bound.
No kernel may reach another device: no remote copies, remote signals or barrier semaphores. Data moves between devices by JAX's collectives and lax.ppermute only.
A program may use at most 192 MiB of HBM per device.

```python
import math
import jax
import jax.numpy as jnp
from jax import lax

D = 1024
H = 16
HD = 64
FF = 4096
DD = 512
DH = 16
DHD = 32
DFF = 2048
CAP = 1024
SLOTS = 8
ITEM_S = 64
ITEM_M = 196
ITEM_L = 784
NS_STEPS = 5
TOKENS = 8192
ENC_COLS = 12800
DEC_COLS = 6144
N_DP = 8
N_MP = 4


def piece_scales(widths, fans, ranks):
    block_width = sum(widths) // ranks
    within = jnp.arange(block_width * ranks) % block_width
    scales = jnp.zeros((block_width * ranks,), jnp.float32)
    start_col = 0
    for piece_width, fan_in in zip(widths, fans):
        stop_col = start_col + piece_width // ranks
        scales = scales + jnp.where((within >= start_col) & (within < stop_col), fan_in ** (-0.5), 0.0)
        start_col = stop_col
    return scales


def last_piece_flag(widths, ranks):
    block_width = sum(widths) // ranks
    within = jnp.arange(block_width * ranks) % block_width
    return within >= block_width - widths[-1] // ranks


def feature_ramp(width, top):
    position = jnp.arange(width, dtype=jnp.float32) / (width - 1)
    return 2.0 / (1.0 + top) * (1.0 + (top - 1.0) * position)


def parameter_count():
    return D * ENC_COLS + DD * DEC_COLS + 4 * D + 4 * DD


def norm_rows(key, width, base, rise):
    gain_key, shift_key = jax.random.split(key)
    ramp = base * (1.0 + rise * jnp.arange(width, dtype=jnp.float32) / (width - 1))
    gains = ramp[None, :] * jax.random.uniform(gain_key, (2, width), jnp.float32, 0.9, 1.07)
    shifts = jax.random.uniform(shift_key, (2, width), jnp.float32, -0.45, 0.45)
    return jnp.stack([gains[0], shifts[0], gains[1], shifts[1]])


def draw_patches(key, part):
    key = jax.random.fold_in(key, 21)
    noise = jnp.clip(jax.random.normal(key, (TOKENS, D), jnp.float32), -4.0, 4.0)
    return (noise * feature_ramp(D, 3.0)[None, :]).astype(jnp.bfloat16)


def draw_cotangent(key, part):
    key = jax.random.fold_in(key, 22)
    noise = jnp.clip(jax.random.normal(key, (TOKENS, DD), jnp.float32), -4.0, 4.0)
    return (noise * feature_ramp(DD, 3.0)[None, :]).astype(jnp.bfloat16)


def draw_enc_master(key, part):
    key = jax.random.fold_in(key, 11)
    widths = [3 * D, D, FF, FF, DD]
    noise = jax.random.normal(key, (D, ENC_COLS), jnp.float32)
    ramp = feature_ramp(D, 3.0)
    row_factor = jnp.where(last_piece_flag(widths, N_MP)[None, :], ramp[:, None], 1.0)
    return noise * piece_scales(widths, [D // 4, D // 16, D // 4, FF, D], N_MP)[None, :] * row_factor


def draw_dec_master(key, part):
    key = jax.random.fold_in(key, 12)
    noise = jax.random.normal(key, (DD, DEC_COLS), jnp.float32)
    return noise * piece_scales([3 * DD, DD, DFF, DFF], [DD // 4, DD // 16, DD // 4, DFF], N_MP)[None, :]


def draw_enc_norms(key, part):
    key = jax.random.fold_in(key, 13)
    return norm_rows(key, D, 0.28, 2.0)


def draw_dec_norms(key, part):
    key = jax.random.fold_in(key, 14)
    return norm_rows(key, DD, 0.28, 2.0)


def draw_enc_moment(key, part):
    key = jax.random.fold_in(key, 15)
    return jax.random.normal(key, (D, ENC_COLS), jnp.float32) * (100.0 / math.sqrt(parameter_count()))


def draw_dec_moment(key, part):
    key = jax.random.fold_in(key, 16)
    return jax.random.normal(key, (DD, DEC_COLS), jnp.float32) * (100.0 / math.sqrt(parameter_count()))


def draw_enc_norm_moment(key, part):
    key = jax.random.fold_in(key, 17)
    return jax.random.normal(key, (4, D), jnp.float32) * (300.0 / math.sqrt(parameter_count()))


def draw_dec_norm_moment(key, part):
    key = jax.random.fold_in(key, 18)
    return jax.random.normal(key, (4, DD), jnp.float32) * (300.0 / math.sqrt(parameter_count()))


def draw_item_lengths(key, part):
    key = jax.random.fold_in(key, 19)
    layouts = [[ITEM_L, ITEM_M], [ITEM_L, ITEM_S, ITEM_S, ITEM_S], [ITEM_M] * 5, [ITEM_M] * 4 + [ITEM_S] * 3, [ITEM_L, ITEM_S], [ITEM_M] + [ITEM_S] * 7, [ITEM_M, ITEM_M, ITEM_S, ITEM_S]]
    table = jnp.array([row + [0] * (SLOTS - len(row)) for row in layouts], jnp.int32)
    pick_key, last_key, order_key = jax.random.split(key, 3)
    picks = jax.random.randint(pick_key, (N_DP,), 0, 7)
    last_pick = jnp.array([0, 1, 4], jnp.int32)[jax.random.randint(last_key, (), 0, 3)]
    picks = picks.at[N_DP - 1].set(last_pick)
    rows_all = table[picks]
    order_scores = jax.random.randint(order_key, (N_DP, SLOTS), 0, 1000) * SLOTS + jnp.arange(SLOTS)[None, :]
    order_scores = jnp.where(rows_all > 0, order_scores, (1 << 20) + jnp.arange(SLOTS)[None, :])
    order = jnp.argsort(order_scores, axis=1)
    return jnp.take_along_axis(rows_all, order, axis=1).astype(jnp.int32)


def setup_inputs(seed: int = 0) -> dict:
    arg_keys = jax.random.split(jax.random.key(seed), 12)
    return {
        "patches": draw_patches(jax.random.fold_in(arg_keys[11], 71), 0),
        "cotangent": draw_cotangent(jax.random.fold_in(arg_keys[11], 71), 0),
        "item_lengths": draw_item_lengths(jax.random.fold_in(arg_keys[11], 71), 0),
        "enc_master": draw_enc_master(jax.random.fold_in(arg_keys[11], 71), 0),
        "dec_master": draw_dec_master(jax.random.fold_in(arg_keys[11], 71), 0),
        "enc_norms": draw_enc_norms(jax.random.fold_in(arg_keys[11], 71), 0),
        "dec_norms": draw_dec_norms(jax.random.fold_in(arg_keys[11], 71), 0),
        "enc_moment": draw_enc_moment(jax.random.fold_in(arg_keys[11], 71), 0),
        "dec_moment": draw_dec_moment(jax.random.fold_in(arg_keys[11], 71), 0),
        "enc_norm_moment": draw_enc_norm_moment(jax.random.fold_in(arg_keys[11], 71), 0),
        "dec_norm_moment": draw_dec_norm_moment(jax.random.fold_in(arg_keys[11], 71), 0),
    }


highest = lax.Precision.HIGHEST
ln_eps = 1e-06
masked_score = -1e+30
newton_first = 3.4445
newton_second = -4.775
newton_third = 2.0315
momentum_keep = 0.5
clip_bound = 100.0
rate_enc = 0.2
rate_dec = 0.3
rate_norm = 1.0
decay_rate = 0.01

@jax.custom_vjp
def low(v):
    return lax.optimization_barrier(v.astype(jnp.bfloat16)).astype(jnp.float32)

@jax.custom_vjp
def low_back(v):
    return v

def low_keep(v):
    return (low(v), None)

def low_pass(kept, grad):
    return (grad,)

def back_keep(v):
    return (v, None)

def back_low(kept, grad):
    return (low(grad),)
low.defvjp(low_keep, low_pass)
low_back.defvjp(back_keep, back_low)

def layer_norm(values, gain_row, shift_row):
    center = values - lax.optimization_barrier(jnp.mean(values, axis=-1, keepdims=True))
    spread = lax.optimization_barrier(jnp.mean(center * center, axis=-1, keepdims=True))
    return center * lax.rsqrt(spread + ln_eps) * gain_row + shift_row

def segments_of(lengths, row_count):
    item_ends = jnp.cumsum(lengths).astype(jnp.int32)
    position = jnp.arange(row_count, dtype=jnp.int32)
    segment = lax.optimization_barrier(jnp.sum((position[:, None] >= item_ends[None, :]).astype(jnp.int32), axis=1)).astype(jnp.int32)
    live_mask = (position < item_ends[-1]).astype(jnp.float32)
    return (segment, live_mask)

def attend(query_part, key_part, value_part, segment, head_count, head_width):
    row_count = query_part.shape[0]
    query_heads = query_part.reshape(row_count, head_count, head_width)
    key_heads = key_part.reshape(row_count, head_count, head_width)
    value_heads = value_part.reshape(row_count, head_count, head_width)
    scores = low_back(jnp.einsum('qhd,khd->hqk', query_heads, key_heads, precision=highest) * head_width ** (-0.5))
    same = (segment[:, None] == segment[None, :])[None]
    scores = jnp.where(same, scores, masked_score)
    attention = jax.nn.softmax(scores, axis=-1)
    heads_out = jnp.einsum('hqk,khd->qhd', low(attention), value_heads, precision=highest)
    return heads_out.reshape(row_count, head_count * head_width)

def residual_block(values, segment, weights, norm_values, head_count, head_width, hidden_width):
    group_cols = weights.shape[1] // N_MP
    inner_width = head_count * head_width // N_MP
    local_heads = head_count // N_MP
    hidden_part = hidden_width // N_MP
    normed = low(layer_norm(values, norm_values[0], norm_values[1]))
    attended = jnp.zeros_like(values)
    for group_rank in range(N_MP):
        group_piece = weights[:, group_rank * group_cols:(group_rank + 1) * group_cols]
        mixed_all = jnp.dot(low_back(normed), group_piece[:, :3 * inner_width], precision=highest)
        query_part = low_back(low(mixed_all[:, :inner_width]))
        key_part = low_back(low(mixed_all[:, inner_width:2 * inner_width]))
        value_part = low_back(low(mixed_all[:, 2 * inner_width:3 * inner_width]))
        heads_out = low_back(low(attend(query_part, key_part, value_part, segment, local_heads, head_width)))
        out_proj = group_piece[:, 3 * inner_width:4 * inner_width]
        attended = attended + low_back(low(jnp.dot(heads_out, out_proj.T, precision=highest)))
    middle = values + attended
    normed_two = low(layer_norm(middle, norm_values[2], norm_values[3]))
    fed_out = jnp.zeros_like(values)
    for group_rank in range(N_MP):
        group_piece = weights[:, group_rank * group_cols:(group_rank + 1) * group_cols]
        up_proj = group_piece[:, 4 * inner_width:4 * inner_width + hidden_part]
        down_proj = group_piece[:, 4 * inner_width + hidden_part:4 * inner_width + 2 * hidden_part]
        hidden = low_back(jnp.dot(low_back(normed_two), up_proj, precision=highest))
        activated = low(jax.nn.gelu(hidden, approximate=False))
        fed_out = fed_out + low_back(low(jnp.dot(activated, down_proj.T, precision=highest)))
    return middle + fed_out

def forward(values, segment, enc_weights, dec_weights, enc_norm_values, dec_norm_values):
    encoded = residual_block(values, segment, enc_weights, enc_norm_values, H, HD, FF)
    encoded_low = low(encoded)
    group_cols = enc_weights.shape[1] // N_MP
    bridge_start = 4 * (D // N_MP) + 2 * (FF // N_MP)
    bridged = []
    for group_rank in range(N_MP):
        bridge = enc_weights[:, group_rank * group_cols + bridge_start:(group_rank + 1) * group_cols]
        bridged.append(low_back(low(jnp.dot(low_back(encoded_low), bridge, precision=highest))))
    decoder_in = jnp.concatenate(bridged, axis=1)
    return residual_block(decoder_in, segment, dec_weights, dec_norm_values, DH, DHD, DFF)

def orthogonalize(matrix):
    gram = jnp.dot(matrix, matrix.T, precision=highest)
    norm_size = jnp.sqrt(jnp.trace(gram)) + 1e-07
    iterate = matrix / norm_size
    gram = gram / (norm_size * norm_size)
    for newton_step in range(NS_STEPS):
        if newton_step > 0:
            gram = jnp.dot(iterate, iterate.T, precision=highest)
        mix_matrix = newton_second * gram + newton_third * jnp.dot(gram, gram, precision=highest)
        iterate = newton_first * iterate + jnp.dot(mix_matrix, iterate, precision=highest)
    return iterate

def muon_update(moment, master, widths, model_width, rate):
    group_cols = moment.shape[1] // N_MP
    updates = []
    start_col = 0
    for piece_width in widths:
        whole_matrix = jnp.concatenate([moment[:, group_rank * group_cols + start_col:group_rank * group_cols + start_col + piece_width] for group_rank in range(N_MP)], axis=1)
        updates.append(orthogonalize(whole_matrix) * (0.2 * math.sqrt(max(model_width, piece_width * N_MP))))
        start_col += piece_width
    pieces = []
    for group_rank in range(N_MP):
        for update_part, piece_width in zip(updates, widths):
            pieces.append(update_part[:, group_rank * piece_width:(group_rank + 1) * piece_width])
    step_all = jnp.concatenate(pieces, axis=1)
    return master * (1.0 - rate * decay_rate) - rate * step_all

def reference(patches, cotangent, item_lengths, enc_master, dec_master, enc_norms, dec_norms, enc_moment, dec_moment, enc_norm_moment, dec_norm_moment):
    enc_weights = enc_master.astype(jnp.bfloat16).astype(jnp.float32)
    dec_weights = dec_master.astype(jnp.bfloat16).astype(jnp.float32)
    enc_norm_low = enc_norms.astype(jnp.bfloat16).astype(jnp.float32)
    dec_norm_low = dec_norms.astype(jnp.bfloat16).astype(jnp.float32)

    def per_device(totals, device_inputs):
        device_values, device_back, lengths = device_inputs
        segment, live_mask = segments_of(lengths, CAP)

        def run_device(values, enc_w, dec_w, enc_n, dec_n):
            return forward(values, segment, enc_w, dec_w, enc_n, dec_n)
        output, pull = jax.vjp(run_device, device_values.astype(jnp.float32), enc_weights, dec_weights, enc_norm_low, dec_norm_low)
        grads = pull(device_back.astype(jnp.float32) * live_mask[:, None])
        totals = tuple((total + part for total, part in zip(totals, grads[1:])))
        return (totals, (output, grads[0]))
    zeros = (jnp.zeros_like(enc_weights), jnp.zeros_like(dec_weights), jnp.zeros_like(enc_norm_low), jnp.zeros_like(dec_norm_low))
    totals, (outputs, input_grads) = lax.scan(per_device, zeros, (patches.reshape(N_DP, CAP, D), cotangent.reshape(N_DP, CAP, DD), item_lengths))
    squares = jnp.sum(totals[0] * totals[0]) + jnp.sum(totals[1] * totals[1]) + jnp.sum(totals[2] * totals[2]) + jnp.sum(totals[3] * totals[3])
    grad_norm = jnp.sqrt(squares)
    factor = clip_bound * lax.rsqrt(squares + 1e-06)
    enc_grad = totals[0] * factor
    dec_grad = totals[1] * factor
    enc_norm_grad = totals[2] * factor
    dec_norm_grad = totals[3] * factor
    dec_shift_grad = dec_norm_grad[3]
    enc_moment_new = momentum_keep * enc_moment + enc_grad
    dec_moment_new = momentum_keep * dec_moment + dec_grad
    enc_norm_moment_new = momentum_keep * enc_norm_moment + enc_norm_grad
    dec_norm_moment_new = momentum_keep * dec_norm_moment + dec_norm_grad
    enc_widths = [3 * D // N_MP, D // N_MP, FF // N_MP, FF // N_MP, DD // N_MP]
    dec_widths = [3 * DD // N_MP, DD // N_MP, DFF // N_MP, DFF // N_MP]
    enc_master_new = muon_update(enc_moment_new, enc_master, enc_widths, D, rate_enc)
    dec_master_new = muon_update(dec_moment_new, dec_master, dec_widths, DD, rate_dec)
    enc_norms_new = enc_norms - rate_norm * enc_norm_moment_new
    dec_norms_new = dec_norms - rate_norm * dec_norm_moment_new
    return (outputs.reshape(TOKENS, DD), input_grads.reshape(TOKENS, D), enc_grad, dec_grad, enc_norm_grad, dec_norm_grad, dec_shift_grad, enc_moment_new, dec_moment_new, enc_norm_moment_new, dec_norm_moment_new, enc_master_new, dec_master_new, enc_norms_new, dec_norms_new, enc_master_new.astype(jnp.bfloat16), dec_master_new.astype(jnp.bfloat16), enc_norms_new.astype(jnp.bfloat16), dec_norms_new.astype(jnp.bfloat16), grad_norm)
```

```python
import math

import jax
import jax.numpy as jnp
from jax import lax
from jax.sharding import PartitionSpec as P

D = 1024
HD = 64
FF = 4096
DD = 512
DHD = 32
DFF = 2048
NS_STEPS = 5


highest = lax.Precision.HIGHEST
ln_eps = 1e-06
masked_score = -1e30
newton_first = 3.4445
newton_second = -4.775
newton_third = 2.0315
momentum_keep = 0.5
clip_bound = 100.0
rate_enc = 0.2
rate_dec = 0.3
rate_norm = 1.0
decay_rate = 0.01


def shortened(array):

    def short(part):
        return part.astype(jnp.bfloat16) if part.dtype == jnp.float32 else part

    return jax.tree.map(short, array)


def layer_norm(values, gain_row, shift_row):
    center = values - jnp.mean(values, axis=-1, keepdims=True)
    spread = jnp.mean(center * center, axis=-1, keepdims=True)
    return center * lax.rsqrt(spread + ln_eps) * gain_row + shift_row


def exact_gelu(hidden_in):
    return jax.nn.gelu(hidden_in, approximate=False)


def model_sum(partial_term):
    share = lax.psum_scatter(
        partial_term.astype(jnp.bfloat16), "mp", scatter_dimension=0, tiled=True
    ).astype(jnp.float32)
    return lax.all_gather(share.astype(jnp.bfloat16), "mp", axis=0, tiled=True).astype(share.dtype)


def model_back(partial_term):
    share = lax.psum_scatter(
        partial_term.astype(jnp.bfloat16), "mp", scatter_dimension=0, tiled=True
    ).astype(jnp.float32)
    return lax.all_gather(share.astype(jnp.bfloat16), "mp", axis=0, tiled=True).astype(share.dtype)


def segments_of(lengths, row_count):
    item_ends = jnp.cumsum(lengths)
    position = jnp.arange(row_count, dtype=jnp.int32)
    segment = jnp.sum((position[:, None] >= item_ends[None, :]).astype(jnp.int32), axis=1)
    live_mask = (position < item_ends[-1]).astype(jnp.float32)
    return (segment, live_mask)


def split_columns(whole_cols, widths):
    pieces = []
    start_col = 0
    for piece_width in widths:
        pieces.append(whole_cols[:, start_col : start_col + piece_width])
        start_col += piece_width
    return pieces


def attend_forward(query_part, key_part, value_part, segment, head_count, head_width, block_rows):
    row_count = query_part.shape[0]
    blocks = row_count // block_rows
    score_scale = head_width ** (-0.5)
    key_heads = key_part.reshape(row_count, head_count, head_width)
    value_heads = value_part.reshape(row_count, head_count, head_width)
    query_blocks = query_part.reshape(blocks, block_rows, head_count, head_width)
    segment_blocks = segment.reshape(blocks, block_rows)

    def attend_block(block_inputs):
        query_block, segment_block = block_inputs
        scores = (
            jnp.einsum("qhd,khd->hqk", query_block, key_heads, preferred_element_type=jnp.float32)
            * score_scale
        )
        scores = jnp.where((segment_block[:, None] == segment[None, :])[None], scores, masked_score)
        row_max = jnp.max(scores, axis=-1, keepdims=True)
        shifted = jnp.exp(scores - row_max)
        row_total = jnp.sum(shifted, axis=-1, keepdims=True)
        attention = (shifted / row_total).astype(jnp.bfloat16)
        block_out = jnp.einsum(
            "hqk,khd->qhd", attention, value_heads, preferred_element_type=jnp.float32
        )
        return (block_out.astype(jnp.bfloat16), row_max + jnp.log(row_total))

    block_outs, logsum = lax.map(attend_block, (query_blocks, segment_blocks))
    return (block_outs.reshape(row_count, head_count * head_width), logsum)


def attend_backward(
    heads_grad,
    query_part,
    key_part,
    value_part,
    segment,
    logsum,
    head_count,
    head_width,
    block_rows,
):
    row_count = query_part.shape[0]
    blocks = row_count // block_rows
    score_scale = head_width ** (-0.5)
    key_heads = key_part.reshape(row_count, head_count, head_width)
    value_heads = value_part.reshape(row_count, head_count, head_width)
    query_blocks = query_part.reshape(blocks, block_rows, head_count, head_width)
    grad_blocks = heads_grad.reshape(blocks, block_rows, head_count, head_width)
    segment_blocks = segment.reshape(blocks, block_rows)

    def backward_block(carried, block_inputs):
        key_total, value_total = carried
        query_block, grad_block, segment_block, logsum_block = block_inputs
        scores = (
            jnp.einsum("qhd,khd->hqk", query_block, key_heads, preferred_element_type=jnp.float32)
            * score_scale
        )
        scores = jnp.where((segment_block[:, None] == segment[None, :])[None], scores, masked_score)
        attention = jnp.exp(scores - logsum_block)
        grad_soft = jnp.einsum(
            "qhd,khd->hqk", grad_block, value_heads, preferred_element_type=jnp.float32
        )
        row_dot = jnp.sum(attention * grad_soft, axis=-1, keepdims=True)
        score_grad = (attention * (grad_soft - row_dot)).astype(jnp.bfloat16)
        query_grad = (
            jnp.einsum("hqk,khd->qhd", score_grad, key_heads, preferred_element_type=jnp.float32)
            * score_scale
        )
        key_total = (
            key_total
            + jnp.einsum(
                "hqk,qhd->khd", score_grad, query_block, preferred_element_type=jnp.float32
            )
            * score_scale
        )
        value_total = value_total + jnp.einsum(
            "hqk,qhd->khd",
            attention.astype(jnp.bfloat16),
            grad_block,
            preferred_element_type=jnp.float32,
        )
        return ((key_total, value_total), query_grad.astype(jnp.bfloat16))

    zeros = jnp.zeros((row_count, head_count, head_width), jnp.float32)
    (key_total, value_total), query_grads = lax.scan(
        backward_block, (zeros, zeros), (query_blocks, grad_blocks, segment_blocks, logsum)
    )
    return (
        query_grads.reshape(row_count, head_count * head_width),
        key_total.reshape(row_count, head_count * head_width).astype(jnp.bfloat16),
        value_total.reshape(row_count, head_count * head_width).astype(jnp.bfloat16),
    )


def block_forward(values, segment, pieces, norm_values, head_width, block_rows):
    qkv_proj, out_proj, up_proj, down_proj = pieces
    inner_width = out_proj.shape[1]
    head_count = inner_width // head_width
    normed_half = layer_norm(values, norm_values[0], norm_values[1]).astype(jnp.bfloat16)
    mixed_all = jnp.dot(normed_half, qkv_proj, preferred_element_type=jnp.float32)
    query_part = mixed_all[:, :inner_width].astype(jnp.bfloat16)
    key_part = mixed_all[:, inner_width : 2 * inner_width].astype(jnp.bfloat16)
    value_part = mixed_all[:, 2 * inner_width :].astype(jnp.bfloat16)
    heads_out, logsum = attend_forward(
        query_part, key_part, value_part, segment, head_count, head_width, block_rows
    )
    middle = values + model_sum(
        jnp.einsum("ti,di->td", heads_out, out_proj, preferred_element_type=jnp.float32)
    )
    normed_two = layer_norm(middle, norm_values[2], norm_values[3]).astype(jnp.bfloat16)
    hidden = jnp.dot(normed_two, up_proj, preferred_element_type=jnp.float32)
    activated = exact_gelu(hidden).astype(jnp.bfloat16)
    output = middle + model_sum(
        jnp.einsum("tf,df->td", activated, down_proj, preferred_element_type=jnp.float32)
    )
    return (
        output,
        (
            normed_half,
            query_part,
            key_part,
            value_part,
            heads_out,
            logsum,
            middle,
            normed_two,
            hidden,
            activated,
        ),
    )


def block_backward(upstream, saved, values, pieces, norm_values, segment, head_width, block_rows):
    (
        normed_half,
        query_part,
        key_part,
        value_part,
        heads_out,
        logsum,
        middle,
        normed_two,
        hidden,
        activated,
    ) = saved
    qkv_proj, out_proj, up_proj, down_proj = pieces
    inner_width = out_proj.shape[1]
    head_count = inner_width // head_width
    upstream_half = upstream.astype(jnp.bfloat16)
    down_grad = jnp.einsum(
        "td,tf->df", upstream_half, activated, preferred_element_type=jnp.float32
    )
    act_grad = jnp.einsum("td,df->tf", upstream_half, down_proj, preferred_element_type=jnp.float32)
    gelu_pull = jax.vjp(exact_gelu, hidden)[1]
    hidden_half = gelu_pull(act_grad)[0].astype(jnp.bfloat16)
    up_grad = jnp.einsum("td,tf->df", normed_two, hidden_half, preferred_element_type=jnp.float32)
    normed_two_grad = model_back(
        jnp.einsum("tf,df->td", hidden_half, up_proj, preferred_element_type=jnp.float32)
    )
    second_pull = jax.vjp(layer_norm, middle, norm_values[2], norm_values[3])[1]
    middle_part, gain_two, shift_two = second_pull(normed_two_grad)
    middle_grad = upstream + middle_part
    middle_half = middle_grad.astype(jnp.bfloat16)
    out_grad = jnp.einsum("td,ti->di", middle_half, heads_out, preferred_element_type=jnp.float32)
    heads_grad = jnp.einsum(
        "td,di->ti", middle_half, out_proj, preferred_element_type=jnp.float32
    ).astype(jnp.bfloat16)
    query_grad, key_grad, value_grad = attend_backward(
        heads_grad,
        query_part,
        key_part,
        value_part,
        segment,
        logsum,
        head_count,
        head_width,
        block_rows,
    )
    mixed_grad = jnp.concatenate([query_grad, key_grad, value_grad], axis=1)
    qkv_grad = jnp.einsum("td,tf->df", normed_half, mixed_grad, preferred_element_type=jnp.float32)
    normed_grad = model_back(
        jnp.einsum("tf,df->td", mixed_grad, qkv_proj, preferred_element_type=jnp.float32)
    )
    first_pull = jax.vjp(layer_norm, values, norm_values[0], norm_values[1])[1]
    values_part, gain_one, shift_one = first_pull(normed_grad)
    return (
        middle_grad + values_part,
        [qkv_grad, out_grad, up_grad, down_grad],
        jnp.stack([gain_one, shift_one, gain_two, shift_two]),
    )


def gram_newton(gram):
    total = None
    for newton_step in range(NS_STEPS):
        gram_half = gram.astype(jnp.bfloat16)
        square = jnp.dot(gram_half, gram_half, preferred_element_type=jnp.float32)
        mix_matrix = newton_second * gram + newton_third * square
        mix_half = mix_matrix.astype(jnp.bfloat16)
        if total is None:
            total = newton_first * jnp.eye(gram.shape[0], dtype=jnp.float32) + mix_matrix
        else:
            total = newton_first * total + jnp.dot(
                mix_half, total.astype(jnp.bfloat16), preferred_element_type=jnp.float32
            )
        if newton_step < NS_STEPS - 1:
            left = newton_first * gram + jnp.dot(
                mix_half, gram_half, preferred_element_type=jnp.float32
            )
            gram = newton_first * left + jnp.dot(
                left.astype(jnp.bfloat16), mix_half, preferred_element_type=jnp.float32
            )
    return total


def slot_rows(enc_rows_half, dec_rows_half, enc_widths, dec_widths, slot_width, data_ranks):
    enc_parts = split_columns(enc_rows_half, enc_widths)
    dec_parts = split_columns(dec_rows_half, dec_widths)
    half_width = slot_width // 2

    def widened(part, width):
        return jnp.pad(part, ((0, 0), (0, width - part.shape[1])))

    slots = [widened(part, slot_width) for part in enc_parts]
    for first in range(0, len(dec_parts), 2):
        upper = jnp.pad(widened(dec_parts[first], half_width), ((0, 0), (0, half_width)))
        lower = jnp.pad(widened(dec_parts[first + 1], half_width), ((0, 0), (half_width, 0)))
        slots.append(jnp.concatenate([upper, lower], axis=0))
    empty = jnp.zeros_like(slots[0])
    return jnp.stack(slots + [empty] * (data_ranks - len(slots)))


def unslot(rows_back, enc_widths, dec_widths, dec_rows):
    slot_width = rows_back.shape[2]
    enc_results = [rows_back[k][:, :width] for k, width in enumerate(enc_widths)]
    dec_results = []
    for place, width in enumerate(dec_widths):
        slot = rows_back[len(enc_widths) + place // 2]
        odd = place % 2
        dec_results.append(
            slot[
                odd * dec_rows : (odd + 1) * dec_rows,
                odd * (slot_width // 2) : odd * (slot_width // 2) + width,
            ]
        )
    return enc_results, dec_results


def apply_step(master, ortho_rows, widths, model_width, rate, model_ranks):
    steps_all = [
        orthogonal * (0.2 * math.sqrt(max(model_width, piece_width * model_ranks)))
        for orthogonal, piece_width in zip(ortho_rows, widths)
    ]
    return master * (1.0 - rate * decay_rate) - rate * jnp.concatenate(steps_all, axis=1)


def local(
    patches,
    cotangent,
    item_lengths,
    enc_master,
    dec_master,
    enc_norms,
    dec_norms,
    enc_moment,
    dec_moment,
    enc_norm_moment,
    dec_norm_moment,
):
    model_ranks = lax.axis_size("mp")
    data_ranks = lax.axis_size("dp")
    enc_widths = [
        3 * D // model_ranks,
        D // model_ranks,
        FF // model_ranks,
        FF // model_ranks,
        DD // model_ranks,
    ]
    dec_widths = [3 * DD // model_ranks, DD // model_ranks, DFF // model_ranks, DFF // model_ranks]
    enc_low, dec_low, enc_norm_low, dec_norm_low = (
        lax.all_gather(enc_master.astype(jnp.bfloat16), "dp", axis=0, tiled=True),
        lax.all_gather(dec_master.astype(jnp.bfloat16), "dp", axis=0, tiled=True),
        lax.all_gather(enc_norms.astype(jnp.bfloat16), "dp", axis=1, tiled=True),
        lax.all_gather(dec_norms.astype(jnp.bfloat16), "dp", axis=1, tiled=True),
    )
    enc_pieces = split_columns(enc_low, enc_widths)
    dec_pieces = split_columns(dec_low, dec_widths)
    enc_norm_values = enc_norm_low.astype(jnp.float32)
    dec_norm_values = dec_norm_low.astype(jnp.float32)
    row_count = patches.shape[0]
    block_rows = min(512, row_count)
    segment, live_mask = segments_of(item_lengths[0], row_count)
    inputs = patches.astype(jnp.float32)
    encoded, enc_saved = block_forward(
        inputs, segment, enc_pieces[:4], enc_norm_values, HD, block_rows
    )
    encoded_half = encoded.astype(jnp.bfloat16)
    bridge = enc_pieces[4]
    bridged = jnp.dot(encoded_half, bridge, preferred_element_type=jnp.float32).astype(jnp.bfloat16)
    joined = lax.all_gather(bridged, "mp", axis=1, tiled=True)
    decoder_in = joined.astype(jnp.float32)
    decoded, dec_saved = block_forward(
        decoder_in, segment, dec_pieces, dec_norm_values, DHD, block_rows
    )
    upstream = cotangent.astype(jnp.float32) * live_mask[:, None]
    dec_in_grad, dec_grads, dec_norm_grads = block_backward(
        upstream, dec_saved, decoder_in, dec_pieces, dec_norm_values, segment, DHD, block_rows
    )
    share_width = bridge.shape[1]
    bridge_in_grad = lax.dynamic_slice_in_dim(
        dec_in_grad, lax.axis_index("mp") * share_width, share_width, 1
    ).astype(jnp.bfloat16)
    bridge_grad = jnp.einsum(
        "td,tf->df", encoded_half, bridge_in_grad, preferred_element_type=jnp.float32
    )
    encoded_grad = model_back(
        jnp.einsum("tf,df->td", bridge_in_grad, bridge, preferred_element_type=jnp.float32)
    )
    input_grad, enc_grads, enc_norm_grads = block_backward(
        encoded_grad, enc_saved, inputs, enc_pieces[:4], enc_norm_values, segment, HD, block_rows
    )
    enc_sum_rows, dec_sum_rows, enc_norm_rows, dec_norm_rows = (
        lax.psum_scatter(
            shortened(jnp.concatenate(enc_grads + [bridge_grad], axis=1)),
            "dp",
            scatter_dimension=0,
            tiled=True,
        ).astype(jnp.float32),
        lax.psum_scatter(
            shortened(jnp.concatenate(dec_grads, axis=1)), "dp", scatter_dimension=0, tiled=True
        ).astype(jnp.float32),
        lax.psum_scatter(enc_norm_grads, "dp", scatter_dimension=1, tiled=True),
        lax.psum_scatter(dec_norm_grads, "dp", scatter_dimension=1, tiled=True),
    )
    local_sum = (
        jnp.sum(enc_sum_rows * enc_sum_rows)
        + jnp.sum(dec_sum_rows * dec_sum_rows)
        + (jnp.sum(enc_norm_rows * enc_norm_rows) + jnp.sum(dec_norm_rows * dec_norm_rows))
        / model_ranks
    )
    squares = lax.psum(local_sum, ("dp", "mp"))
    grad_norm = jnp.sqrt(squares)
    factor = clip_bound * lax.rsqrt(squares + 1e-06)
    enc_grad = enc_sum_rows * factor
    dec_grad = dec_sum_rows * factor
    enc_norm_grad = enc_norm_rows * factor
    dec_norm_grad = dec_norm_rows * factor
    dec_shift_grad = dec_norm_grad[3]
    enc_moment_new = momentum_keep * enc_moment + enc_grad
    dec_moment_new = momentum_keep * dec_moment + dec_grad
    enc_norm_moment_new = momentum_keep * enc_norm_moment + enc_norm_grad
    dec_norm_moment_new = momentum_keep * dec_norm_moment + dec_norm_grad
    slot_width = max(enc_widths)
    enc_rows = enc_master.shape[0]
    dec_rows = dec_master.shape[0]
    slots = slot_rows(
        enc_moment_new.astype(jnp.bfloat16),
        dec_moment_new.astype(jnp.bfloat16),
        enc_widths,
        dec_widths,
        slot_width,
        data_ranks,
    )
    own = lax.all_to_all(slots, "dp", 0, 0).reshape(data_ranks * enc_rows, slot_width)
    gram = lax.psum(
        lax.dot_general(
            own, own, (((1,), (1,)), ((), ())), preferred_element_type=jnp.float32
        ),
        "mp",
    )
    data_rank = lax.axis_index("dp")
    paired = jnp.logical_and(
        data_rank >= len(enc_widths), data_rank < len(enc_widths) + len(dec_widths) // 2
    )
    row_index = jnp.arange(gram.shape[0], dtype=jnp.int32)
    upper_row = (row_index % enc_rows) < dec_rows
    diagonal = jnp.sum(jnp.where(row_index[:, None] == row_index[None, :], gram, 0.0), axis=1)
    upper_trace = jnp.sum(jnp.where(upper_row, diagonal, 0.0))
    lower_trace = jnp.sum(jnp.where(upper_row, 0.0, diagonal))
    row_trace = jnp.where(
        paired, jnp.where(upper_row, upper_trace, lower_trace), upper_trace + lower_trace
    )
    row_scale = 1.0 / (jnp.sqrt(row_trace) + 1e-07)
    product = gram_newton(gram * row_scale[:, None] * row_scale[None, :])
    orthogonal = jnp.dot(
        (product * row_scale[None, :]).astype(jnp.bfloat16),
        own,
        preferred_element_type=jnp.float32,
    ).astype(jnp.bfloat16)
    rows_back = lax.all_to_all(
        orthogonal.reshape(data_ranks, enc_rows, slot_width), "dp", 0, 0
    ).astype(jnp.float32)
    enc_results, dec_results = unslot(rows_back, enc_widths, dec_widths, dec_rows)
    enc_master_new = apply_step(enc_master, enc_results, enc_widths, D, rate_enc, model_ranks)
    dec_master_new = apply_step(dec_master, dec_results, dec_widths, DD, rate_dec, model_ranks)
    enc_norms_new = enc_norms - rate_norm * enc_norm_moment_new
    dec_norms_new = dec_norms - rate_norm * dec_norm_moment_new
    return (
        decoded,
        input_grad,
        enc_grad,
        dec_grad,
        enc_norm_grad,
        dec_norm_grad,
        dec_shift_grad,
        enc_moment_new,
        dec_moment_new,
        enc_norm_moment_new,
        dec_norm_moment_new,
        enc_master_new,
        dec_master_new,
        enc_norms_new,
        dec_norms_new,
        enc_master_new.astype(jnp.bfloat16),
        dec_master_new.astype(jnp.bfloat16),
        enc_norms_new.astype(jnp.bfloat16),
        dec_norms_new.astype(jnp.bfloat16),
        grad_norm,
    )


def solution(mesh):
    return jax.shard_map(
        local,
        mesh=mesh,
        in_specs=(
            P("dp", None),
            P("dp", None),
            P("dp", None),
            P("dp", "mp"),
            P("dp", "mp"),
            P(None, "dp"),
            P(None, "dp"),
            P("dp", "mp"),
            P("dp", "mp"),
            P(None, "dp"),
            P(None, "dp"),
        ),
        out_specs=(
            P("dp", None),
            P("dp", None),
            P("dp", "mp"),
            P("dp", "mp"),
            P(None, "dp"),
            P(None, "dp"),
            P("dp"),
            P("dp", "mp"),
            P("dp", "mp"),
            P(None, "dp"),
            P(None, "dp"),
            P("dp", "mp"),
            P("dp", "mp"),
            P(None, "dp"),
            P(None, "dp"),
            P("dp", "mp"),
            P("dp", "mp"),
            P(None, "dp"),
            P(None, "dp"),
            P(),
        ),
        check_vma=False,
    )
```

```python
import math

import jax
import jax.numpy as jnp
from jax import lax
from jax.sharding import PartitionSpec as P

D = 1024
HD = 64
FF = 4096
DD = 512
DHD = 32
DFF = 2048
NS_STEPS = 5


highest = lax.Precision.HIGHEST
ln_eps = 1e-06
masked_score = -1e30
newton_first = 3.4445
newton_second = -4.775
newton_third = 2.0315
momentum_keep = 0.5
clip_bound = 100.0
rate_enc = 0.2
rate_dec = 0.3
rate_norm = 1.0
decay_rate = 0.01


def shortened(array):

    def short(part):
        return part.astype(jnp.bfloat16) if part.dtype == jnp.float32 else part

    return jax.tree.map(short, array)


def pair_swap(array, axis, bit):
    size = lax.axis_size(axis)
    return lax.ppermute(array, axis, [(rank, rank ^ bit) for rank in range(size)])


def core_swap(array):
    return pair_swap(array, "mp", 1)


def far_swap(array):
    return pair_swap(array, "mp", 2)


def far_sum(chip_term):
    half = chip_term.astype(jnp.bfloat16)
    return half.astype(jnp.float32) + far_swap(half).astype(jnp.float32)


def chip_sum(partial_term):
    own_rows = partial_term.shape[0] // 2
    received = core_swap(partial_term[own_rows:].astype(jnp.bfloat16))
    return partial_term[:own_rows] + received.astype(jnp.float32)


def both_halves(own_part):
    return jnp.concatenate([own_part, core_swap(own_part)], axis=0)


def sum_everywhere(array):
    for axis in ("mp", "dp"):
        bit = 1
        while bit < lax.axis_size(axis):
            array = array + pair_swap(array, axis, bit)
            bit *= 2
    return array


def gather_small(array):
    rank = lax.axis_index("dp")
    gathered = array[None]
    bit = 1
    while bit < lax.axis_size("dp"):
        other = pair_swap(gathered, "dp", bit)
        lower = (rank & bit) == 0
        gathered = jnp.concatenate(
            [jnp.where(lower, gathered, other), jnp.where(lower, other, gathered)], axis=0
        )
        bit *= 2
    return gathered


def normalize(values):
    center = values - jnp.mean(values, axis=-1, keepdims=True)
    inverse = lax.rsqrt(jnp.mean(center * center, axis=-1, keepdims=True) + ln_eps)
    return center * inverse, inverse


def normalize_back(normal, inverse, gain_row, out_grad):
    scaled = out_grad * gain_row
    mean_grad = jnp.mean(scaled, axis=-1, keepdims=True)
    mean_dot = jnp.mean(scaled * normal, axis=-1, keepdims=True)
    return inverse * (scaled - mean_grad - normal * mean_dot)


def gelu_and_slope(hidden):
    spread = 0.5 + 0.5 * lax.erf(hidden * math.sqrt(0.5))
    density = jnp.exp(-0.5 * hidden * hidden) * (1.0 / math.sqrt(2.0 * math.pi))
    return hidden * spread, spread + hidden * density


def swap_halves(array, chunk_rows, core):
    parts = array.reshape((-1, 2, chunk_rows // 2) + array.shape[1:])
    return jnp.where(core == 0, parts, parts[:, ::-1]).reshape(array.shape)


def segments_of(lengths, row_count):
    item_ends = jnp.cumsum(lengths)
    position = jnp.arange(row_count, dtype=jnp.int32)
    segment = jnp.sum((position[:, None] >= item_ends[None, :]).astype(jnp.int32), axis=1)
    live_mask = (position < item_ends[-1]).astype(jnp.float32)
    return (segment, live_mask)


def split_columns(whole_cols, widths):
    pieces = []
    start_col = 0
    for piece_width in widths:
        pieces.append(whole_cols[:, start_col : start_col + piece_width])
        start_col += piece_width
    return pieces


def attend_forward(query_part, key_part, value_part, segment, head_count, head_width, block_rows):
    row_count = query_part.shape[0]
    blocks = row_count // block_rows
    score_scale = head_width ** (-0.5)
    key_heads = key_part.reshape(row_count, head_count, head_width)
    value_heads = value_part.reshape(row_count, head_count, head_width)
    query_blocks = query_part.reshape(blocks, block_rows, head_count, head_width)
    segment_blocks = segment.reshape(blocks, block_rows)

    def attend_block(block_inputs):
        query_block, segment_block = block_inputs
        scores = (
            jnp.einsum("qhd,khd->hqk", query_block, key_heads, preferred_element_type=jnp.float32)
            * score_scale
        )
        scores = jnp.where((segment_block[:, None] == segment[None, :])[None], scores, masked_score)
        row_max = jnp.max(scores, axis=-1, keepdims=True)
        shifted = jnp.exp(scores - row_max)
        row_total = jnp.sum(shifted, axis=-1, keepdims=True)
        attention = (shifted / row_total).astype(jnp.bfloat16)
        block_out = jnp.einsum(
            "hqk,khd->qhd", attention, value_heads, preferred_element_type=jnp.float32
        )
        return (block_out.astype(jnp.bfloat16), row_max + jnp.log(row_total))

    block_outs, logsum = lax.map(attend_block, (query_blocks, segment_blocks))
    return (block_outs.reshape(row_count, head_count * head_width), logsum)


def attend_backward(
    heads_grad,
    query_part,
    key_part,
    value_part,
    segment,
    logsum,
    head_count,
    head_width,
    block_rows,
):
    row_count = query_part.shape[0]
    blocks = row_count // block_rows
    score_scale = head_width ** (-0.5)
    key_heads = key_part.reshape(row_count, head_count, head_width)
    value_heads = value_part.reshape(row_count, head_count, head_width)
    query_blocks = query_part.reshape(blocks, block_rows, head_count, head_width)
    grad_blocks = heads_grad.reshape(blocks, block_rows, head_count, head_width)
    segment_blocks = segment.reshape(blocks, block_rows)

    def backward_block(carried, block_inputs):
        key_total, value_total = carried
        query_block, grad_block, segment_block, logsum_block = block_inputs
        scores = (
            jnp.einsum("qhd,khd->hqk", query_block, key_heads, preferred_element_type=jnp.float32)
            * score_scale
        )
        scores = jnp.where((segment_block[:, None] == segment[None, :])[None], scores, masked_score)
        attention = jnp.exp(scores - logsum_block)
        grad_soft = jnp.einsum(
            "qhd,khd->hqk", grad_block, value_heads, preferred_element_type=jnp.float32
        )
        row_dot = jnp.sum(attention * grad_soft, axis=-1, keepdims=True)
        score_grad = (attention * (grad_soft - row_dot)).astype(jnp.bfloat16)
        query_grad = (
            jnp.einsum("hqk,khd->qhd", score_grad, key_heads, preferred_element_type=jnp.float32)
            * score_scale
        )
        key_total = (
            key_total
            + jnp.einsum(
                "hqk,qhd->khd", score_grad, query_block, preferred_element_type=jnp.float32
            )
            * score_scale
        )
        value_total = value_total + jnp.einsum(
            "hqk,qhd->khd",
            attention.astype(jnp.bfloat16),
            grad_block,
            preferred_element_type=jnp.float32,
        )
        return ((key_total, value_total), query_grad.astype(jnp.bfloat16))

    zeros = jnp.zeros((row_count, head_count, head_width), jnp.float32)
    (key_total, value_total), query_grads = lax.scan(
        backward_block, (zeros, zeros), (query_blocks, grad_blocks, segment_blocks, logsum)
    )
    return (
        query_grads.reshape(row_count, head_count * head_width),
        key_total.reshape(row_count, head_count * head_width).astype(jnp.bfloat16),
        value_total.reshape(row_count, head_count * head_width).astype(jnp.bfloat16),
    )


def attention_input(own_chunks, norm_values):
    normals = [normalize(own) for own in own_chunks]
    halves = [
        both_halves((normal * norm_values[0] + norm_values[1]).astype(jnp.bfloat16))
        for normal, _ in normals
    ]
    return normals, halves


def block_forward(own_chunks, halves, segment, pieces, norm_values, head_width, block_rows):
    qkv_proj, out_proj, up_proj, down_proj = pieces
    inner_width = out_proj.shape[1]
    head_count = inner_width // head_width
    chunk_rows = halves[0].shape[0]
    normed_half = jnp.concatenate(halves, axis=0)
    mixed_all = jnp.dot(normed_half, qkv_proj, preferred_element_type=jnp.float32).astype(
        jnp.bfloat16
    )
    query_part = mixed_all[:, :inner_width]
    key_part = mixed_all[:, inner_width : 2 * inner_width]
    value_part = mixed_all[:, 2 * inner_width :]
    heads_out, logsum = attend_forward(
        query_part, key_part, value_part, segment, head_count, head_width, block_rows
    )
    middles = []
    for place, own in enumerate(own_chunks):
        rows = heads_out[place * chunk_rows : (place + 1) * chunk_rows]
        chip_term = chip_sum(
            jnp.einsum("ti,di->td", rows, out_proj, preferred_element_type=jnp.float32)
        )
        middles.append(own + far_sum(chip_term))
    seconds, outputs, ups = [], [], []
    for middle in middles:
        normal, inverse = normalize(middle)
        normed_two = both_halves((normal * norm_values[2] + norm_values[3]).astype(jnp.bfloat16))
        hidden = jnp.dot(normed_two, up_proj, preferred_element_type=jnp.float32)
        activated, slope = gelu_and_slope(hidden)
        activated = activated.astype(jnp.bfloat16)
        chip_term = chip_sum(
            jnp.einsum("tf,df->td", activated, down_proj, preferred_element_type=jnp.float32)
        )
        outputs.append(middle + far_sum(chip_term))
        seconds.append((normal, inverse))
        ups.append((normed_two, activated, slope))
    return (
        outputs,
        (normed_half, query_part, key_part, value_part, heads_out, logsum, seconds, ups),
    )


def block_backward(
    own_grads, half_grads, saved, firsts, pieces, norm_values, segment, head_width, block_rows
):
    normed_half, query_part, key_part, value_part, heads_out, logsum, seconds, ups = saved
    qkv_proj, out_proj, up_proj, down_proj = pieces
    inner_width = out_proj.shape[1]
    head_count = inner_width // head_width
    chunk_rows = half_grads[0].shape[0]
    hidden_halves, chip_terms = [], []
    for half_grad, (_, _, slope) in zip(half_grads, ups):
        act_grad = jnp.einsum("td,df->tf", half_grad, down_proj, preferred_element_type=jnp.float32)
        hidden_half = (act_grad * slope).astype(jnp.bfloat16)
        hidden_halves.append(hidden_half)
        chip_terms.append(
            chip_sum(
                jnp.einsum("tf,df->td", hidden_half, up_proj, preferred_element_type=jnp.float32)
            )
        )
    middle_grads, middle_halves, gain_two, shift_two = [], [], 0.0, 0.0
    for own_grad, chip_term, (normal, inverse) in zip(own_grads, chip_terms, seconds):
        gain_two = gain_two + jnp.sum(chip_term * normal, axis=0)
        shift_two = shift_two + jnp.sum(chip_term, axis=0)
        middle_grad = own_grad + normalize_back(
            normal, inverse, norm_values[2], far_sum(chip_term)
        )
        middle_grads.append(middle_grad)
        middle_halves.append(both_halves(middle_grad.astype(jnp.bfloat16)))
    heads_grad = jnp.concatenate(
        [
            jnp.einsum("td,di->ti", half, out_proj, preferred_element_type=jnp.float32).astype(
                jnp.bfloat16
            )
            for half in middle_halves
        ],
        axis=0,
    )
    down_grad = jnp.einsum(
        "td,tf->df",
        jnp.concatenate(half_grads, axis=0),
        jnp.concatenate([activated for _, activated, _ in ups], axis=0),
        preferred_element_type=jnp.float32,
    ).astype(jnp.bfloat16)
    up_grad = jnp.einsum(
        "td,tf->df",
        jnp.concatenate([normed_two for normed_two, _, _ in ups], axis=0),
        jnp.concatenate(hidden_halves, axis=0),
        preferred_element_type=jnp.float32,
    ).astype(jnp.bfloat16)
    out_grad = jnp.einsum(
        "td,ti->di",
        jnp.concatenate(middle_halves, axis=0),
        heads_out,
        preferred_element_type=jnp.float32,
    ).astype(jnp.bfloat16)
    query_grad, key_grad, value_grad = attend_backward(
        heads_grad,
        query_part,
        key_part,
        value_part,
        segment,
        logsum,
        head_count,
        head_width,
        block_rows,
    )
    mixed_grad = jnp.concatenate([query_grad, key_grad, value_grad], axis=1)
    chip_terms = [
        chip_sum(
            jnp.einsum(
                "tf,df->td",
                mixed_grad[place * chunk_rows : (place + 1) * chunk_rows],
                qkv_proj,
                preferred_element_type=jnp.float32,
            )
        )
        for place in range(len(own_grads))
    ]
    qkv_grad = jnp.einsum(
        "td,tf->df", normed_half, mixed_grad, preferred_element_type=jnp.float32
    ).astype(jnp.bfloat16)
    input_grads, gain_one, shift_one = [], 0.0, 0.0
    for middle_grad, chip_term, (normal, inverse) in zip(middle_grads, chip_terms, firsts):
        gain_one = gain_one + jnp.sum(chip_term * normal, axis=0)
        shift_one = shift_one + jnp.sum(chip_term, axis=0)
        input_grads.append(
            middle_grad
            + normalize_back(normal, inverse, norm_values[0], far_sum(chip_term))
        )
    return (
        input_grads,
        [qkv_grad, out_grad, up_grad, down_grad],
        jnp.stack([gain_one, shift_one, gain_two, shift_two]),
    )


def gram_newton(gram):
    total = None
    for newton_step in range(NS_STEPS):
        gram_half = gram.astype(jnp.bfloat16)
        square = jnp.dot(gram_half, gram_half, preferred_element_type=jnp.float32)
        mix_matrix = newton_second * gram + newton_third * square
        mix_half = mix_matrix.astype(jnp.bfloat16)
        if total is None:
            total = newton_first * jnp.eye(gram.shape[0], dtype=jnp.float32) + mix_matrix
        else:
            total = newton_first * total + jnp.dot(
                mix_half, total.astype(jnp.bfloat16), preferred_element_type=jnp.float32
            )
        if newton_step < NS_STEPS - 1:
            left = newton_first * gram + jnp.dot(
                mix_half, gram_half, preferred_element_type=jnp.float32
            )
            gram = newton_first * left + jnp.dot(
                left.astype(jnp.bfloat16), mix_half, preferred_element_type=jnp.float32
            )
    return total


def slot_rows(enc_rows_half, dec_rows_half, enc_widths, dec_widths, slot_width, data_ranks):
    enc_parts = split_columns(enc_rows_half, enc_widths)
    dec_parts = split_columns(dec_rows_half, dec_widths)
    half_width = slot_width // 2

    def widened(part, width):
        return jnp.pad(part, ((0, 0), (0, width - part.shape[1])))

    slots = [widened(part, slot_width) for part in enc_parts]
    for first in range(0, len(dec_parts), 2):
        upper = jnp.pad(widened(dec_parts[first], half_width), ((0, 0), (0, half_width)))
        lower = jnp.pad(widened(dec_parts[first + 1], half_width), ((0, 0), (half_width, 0)))
        slots.append(jnp.concatenate([upper, lower], axis=0))
    empty = jnp.zeros_like(slots[0])
    return jnp.stack(slots + [empty] * (data_ranks - len(slots)))


def unslot(rows_back, enc_widths, dec_widths, dec_rows):
    slot_width = rows_back.shape[2]
    enc_results = [rows_back[k][:, :width] for k, width in enumerate(enc_widths)]
    dec_results = []
    for place, width in enumerate(dec_widths):
        slot = rows_back[len(enc_widths) + place // 2]
        odd = place % 2
        dec_results.append(
            slot[
                odd * dec_rows : (odd + 1) * dec_rows,
                odd * (slot_width // 2) : odd * (slot_width // 2) + width,
            ]
        )
    return enc_results, dec_results


def apply_step(master, ortho_rows, widths, model_width, rate, model_ranks):
    steps_all = [
        orthogonal * (0.2 * math.sqrt(max(model_width, piece_width * model_ranks)))
        for orthogonal, piece_width in zip(ortho_rows, widths)
    ]
    return master * (1.0 - rate * decay_rate) - rate * jnp.concatenate(steps_all, axis=1)


def local(
    patches,
    cotangent,
    item_lengths,
    enc_master,
    dec_master,
    enc_norms,
    dec_norms,
    enc_moment,
    dec_moment,
    enc_norm_moment,
    dec_norm_moment,
):
    model_ranks = lax.axis_size("mp")
    data_ranks = lax.axis_size("dp")
    enc_widths = [
        3 * D // model_ranks,
        D // model_ranks,
        FF // model_ranks,
        FF // model_ranks,
        DD // model_ranks,
    ]
    dec_widths = [3 * DD // model_ranks, DD // model_ranks, DFF // model_ranks, DFF // model_ranks]
    first_cols = enc_widths[0] + enc_widths[1]
    norm_parts = gather_small(
        jnp.concatenate([enc_norms, dec_norms], axis=1).astype(jnp.bfloat16)
    ).astype(jnp.float32)
    enc_share, dec_share = enc_norms.shape[1], dec_norms.shape[1]
    enc_norm_values = jnp.moveaxis(norm_parts[:, :, :enc_share], 0, 1).reshape(4, D)
    dec_norm_values = jnp.moveaxis(norm_parts[:, :, enc_share:], 0, 1).reshape(4, DD)
    first_low, rest_low, dec_low = (
        lax.all_gather(
            enc_master[:, :first_cols].astype(jnp.bfloat16), "dp", axis=0, tiled=True
        ),
        lax.all_gather(
            enc_master[:, first_cols:].astype(jnp.bfloat16), "dp", axis=0, tiled=True
        ),
        lax.all_gather(dec_master.astype(jnp.bfloat16), "dp", axis=0, tiled=True),
    )
    enc_pieces = split_columns(first_low, enc_widths[:2]) + split_columns(rest_low, enc_widths[2:])
    dec_pieces = split_columns(dec_low, dec_widths)
    model_rank = lax.axis_index("mp")
    core = model_rank % 2
    upper_chip = model_rank // 2
    row_count = patches.shape[0]
    block_rows = min(512, row_count)
    chunk_count = 2
    chunk_rows = row_count // chunk_count
    own_count = chunk_rows // 2
    segment, live_mask = segments_of(item_lengths[0], row_count)
    segment = swap_halves(segment, chunk_rows, core)
    live_mask = swap_halves(live_mask, chunk_rows, core)
    inputs = swap_halves(patches, chunk_rows, core)
    upstream = swap_halves(cotangent, chunk_rows, core) * live_mask.astype(jnp.bfloat16)[:, None]

    def chunked(array):
        return [array[k * chunk_rows : (k + 1) * chunk_rows] for k in range(chunk_count)]

    bridge = enc_pieces[4]
    bridge_far = far_swap(bridge)
    bridge_pair = jnp.where(
        upper_chip == 0, jnp.stack([bridge, bridge_far]), jnp.stack([bridge_far, bridge])
    )
    pair_other = core_swap(bridge_pair)
    bridge_all = jnp.stack(
        [
            jnp.where(core == 0, bridge_pair, pair_other),
            jnp.where(core == 0, pair_other, bridge_pair),
        ],
        axis=1,
    )
    share_width = bridge.shape[1]
    bridge_all = jnp.moveaxis(bridge_all.reshape(-1, D, share_width), 0, 1).reshape(D, DD)

    input_chunks = [chunk.astype(jnp.float32) for chunk in chunked(inputs)]
    normals_all = [normalize(chunk) for chunk in input_chunks]
    enc_firsts = [(normal[:own_count], inverse[:own_count]) for normal, inverse in normals_all]
    enc_halves = [
        (normal * enc_norm_values[0] + enc_norm_values[1]).astype(jnp.bfloat16)
        for normal, _ in normals_all
    ]
    encoded, enc_saved = block_forward(
        [chunk[:own_count] for chunk in input_chunks],
        enc_halves,
        segment,
        enc_pieces[:4],
        enc_norm_values,
        HD,
        block_rows,
    )
    encoded_own = [chunk.astype(jnp.bfloat16) for chunk in encoded]
    decoder_in = [
        jnp.dot(chunk, bridge_all, preferred_element_type=jnp.float32)
        .astype(jnp.bfloat16)
        .astype(jnp.float32)
        for chunk in encoded_own
    ]
    encoded_half = jnp.concatenate([both_halves(chunk) for chunk in encoded_own], axis=0)
    dec_firsts, dec_halves = attention_input(decoder_in, dec_norm_values)
    decoded, dec_saved = block_forward(
        decoder_in, dec_halves, segment, dec_pieces, dec_norm_values, DHD, block_rows
    )
    upstream_halves = chunked(upstream)
    dec_in_grads, dec_grads, dec_norm_grads = block_backward(
        [half[:own_count].astype(jnp.float32) for half in upstream_halves],
        upstream_halves,
        dec_saved,
        dec_firsts,
        dec_pieces,
        dec_norm_values,
        segment,
        DHD,
        block_rows,
    )
    bridge_halves = [both_halves(grad.astype(jnp.bfloat16)) for grad in dec_in_grads]
    encoded_grads = [
        jnp.einsum("tf,df->td", half, bridge_all, preferred_element_type=jnp.float32)
        for half in bridge_halves
    ]
    bridge_in_grad = lax.dynamic_slice_in_dim(
        jnp.concatenate(bridge_halves, axis=0), model_rank * share_width, share_width, 1
    )
    bridge_grad = jnp.einsum(
        "td,tf->df", encoded_half, bridge_in_grad, preferred_element_type=jnp.float32
    ).astype(jnp.bfloat16)
    input_grads, enc_grads, enc_norm_grads = block_backward(
        [grad[:own_count] for grad in encoded_grads],
        [grad.astype(jnp.bfloat16) for grad in encoded_grads],
        enc_saved,
        enc_firsts,
        enc_pieces[:4],
        enc_norm_values,
        segment,
        HD,
        block_rows,
    )

    def natural(own_chunks):
        return swap_halves(
            jnp.concatenate([both_halves(own) for own in own_chunks], axis=0), chunk_rows, core
        )

    decoded = natural(decoded)
    input_grad = natural(input_grads)

    def scattered(parts):
        return lax.psum_scatter(
            jnp.concatenate(parts, axis=1), "dp", scatter_dimension=0, tiled=True
        ).astype(jnp.float32)

    dec_sum_rows = scattered(dec_grads)
    late_rows = scattered(enc_grads[:2] + [bridge_grad])
    early_rows = scattered(enc_grads[2:])
    enc_sum_rows = jnp.concatenate(
        [late_rows[:, :first_cols], early_rows, late_rows[:, first_cols:]], axis=1
    )
    norm_sums = sum_everywhere(jnp.concatenate([enc_norm_grads, dec_norm_grads], axis=1))
    data_rank = lax.axis_index("dp")
    enc_norm_rows = lax.dynamic_slice_in_dim(norm_sums[:, :D], data_rank * enc_share, enc_share, 1)
    dec_norm_rows = lax.dynamic_slice_in_dim(norm_sums[:, D:], data_rank * dec_share, dec_share, 1)
    local_sum = jnp.sum(enc_sum_rows * enc_sum_rows) + jnp.sum(dec_sum_rows * dec_sum_rows)
    squares = sum_everywhere(jnp.full((8, 128), local_sum))[0, 0] + jnp.sum(norm_sums * norm_sums)
    grad_norm = jnp.sqrt(squares)
    factor = clip_bound * lax.rsqrt(squares + 1e-06)
    enc_grad = enc_sum_rows * factor
    dec_grad = dec_sum_rows * factor
    enc_norm_grad = enc_norm_rows * factor
    dec_norm_grad = dec_norm_rows * factor
    dec_shift_grad = dec_norm_grad[3]
    enc_moment_new = momentum_keep * enc_moment + enc_grad
    dec_moment_new = momentum_keep * dec_moment + dec_grad
    enc_norm_moment_new = momentum_keep * enc_norm_moment + enc_norm_grad
    dec_norm_moment_new = momentum_keep * dec_norm_moment + dec_norm_grad
    slot_width = max(enc_widths)
    enc_rows = enc_master.shape[0]
    dec_rows = dec_master.shape[0]
    slots = slot_rows(
        enc_moment_new.astype(jnp.bfloat16),
        dec_moment_new.astype(jnp.bfloat16),
        enc_widths,
        dec_widths,
        slot_width,
        data_ranks,
    )
    own = lax.all_to_all(slots, "dp", 0, 0).reshape(data_ranks * enc_rows, slot_width)
    gram = lax.psum(
        lax.dot_general(
            own, own, (((1,), (1,)), ((), ())), preferred_element_type=jnp.float32
        ),
        "mp",
    )
    paired = jnp.logical_and(
        data_rank >= len(enc_widths), data_rank < len(enc_widths) + len(dec_widths) // 2
    )
    row_index = jnp.arange(gram.shape[0], dtype=jnp.int32)
    upper_row = (row_index % enc_rows) < dec_rows
    diagonal = jnp.sum(jnp.where(row_index[:, None] == row_index[None, :], gram, 0.0), axis=1)
    upper_trace = jnp.sum(jnp.where(upper_row, diagonal, 0.0))
    lower_trace = jnp.sum(jnp.where(upper_row, 0.0, diagonal))
    row_trace = jnp.where(
        paired, jnp.where(upper_row, upper_trace, lower_trace), upper_trace + lower_trace
    )
    row_scale = 1.0 / (jnp.sqrt(row_trace) + 1e-07)
    product = gram_newton(gram * row_scale[:, None] * row_scale[None, :])
    orthogonal = jnp.dot(
        (product * row_scale[None, :]).astype(jnp.bfloat16),
        own,
        preferred_element_type=jnp.float32,
    ).astype(jnp.bfloat16)
    rows_back = lax.all_to_all(
        orthogonal.reshape(data_ranks, enc_rows, slot_width), "dp", 0, 0
    ).astype(jnp.float32)
    enc_results, dec_results = unslot(rows_back, enc_widths, dec_widths, dec_rows)
    enc_master_new = apply_step(enc_master, enc_results, enc_widths, D, rate_enc, model_ranks)
    dec_master_new = apply_step(dec_master, dec_results, dec_widths, DD, rate_dec, model_ranks)
    enc_norms_new = enc_norms - rate_norm * enc_norm_moment_new
    dec_norms_new = dec_norms - rate_norm * dec_norm_moment_new
    return (
        decoded,
        input_grad,
        enc_grad,
        dec_grad,
        enc_norm_grad,
        dec_norm_grad,
        dec_shift_grad,
        enc_moment_new,
        dec_moment_new,
        enc_norm_moment_new,
        dec_norm_moment_new,
        enc_master_new,
        dec_master_new,
        enc_norms_new,
        dec_norms_new,
        enc_master_new.astype(jnp.bfloat16),
        dec_master_new.astype(jnp.bfloat16),
        enc_norms_new.astype(jnp.bfloat16),
        dec_norms_new.astype(jnp.bfloat16),
        grad_norm,
    )


def solution(mesh):
    return jax.shard_map(
        local,
        mesh=mesh,
        in_specs=(
            P("dp", None),
            P("dp", None),
            P("dp", None),
            P("dp", "mp"),
            P("dp", "mp"),
            P(None, "dp"),
            P(None, "dp"),
            P("dp", "mp"),
            P("dp", "mp"),
            P(None, "dp"),
            P(None, "dp"),
        ),
        out_specs=(
            P("dp", None),
            P("dp", None),
            P("dp", "mp"),
            P("dp", "mp"),
            P(None, "dp"),
            P(None, "dp"),
            P("dp"),
            P("dp", "mp"),
            P("dp", "mp"),
            P(None, "dp"),
            P(None, "dp"),
            P("dp", "mp"),
            P("dp", "mp"),
            P(None, "dp"),
            P(None, "dp"),
            P("dp", "mp"),
            P("dp", "mp"),
            P(None, "dp"),
            P(None, "dp"),
            P(),
        ),
        check_vma=False,
    )
```

```python
import functools
import math

import jax
import jax.numpy as jnp
from jax import lax
from jax.experimental import pallas as pl
from jax.experimental.pallas import tpu as pltpu
from jax.sharding import PartitionSpec as P

D = 1024
HD = 64
FF = 4096
DD = 512
DHD = 32
DFF = 2048
NS_STEPS = 5


highest = lax.Precision.HIGHEST
ln_eps = 1e-06
masked_score = -1e30
newton_first = 3.4445
newton_second = -4.775
newton_third = 2.0315
momentum_keep = 0.5
clip_bound = 100.0
rate_enc = 0.2
rate_dec = 0.3
rate_norm = 1.0
decay_rate = 0.01
kernel_vmem = 32 * 1024 * 1024
newton_vmem = 48 * 1024 * 1024


def shortened(array):

    def short(part):
        return part.astype(jnp.bfloat16) if part.dtype == jnp.float32 else part

    return jax.tree.map(short, array)


def pair_swap(array, axis, bit):
    size = lax.axis_size(axis)
    return lax.ppermute(array, axis, [(rank, rank ^ bit) for rank in range(size)])


def core_swap(array):
    return pair_swap(array, "mp", 1)


def far_swap(array):
    return pair_swap(array, "mp", 2)


def far_sum(chip_term):
    half = chip_term.astype(jnp.bfloat16)
    return half.astype(jnp.float32) + far_swap(half).astype(jnp.float32)


def chip_sum(partial_term):
    own_rows = partial_term.shape[0] // 2
    received = core_swap(partial_term[own_rows:].astype(jnp.bfloat16))
    return partial_term[:own_rows] + received.astype(jnp.float32)


def both_halves(own_part):
    return jnp.concatenate([own_part, core_swap(own_part)], axis=0)


def sum_everywhere(array):
    for axis in ("mp", "dp"):
        bit = 1
        while bit < lax.axis_size(axis):
            array = array + pair_swap(array, axis, bit)
            bit *= 2
    return array


def gather_small(array):
    rank = lax.axis_index("dp")
    gathered = array[None]
    bit = 1
    while bit < lax.axis_size("dp"):
        other = pair_swap(gathered, "dp", bit)
        lower = (rank & bit) == 0
        gathered = jnp.concatenate(
            [jnp.where(lower, gathered, other), jnp.where(lower, other, gathered)], axis=0
        )
        bit *= 2
    return gathered


def assemble_kernel(rank_ref, *refs):
    whole_ref = refs[-1]
    rows = refs[0].shape[0]
    for bit, part_ref in enumerate(refs[:-1]):
        place = pl.multiple_of((rank_ref[0] ^ bit) * rows, rows)
        whole_ref[pl.ds(place, rows), :] = part_ref[...]


def assemble(parts):
    rows, columns = parts[0].shape
    spec = pl.BlockSpec(memory_space=pltpu.VMEM)
    return pl.pallas_call(
        assemble_kernel,
        in_specs=[pl.BlockSpec(memory_space=pltpu.SMEM)] + [spec] * len(parts),
        out_specs=spec,
        out_shape=jax.ShapeDtypeStruct((len(parts) * rows, columns), parts[0].dtype),
        compiler_params=pltpu.CompilerParams(vmem_limit_bytes=kernel_vmem),
        cost_estimate=pl.CostEstimate(
            flops=0, bytes_accessed=4 * len(parts) * rows * columns, transcendentals=0
        ),
        name="assemble",
    )(lax.axis_index("dp").reshape(1), *parts)


class Gather:
    def __init__(self, array):
        self.general = lax.axis_size("dp") != 8
        if self.general:
            self.whole = lax.all_gather(array, "dp", axis=0, tiled=True)
            self.lined = [array]
        else:
            self.lined = [array] + [pair_swap(array, "dp", 2 * bit) for bit in (1, 2, 3)]
            self.crossed = None

    def turn(self, values):
        if self.general:
            return values
        values, self.lined = lax.optimization_barrier((values, self.lined))
        self.cross()
        return values

    def cross(self):
        self.crossed = [pair_swap(part, "dp", 1) for part in self.lined]

    def result(self):
        if self.general:
            return self.whole
        if self.crossed is None:
            self.cross()
        return assemble([part for pair in zip(self.lined, self.crossed) for part in pair])


def collect(slots):
    ranks = lax.axis_size("dp")
    rank = lax.axis_index("dp")
    width = max(rows.shape[1] for rows in slots.values())
    padded = {
        owner: jnp.pad(rows, ((0, 0), (0, width - rows.shape[1])))
        for owner, rows in slots.items()
    }
    parts = []
    for bit in range(ranks):
        value = None
        for owner, rows in padded.items():
            value = rows if value is None else jnp.where(rank ^ bit == owner, rows, value)
        if bit:
            value = lax.ppermute(value, "dp", [(owner ^ bit, owner) for owner in padded])
        parts.append(value)
    return assemble(parts)


def after(value, anchor):
    return lax.optimization_barrier((value, anchor))[0]


def fold(kept, received):
    return (kept.astype(jnp.float32) + received.astype(jnp.float32)).astype(jnp.bfloat16)


def split_rows(array, place):
    half = array.shape[0] // 2
    return (
        lax.dynamic_slice_in_dim(array, (1 - place) * half, half, 0),
        lax.dynamic_slice_in_dim(array, place * half, half, 0),
    )


class Scatter:
    def __init__(self, groups):
        self.phase = 0
        self.general = lax.axis_size("dp") != 8
        self.rank = lax.axis_index("dp")
        if self.general:
            whole = jnp.concatenate(
                [
                    sum(
                        jnp.einsum("td,tf->df", left, right, preferred_element_type=jnp.float32)
                        for left, right in zip(lefts, rights)
                    ).astype(jnp.bfloat16)
                    for lefts, rights in groups
                ],
                axis=1,
            )
            self.total = lax.psum_scatter(whole, "dp", scatter_dimension=0, tiled=True)
            self.received = self.total
        else:
            self.sent, self.kept = weight_grads(groups, self.rank % 2)
            self.received = pair_swap(self.sent, "dp", 1)

    def turn(self, values):
        if self.general or self.phase == 2:
            return values
        values, self.received = lax.optimization_barrier((values, self.received))
        self.advance()
        return values

    def advance(self):
        place = self.rank // 2 % 2 if self.phase == 0 else self.rank // 4
        self.sent, self.kept = split_rows(fold(self.kept, self.received), place)
        self.received = pair_swap(self.sent, "dp", 2 << self.phase)
        self.phase += 1

    def result(self):
        if self.general:
            return self.total.astype(jnp.float32)
        while self.phase < 2:
            self.advance()
        return self.kept.astype(jnp.float32) + self.received.astype(jnp.float32)

    def direct_result(self):
        if self.general:
            return self.total.astype(jnp.float32)
        pairs = fold(self.kept, self.received)
        rows = pairs.shape[0] // 4
        outer = self.rank // 2

        def block(place):
            return lax.dynamic_slice_in_dim(pairs, (place % 2 * 2 + place // 2) * rows, rows, 0)

        total = block(outer).astype(jnp.float32)
        for bit in (3, 2, 1):
            total = total + pair_swap(block(outer ^ bit), "dp", 2 * bit).astype(jnp.float32)
        return total


def normalize(values):
    center = values - jnp.mean(values, axis=-1, keepdims=True)
    inverse = lax.rsqrt(jnp.mean(center * center, axis=-1, keepdims=True) + ln_eps)
    return center * inverse, inverse


def normalize_back(normal, inverse, gain_row, out_grad):
    scaled = out_grad * gain_row
    mean_grad = jnp.mean(scaled, axis=-1, keepdims=True)
    mean_dot = jnp.mean(scaled * normal, axis=-1, keepdims=True)
    return inverse * (scaled - mean_grad - normal * mean_dot)


def gelu_and_slope(hidden):
    spread = 0.5 + 0.5 * lax.erf(hidden * math.sqrt(0.5))
    density = jnp.exp(-0.5 * hidden * hidden) * (1.0 / math.sqrt(2.0 * math.pi))
    return hidden * spread, spread + hidden * density


def swap_halves(array, chunk_rows, core):
    parts = array.reshape((-1, 2, chunk_rows // 2) + array.shape[1:])
    return jnp.where(core == 0, parts, parts[:, ::-1]).reshape(array.shape)


def segments_of(lengths, row_count):
    item_ends = jnp.cumsum(lengths)
    position = jnp.arange(row_count, dtype=jnp.int32)
    segment = jnp.sum((position[:, None] >= item_ends[None, :]).astype(jnp.int32), axis=1)
    live_mask = (position < item_ends[-1]).astype(jnp.float32)
    return (segment, live_mask)


def split_columns(whole_cols, widths):
    pieces = []
    start_col = 0
    for piece_width in widths:
        pieces.append(whole_cols[:, start_col : start_col + piece_width])
        start_col += piece_width
    return pieces


def head_mask(head, head_width, inner_width):
    lane = lax.broadcasted_iota(jnp.int32, (1, inner_width), 1)
    inside = jnp.logical_and(lane >= head * head_width, lane < (head + 1) * head_width)
    return jnp.where(inside, 1.0, 0.0)


def masked_rows(rows, head, head_width):
    mask = head_mask(head, head_width, rows.shape[1])
    return (rows.astype(jnp.float32) * mask).astype(jnp.bfloat16)


def last_dims(left, right):
    return lax.dot_general(
        left, right, (((1,), (1,)), ((), ())), preferred_element_type=jnp.float32
    )


def segment_bias(key_segment_ref, query_segment_ref):
    return jnp.where(key_segment_ref[...] == query_segment_ref[...], 0.0, masked_score)


def attend_forward_kernel(
    head_width, key_segment_ref, query_segment_ref, query_ref, key_ref, value_ref, out_ref,
    logsum_ref,
):
    block_rows, inner_width = query_ref.shape
    score_scale = head_width ** (-0.5)
    bias = segment_bias(key_segment_ref, query_segment_ref)
    joined = jnp.zeros((block_rows, inner_width), jnp.float32)
    logsums = []
    for head in range(inner_width // head_width):
        query = masked_rows(query_ref[...], head, head_width)
        scores = last_dims(query, key_ref[...]) * score_scale + bias
        top = jnp.max(scores, axis=1, keepdims=True)
        shifted = jnp.exp(scores - top)
        total = jnp.sum(shifted, axis=1, keepdims=True)
        part = jnp.dot(
            shifted.astype(jnp.bfloat16), value_ref[...], preferred_element_type=jnp.float32
        )
        joined += part * (head_mask(head, head_width, inner_width) / total)
        logsums.append(jnp.broadcast_to(top + jnp.log(total), (block_rows, 128)))
    out_ref[...] = joined.astype(jnp.bfloat16)
    lane = lax.broadcasted_iota(jnp.int32, (block_rows, 128), 1)
    stacked = logsums[0]
    for head in range(1, len(logsums)):
        stacked = jnp.where(lane == head, logsums[head], stacked)
    logsum_ref[...] = stacked.T[: len(logsums), :]


def attend_forward(mixed_all, segment, first_block, block_count, head_width, block_rows):
    row_count = mixed_all.shape[0]
    inner_width = mixed_all.shape[1] // 3
    head_count = inner_width // head_width
    return pl.pallas_call(
        functools.partial(attend_forward_kernel, head_width),
        grid=(block_count,),
        in_specs=[
            pl.BlockSpec((1, row_count), lambda i: (0, 0)),
            pl.BlockSpec((block_rows, 1), lambda i: (first_block + i, 0)),
            pl.BlockSpec((block_rows, inner_width), lambda i: (first_block + i, 0)),
            pl.BlockSpec((row_count, inner_width), lambda i: (0, 1)),
            pl.BlockSpec((row_count, inner_width), lambda i: (0, 2)),
        ],
        out_specs=[
            pl.BlockSpec((block_rows, inner_width), lambda i: (i, 0)),
            pl.BlockSpec((head_count, block_rows), lambda i: (0, i)),
        ],
        out_shape=[
            jax.ShapeDtypeStruct((block_count * block_rows, inner_width), jnp.bfloat16),
            jax.ShapeDtypeStruct((head_count, block_count * block_rows), jnp.float32),
        ],
        compiler_params=pltpu.CompilerParams(
            dimension_semantics=("arbitrary",), vmem_limit_bytes=kernel_vmem
        ),
        cost_estimate=pl.CostEstimate(
            flops=4 * block_count * block_rows * row_count * inner_width * head_count,
            bytes_accessed=8 * row_count * inner_width,
            transcendentals=block_count * block_rows * row_count * head_count,
        ),
        name="attend_forward",
    )(segment.reshape(1, row_count), segment.reshape(row_count, 1), mixed_all, mixed_all, mixed_all)


def attend_backward_kernel(
    head_width, key_segment_ref, query_segment_ref, grad_ref, logsum_ref, query_ref, key_ref,
    value_ref, out_ref, turned_ref, key_total_ref, value_total_ref,
):
    step = pl.program_id(0)
    block_rows, inner_width = query_ref.shape

    @pl.when(step == 0)
    def begin():
        turned_ref[...] = key_ref[...].astype(jnp.float32).T.astype(jnp.bfloat16)
        key_total_ref[...] = jnp.zeros_like(key_total_ref)
        value_total_ref[...] = jnp.zeros_like(value_total_ref)

    score_scale = head_width ** (-0.5)
    bias = segment_bias(key_segment_ref, query_segment_ref)
    parts = []
    for head in range(inner_width // head_width):
        query = masked_rows(query_ref[...], head, head_width)
        grad = masked_rows(grad_ref[...], head, head_width)
        scores = last_dims(key_ref[...], query) * score_scale + bias
        attention = jnp.exp(scores - logsum_ref[head : head + 1, :])
        weighted = attention * last_dims(value_ref[...], grad)
        row_dot = jnp.sum(weighted, axis=0, keepdims=True)
        score_grad = (weighted - attention * row_dot).astype(jnp.bfloat16)
        value_total_ref[...] += jnp.dot(
            attention.astype(jnp.bfloat16), grad, preferred_element_type=jnp.float32
        )
        key_total_ref[...] += jnp.dot(score_grad, query, preferred_element_type=jnp.float32)
        parts.append(
            jnp.dot(
                turned_ref[head * head_width : (head + 1) * head_width, :],
                score_grad,
                preferred_element_type=jnp.float32,
            )
        )
    query_grad = (jnp.concatenate(parts, axis=0) * score_scale).T
    rows = pl.ds(pl.multiple_of(step * block_rows, block_rows), block_rows)
    out_ref[rows, :inner_width] = query_grad.astype(jnp.bfloat16)

    @pl.when(step == pl.num_programs(0) - 1)
    def finish():
        out_ref[:, inner_width : 2 * inner_width] = (key_total_ref[...] * score_scale).astype(
            jnp.bfloat16
        )
        out_ref[:, 2 * inner_width :] = value_total_ref[...].astype(jnp.bfloat16)


def attend_backward(heads_grad, mixed_all, logsum, segment, head_width, block_rows):
    row_count, inner_width = heads_grad.shape
    head_count = inner_width // head_width
    return pl.pallas_call(
        functools.partial(attend_backward_kernel, head_width),
        grid=(row_count // block_rows,),
        in_specs=[
            pl.BlockSpec((row_count, 1), lambda i: (0, 0)),
            pl.BlockSpec((1, block_rows), lambda i: (0, i)),
            pl.BlockSpec((block_rows, inner_width), lambda i: (i, 0)),
            pl.BlockSpec((head_count, block_rows), lambda i: (0, i)),
            pl.BlockSpec((block_rows, inner_width), lambda i: (i, 0)),
            pl.BlockSpec((row_count, inner_width), lambda i: (0, 1)),
            pl.BlockSpec((row_count, inner_width), lambda i: (0, 2)),
        ],
        out_specs=pl.BlockSpec((row_count, 3 * inner_width), lambda i: (0, 0)),
        out_shape=jax.ShapeDtypeStruct((row_count, 3 * inner_width), jnp.bfloat16),
        scratch_shapes=[
            pltpu.VMEM((inner_width, row_count), jnp.bfloat16),
            pltpu.VMEM((row_count, inner_width), jnp.float32),
            pltpu.VMEM((row_count, inner_width), jnp.float32),
        ],
        compiler_params=pltpu.CompilerParams(
            dimension_semantics=("arbitrary",), vmem_limit_bytes=kernel_vmem
        ),
        cost_estimate=pl.CostEstimate(
            flops=10 * row_count * row_count * inner_width * head_count,
            bytes_accessed=14 * row_count * inner_width,
            transcendentals=row_count * row_count * head_count,
        ),
        name="attend_backward",
    )(
        segment.reshape(row_count, 1),
        segment.reshape(1, row_count),
        heads_grad,
        logsum,
        mixed_all,
        mixed_all,
        mixed_all,
    )


def attention_input(own_chunks, norm_values):
    normals = [normalize(own) for own in own_chunks]
    halves = [
        both_halves((normal * norm_values[0] + norm_values[1]).astype(jnp.bfloat16))
        for normal, _ in normals
    ]
    return normals, halves


def block_forward(own_chunks, halves, segment, pieces, norm_values, head_width, hook):
    halves = hook("input", halves)
    qkv_proj, out_proj = pieces[:2]
    chunk_rows = halves[0].shape[0]
    normed_half = jnp.concatenate(halves, axis=0)
    mixed_all = jnp.dot(normed_half, qkv_proj, preferred_element_type=jnp.float32).astype(
        jnp.bfloat16
    )
    heads_out, logsums, middles = [], [], []
    for place, own in enumerate(own_chunks):
        rows, logsum = attend_forward(mixed_all, segment, place, 1, head_width, chunk_rows)
        if place == 0:
            rows = hook("heads", rows)
        heads_out.append(rows)
        logsums.append(logsum)
        chip_term = chip_sum(
            jnp.einsum("ti,di->td", rows, out_proj, preferred_element_type=jnp.float32)
        )
        middles.append(own + far_sum(chip_term))
    middles = hook("middle", middles)
    up_proj, down_proj = pieces[2:4]
    seconds, outputs, ups = [], [], []
    for middle in middles:
        normal, inverse = normalize(middle)
        normed_two = both_halves((normal * norm_values[2] + norm_values[3]).astype(jnp.bfloat16))
        hidden = jnp.dot(normed_two, up_proj, preferred_element_type=jnp.float32)
        activated, slope = gelu_and_slope(hidden)
        activated = activated.astype(jnp.bfloat16)
        chip_term = chip_sum(
            jnp.einsum("tf,df->td", activated, down_proj, preferred_element_type=jnp.float32)
        )
        outputs.append(middle + far_sum(chip_term))
        seconds.append((normal, inverse))
        ups.append((normed_two, activated, slope))
    return (
        outputs,
        (normed_half, mixed_all, heads_out, logsums, seconds, ups),
    )


def block_backward(
    own_grads, half_grads, saved, firsts, pieces, norm_values, segment, head_width, hook
):
    normed_half, mixed_all, heads_out, logsums, seconds, ups = saved
    qkv_proj, out_proj, up_proj, down_proj = pieces
    chunk_rows = half_grads[0].shape[0]
    down_group = (half_grads, [activated for _, activated, _ in ups])
    half_grads = hook("start", half_grads, down_group)
    hidden_halves, chip_terms = [], []
    for half_grad, (_, _, slope) in zip(half_grads, ups):
        act_grad = jnp.einsum("td,df->tf", half_grad, down_proj, preferred_element_type=jnp.float32)
        hidden_half = (act_grad * slope).astype(jnp.bfloat16)
        hidden_halves.append(hidden_half)
        chip_terms.append(
            chip_sum(
                jnp.einsum("tf,df->td", hidden_half, up_proj, preferred_element_type=jnp.float32)
            )
        )
    up_group = ([normed_two for normed_two, _, _ in ups], hidden_halves)
    normed_grads = hook("sums", [far_sum(chip_term) for chip_term in chip_terms], up_group)
    middle_grads, middle_halves, gain_two, shift_two = [], [], 0.0, 0.0
    for own_grad, chip_term, normed_grad, (normal, inverse) in zip(
        own_grads, chip_terms, normed_grads, seconds
    ):
        gain_two = gain_two + jnp.sum(chip_term * normal, axis=0)
        shift_two = shift_two + jnp.sum(chip_term, axis=0)
        middle_grad = own_grad + normalize_back(normal, inverse, norm_values[2], normed_grad)
        middle_grads.append(middle_grad)
        middle_halves.append(both_halves(middle_grad.astype(jnp.bfloat16)))
    out_group = (middle_halves, heads_out)
    middle_halves = hook("middle", middle_halves, out_group)
    heads_grad = jnp.concatenate(
        [
            jnp.einsum("td,di->ti", half, out_proj, preferred_element_type=jnp.float32).astype(
                jnp.bfloat16
            )
            for half in middle_halves
        ],
        axis=0,
    )
    mixed_grad = attend_backward(
        heads_grad, mixed_all, jnp.concatenate(logsums, axis=1), segment, head_width, chunk_rows
    )
    qkv_group = ([normed_half], [mixed_grad])
    mixed_grad = hook("mixed", mixed_grad, qkv_group)
    chip_terms = [
        chip_sum(
            jnp.einsum(
                "tf,df->td",
                mixed_grad[place * chunk_rows : (place + 1) * chunk_rows],
                qkv_proj,
                preferred_element_type=jnp.float32,
            )
        )
        for place in range(len(own_grads))
    ]
    input_grads, gain_one, shift_one = [], 0.0, 0.0
    for middle_grad, chip_term, (normal, inverse) in zip(middle_grads, chip_terms, firsts):
        gain_one = gain_one + jnp.sum(chip_term * normal, axis=0)
        shift_one = shift_one + jnp.sum(chip_term, axis=0)
        input_grads.append(
            middle_grad
            + normalize_back(normal, inverse, norm_values[0], far_sum(chip_term))
        )
    return (
        input_grads,
        [qkv_group, out_group, up_group, down_group],
        jnp.stack([gain_one, shift_one, gain_two, shift_two]),
    )


def weight_grads_kernel(counts, parity_ref, *refs):
    sent_ref, kept_ref = refs[-2:]
    even = parity_ref[0] == 0
    place, column = 0, 0
    for count in counts:
        total = 0.0
        for k in range(count):
            total = total + lax.dot_general(
                refs[place + k][...],
                refs[place + count + k][...],
                (((0,), (0,)), ((), ())),
                preferred_element_type=jnp.float32,
            )
        half = total.shape[0] // 2
        columns = slice(column, column + total.shape[1])
        upper, lower = total[:half], total[half:]
        sent_ref[:, columns] = jnp.where(even, lower, upper).astype(jnp.bfloat16)
        kept_ref[:, columns] = jnp.where(even, upper, lower).astype(jnp.bfloat16)
        place += 2 * count
        column += total.shape[1]


def weight_grads(groups, parity):
    width = groups[0][0][0].shape[1]
    specs, operands, flops = [], [], 0
    for lefts, rights in groups:
        for left in lefts:
            specs.append(
                pl.BlockSpec((left.shape[0], width // 4), lambda i: (0, i % 2 * 2 + i // 2))
            )
            operands.append(left)
        for right in rights:
            specs.append(pl.BlockSpec(right.shape, lambda i: (0, 0)))
            operands.append(right)
            flops += 2 * width * right.shape[0] * right.shape[1]
    columns = sum(rights[0].shape[1] for _, rights in groups)
    half = jax.ShapeDtypeStruct((width // 2, columns), jnp.bfloat16)
    return pl.pallas_call(
        functools.partial(weight_grads_kernel, [len(lefts) for lefts, _ in groups]),
        grid=(4,),
        in_specs=[pl.BlockSpec(memory_space=pltpu.SMEM)] + specs,
        out_specs=[pl.BlockSpec((width // 8, columns), lambda i: (i, 0))] * 2,
        out_shape=[half, half],
        compiler_params=pltpu.CompilerParams(
            dimension_semantics=("arbitrary",), vmem_limit_bytes=kernel_vmem
        ),
        cost_estimate=pl.CostEstimate(
            flops=flops,
            bytes_accessed=2 * sum(operand.size for operand in operands) + 2 * width * columns,
            transcendentals=0,
        ),
        name="weight_grads",
    )(parity.reshape(1), *operands)


low_set = ((0, 0), (0, 1), (0, 2), (0, 3), (1, 1))
high_set = ((2, 2), (2, 3), (3, 3), (1, 2), (1, 3))


def newton_kernel(
    enc_rows, dec_rows, paired_ref, low_ref, high_ref, own_ref, out_ref, gram_ref, total_ref,
    mix_ref, gram_half_ref, total_half_ref,
):
    size = gram_ref.shape[0]
    block = size // 4
    tile = size // 2

    def in_upper(axis, count, start):
        shape = (count, 1) if axis == 0 else (1, count)
        place = start + lax.broadcasted_iota(jnp.int32, shape, axis)
        return place % enc_rows < dec_rows

    row = lax.broadcasted_iota(jnp.int32, (block, block), 0)
    column = lax.broadcasted_iota(jnp.int32, (block, block), 1)
    upper_trace, whole_trace = 0.0, 0.0
    for places, blocks_ref in ((low_set, low_ref), (high_set, high_ref)):
        for k, (i, j) in enumerate(places):
            value = blocks_ref[k * block : (k + 1) * block, :]
            gram_ref[i * block : (i + 1) * block, j * block : (j + 1) * block] = value
            if i != j:
                gram_ref[j * block : (j + 1) * block, i * block : (i + 1) * block] = value.T
            else:
                diagonal = jnp.where(row == column, value, 0.0)
                whole_trace += jnp.sum(diagonal)
                upper_trace += jnp.sum(
                    jnp.where(in_upper(0, block, i * block), diagonal, 0.0)
                )
    paired = paired_ref[0] == 1
    upper_scale = 1.0 / (jnp.sqrt(jnp.where(paired, upper_trace, whole_trace)) + 1e-07)
    lower_scale = 1.0 / (
        jnp.sqrt(jnp.where(paired, whole_trace - upper_trace, whole_trace)) + 1e-07
    )
    column_scale = jnp.where(in_upper(1, size, 0), upper_scale, lower_scale)

    def rows_of(step):
        return pl.ds(pl.multiple_of(step * tile, tile), tile)

    def times(left, right):
        return jnp.dot(left, right, preferred_element_type=jnp.float32)

    @pl.loop(0, size // tile)
    def _(step):
        rows = rows_of(step)
        row_scale = jnp.where(in_upper(0, tile, step * tile), upper_scale, lower_scale)
        scaled = gram_ref[rows, :] * row_scale * column_scale
        gram_ref[rows, :] = scaled
        gram_half_ref[0, rows, :] = scaled.astype(jnp.bfloat16)

    for newton_step in range(NS_STEPS):
        now, later = newton_step % 2, (newton_step + 1) % 2

        @pl.loop(0, size // tile)
        def _(step):
            rows = rows_of(step)
            square = times(gram_half_ref[now, rows, :], gram_half_ref[now])
            mix = newton_second * gram_ref[rows, :] + newton_third * square
            mix_ref[rows, :] = mix.astype(jnp.bfloat16)
            if newton_step == 0:
                same = lax.broadcasted_iota(
                    jnp.int32, (tile, size), 0
                ) + step * tile == lax.broadcasted_iota(jnp.int32, (tile, size), 1)
                total = jnp.where(same, newton_first, 0.0) + mix
                total_ref[rows, :] = total
                total_half_ref[later, rows, :] = total.astype(jnp.bfloat16)

        @pl.loop(0, size // tile)
        def _(step):
            rows = rows_of(step)
            mix = mix_ref[rows, :]
            if newton_step > 0:
                total = newton_first * total_ref[rows, :] + times(mix, total_half_ref[now])
                if newton_step == NS_STEPS - 1:
                    out_ref[rows, :] = times(
                        (total * column_scale).astype(jnp.bfloat16), own_ref[...]
                    ).astype(jnp.bfloat16)
                else:
                    total_ref[rows, :] = total
                    total_half_ref[later, rows, :] = total.astype(jnp.bfloat16)
            if newton_step < NS_STEPS - 1:
                left = newton_first * gram_ref[rows, :] + times(mix, gram_half_ref[now])
                gram = newton_first * left + times(left.astype(jnp.bfloat16), mix_ref[...])
                gram_ref[rows, :] = gram
                gram_half_ref[later, rows, :] = gram.astype(jnp.bfloat16)


def newton(low_blocks, high_blocks, own, paired, enc_rows, dec_rows):
    size, width = own.shape
    whole = pl.BlockSpec(memory_space=pltpu.VMEM)
    return pl.pallas_call(
        functools.partial(newton_kernel, enc_rows, dec_rows),
        in_specs=[pl.BlockSpec(memory_space=pltpu.SMEM)] + [whole] * 3,
        out_specs=whole,
        out_shape=jax.ShapeDtypeStruct((size, width), jnp.bfloat16),
        scratch_shapes=[
            pltpu.VMEM((size, size), jnp.float32),
            pltpu.VMEM((size, size), jnp.float32),
            pltpu.VMEM((size, size), jnp.bfloat16),
            pltpu.VMEM((2, size, size), jnp.bfloat16),
            pltpu.VMEM((2, size, size), jnp.bfloat16),
        ],
        compiler_params=pltpu.CompilerParams(vmem_limit_bytes=newton_vmem),
        cost_estimate=pl.CostEstimate(
            flops=36 * size * size * size, bytes_accessed=20 * size * size, transcendentals=0
        ),
        name="newton",
    )(paired.astype(jnp.int32).reshape(1), low_blocks, high_blocks, own)


def gram_sum(gram):
    size = gram.shape[0] // 4

    def packed(places):
        return jnp.concatenate(
            [gram[i * size : (i + 1) * size, j * size : (j + 1) * size] for i, j in places],
            axis=0,
        )

    lower_core = lax.axis_index("mp") % 2 == 0
    low_blocks, high_blocks = packed(low_set), packed(high_set)
    own = jnp.where(lower_core, low_blocks, high_blocks)
    own = own + core_swap(jnp.where(lower_core, high_blocks, low_blocks))
    own = own + far_swap(own)
    other = core_swap(own)
    return jnp.where(lower_core, own, other), jnp.where(lower_core, other, own)


enc_slots = (2, 5, 3, 4, 7)
dec_slots = (0, 6)


def slot_rows(enc_rows_half, dec_rows_half, enc_widths, dec_widths, slot_width, data_ranks):
    enc_parts = split_columns(enc_rows_half, enc_widths)
    dec_parts = split_columns(dec_rows_half, dec_widths)
    half_width = slot_width // 2

    def widened(part, width):
        return jnp.pad(part, ((0, 0), (0, width - part.shape[1])))

    empty = jnp.zeros((enc_rows_half.shape[0], slot_width), enc_rows_half.dtype)
    slots = [empty] * data_ranks
    for part, slot in zip(enc_parts, enc_slots):
        slots[slot] = widened(part, slot_width)
    for place, slot in enumerate(dec_slots):
        upper = jnp.pad(widened(dec_parts[2 * place], half_width), ((0, 0), (0, half_width)))
        lower = jnp.pad(widened(dec_parts[2 * place + 1], half_width), ((0, 0), (half_width, 0)))
        slots[slot] = jnp.concatenate([upper, lower], axis=0)
    return jnp.stack(slots)


def unslot(rows_back, enc_widths, dec_widths, dec_rows):
    slot_width = rows_back.shape[2]
    enc_results = [rows_back[slot][:, :width] for slot, width in zip(enc_slots, enc_widths)]
    dec_results = []
    for place, width in enumerate(dec_widths):
        slot = rows_back[dec_slots[place // 2]]
        odd = place % 2
        dec_results.append(
            slot[
                odd * dec_rows : (odd + 1) * dec_rows,
                odd * (slot_width // 2) : odd * (slot_width // 2) + width,
            ]
        )
    return enc_results, dec_results


def apply_step(master, ortho_rows, widths, model_width, rate, model_ranks):
    steps_all = [
        orthogonal * (0.2 * math.sqrt(max(model_width, piece_width * model_ranks)))
        for orthogonal, piece_width in zip(ortho_rows, widths)
    ]
    return master * (1.0 - rate * decay_rate) - rate * jnp.concatenate(steps_all, axis=1)


def local(
    patches,
    cotangent,
    item_lengths,
    enc_master,
    dec_master,
    enc_norms,
    dec_norms,
    enc_moment,
    dec_moment,
    enc_norm_moment,
    dec_norm_moment,
):
    model_ranks = lax.axis_size("mp")
    data_ranks = lax.axis_size("dp")
    enc_widths = [
        3 * D // model_ranks,
        D // model_ranks,
        FF // model_ranks,
        FF // model_ranks,
        DD // model_ranks,
    ]
    dec_widths = [3 * DD // model_ranks, DD // model_ranks, DFF // model_ranks, DFF // model_ranks]
    first_cols = enc_widths[0] + enc_widths[1]
    norm_parts = gather_small(
        jnp.concatenate([enc_norms, dec_norms], axis=1).astype(jnp.bfloat16)
    ).astype(jnp.float32)
    enc_share, dec_share = enc_norms.shape[1], dec_norms.shape[1]
    enc_norm_values = jnp.moveaxis(norm_parts[:, :, :enc_share], 0, 1).reshape(4, D)
    dec_norm_values = jnp.moveaxis(norm_parts[:, :, enc_share:], 0, 1).reshape(4, DD)
    enc_half = enc_master.astype(jnp.bfloat16)
    up_cols = first_cols + enc_widths[2]
    first_gather = Gather(enc_half[:, :first_cols])
    up_gather = Gather(after(enc_half[:, first_cols:up_cols], first_gather.lined))
    rest_gather = Gather(after(enc_half[:, up_cols:], up_gather.lined))
    dec_low = lax.all_gather(
        after(dec_master.astype(jnp.bfloat16), rest_gather.lined), "dp", axis=0, tiled=True
    )
    enc_pieces = split_columns(first_gather.result(), enc_widths[:2])
    dec_pieces = split_columns(dec_low, dec_widths)
    model_rank = lax.axis_index("mp")
    core = model_rank % 2
    upper_chip = model_rank // 2
    row_count = patches.shape[0]
    enc_rows = enc_master.shape[0]
    dec_rows = dec_master.shape[0]
    chunk_count = 2
    chunk_rows = row_count // chunk_count
    own_count = chunk_rows // 2
    segment, live_mask = segments_of(item_lengths[0], row_count)
    segment = swap_halves(segment, chunk_rows, core)
    live_mask = swap_halves(live_mask, chunk_rows, core)
    inputs = swap_halves(patches, chunk_rows, core)
    upstream = swap_halves(cotangent, chunk_rows, core) * live_mask.astype(jnp.bfloat16)[:, None]

    def chunked(array):
        return [array[k * chunk_rows : (k + 1) * chunk_rows] for k in range(chunk_count)]

    slot_width = max(enc_widths)

    def to_owners(enc_part, dec_part):
        slots = slot_rows(
            enc_part.astype(jnp.bfloat16),
            dec_part.astype(jnp.bfloat16),
            enc_widths,
            dec_widths,
            slot_width,
            data_ranks,
        )
        moved = lax.all_to_all(slots, "dp", 0, 0)
        return moved.reshape(-1, slot_width)

    input_chunks = [chunk.astype(jnp.float32) for chunk in chunked(inputs)]
    normals_all = [normalize(chunk) for chunk in input_chunks]
    enc_firsts = [(normal[:own_count], inverse[:own_count]) for normal, inverse in normals_all]
    enc_halves = [
        (normal * enc_norm_values[0] + enc_norm_values[1]).astype(jnp.bfloat16)
        for normal, _ in normals_all
    ]
    late_pieces = {}

    def enc_forward_hook(name, values):
        if name == "input":
            values = up_gather.turn(values)
        if name == "heads":
            values = rest_gather.turn(values)
        if name == "middle":
            down_low, bridge = split_columns(rest_gather.result(), enc_widths[3:])
            enc_pieces.extend([up_gather.result(), down_low, bridge])
            late_pieces["bridge"] = whole_bridge(bridge)
        return values

    def whole_bridge(bridge):
        bridge_far = far_swap(bridge)
        bridge_pair = jnp.where(
            upper_chip == 0, jnp.stack([bridge, bridge_far]), jnp.stack([bridge_far, bridge])
        )
        pair_other = core_swap(bridge_pair)
        bridge_all = jnp.stack(
            [
                jnp.where(core == 0, bridge_pair, pair_other),
                jnp.where(core == 0, pair_other, bridge_pair),
            ],
            axis=1,
        )
        share_width = bridge.shape[1]
        return jnp.moveaxis(bridge_all.reshape(-1, D, share_width), 0, 1).reshape(D, DD)

    encoded, enc_saved = block_forward(
        [chunk[:own_count] for chunk in input_chunks],
        enc_halves,
        segment,
        enc_pieces,
        enc_norm_values,
        HD,
        enc_forward_hook,
    )
    bridge_all = late_pieces["bridge"]
    encoded_own = [chunk.astype(jnp.bfloat16) for chunk in encoded]
    decoder_in = [
        jnp.dot(chunk, bridge_all, preferred_element_type=jnp.float32)
        .astype(jnp.bfloat16)
        .astype(jnp.float32)
        for chunk in encoded_own
    ]
    encoded_halves = [both_halves(chunk) for chunk in encoded_own]
    dec_firsts, dec_halves = attention_input(decoder_in, dec_norm_values)
    decoded, dec_saved = block_forward(
        decoder_in,
        dec_halves,
        segment,
        dec_pieces,
        dec_norm_values,
        DHD,
        lambda name, values: values,
    )
    old_enc, old_dec, _ = lax.optimization_barrier((enc_moment, dec_moment, encoded_own[0]))
    old_slots = to_owners(old_enc, old_dec)
    upstream_halves = chunked(upstream)
    dec_in_grads, dec_groups, dec_norm_grads = block_backward(
        [half[:own_count].astype(jnp.float32) for half in upstream_halves],
        upstream_halves,
        dec_saved,
        dec_firsts,
        dec_pieces,
        dec_norm_values,
        segment,
        DHD,
        lambda name, values, group: values,
    )
    dec_scatter = Scatter(dec_groups)
    bridge_halves = [both_halves(grad.astype(jnp.bfloat16)) for grad in dec_in_grads]
    bridge_halves, old_slots = lax.optimization_barrier((bridge_halves, old_slots))
    encoded_grads = [
        jnp.einsum("tf,df->td", half, bridge_all, preferred_element_type=jnp.float32)
        for half in bridge_halves
    ]
    share_width = enc_widths[4]
    bridge_in_grad = [
        lax.dynamic_slice_in_dim(half, model_rank * share_width, share_width, 1)
        for half in bridge_halves
    ]
    scatters = {}

    def enc_hook(name, values, group):
        if name == "start":
            scatters["down"] = Scatter([group, (encoded_halves, bridge_in_grad)])
        if name == "sums":
            values = dec_scatter.turn(values)
            scatters["up"] = Scatter([group])
        if name == "middle":
            values = dec_scatter.turn(values)
            values = scatters["down"].turn(values)
            scatters["out"] = group
        if name == "mixed":
            values = scatters["down"].turn(values)
            values = scatters["up"].turn(values)
            scatters["late"] = Scatter([group, scatters["out"]])
        return values

    input_grads, _, enc_norm_grads = block_backward(
        [grad[:own_count] for grad in encoded_grads],
        [grad.astype(jnp.bfloat16) for grad in encoded_grads],
        enc_saved,
        enc_firsts,
        enc_pieces[:4],
        enc_norm_values,
        segment,
        HD,
        enc_hook,
    )
    dec_sum_rows = dec_scatter.result()
    up_rows = scatters["up"].result()
    down_rows, bridge_rows = split_columns(scatters["down"].result(), enc_widths[3:])

    half_width = slot_width // 2
    half_rows = [
        jnp.pad(part, ((0, 0), (0, half_width - part.shape[1])))
        for part in split_columns(dec_sum_rows, dec_widths)
    ]

    def owned(slots):
        whole = collect({slot: rows.astype(jnp.bfloat16) for slot, rows in slots.items()})
        return jnp.pad(whole, ((0, 0), (0, slot_width - whole.shape[1])))

    wide_slots = owned(
        {
            enc_slots[2]: up_rows,
            enc_slots[3]: down_rows,
            dec_slots[0]: jnp.concatenate(half_rows[:2], axis=0),
            dec_slots[1]: jnp.concatenate(half_rows[2:], axis=0),
        }
    )

    def natural(own_chunks):
        return swap_halves(
            jnp.concatenate([both_halves(own) for own in own_chunks], axis=0), chunk_rows, core
        )

    decoded = natural(decoded)
    input_grad = natural(input_grads)

    qkv_rows, out_rows = split_columns(scatters["late"].result(), enc_widths[:2])
    enc_sum_rows = jnp.concatenate([qkv_rows, out_rows, up_rows, down_rows, bridge_rows], axis=1)
    norm_sums = sum_everywhere(jnp.concatenate([enc_norm_grads, dec_norm_grads], axis=1))
    data_rank = lax.axis_index("dp")
    enc_norm_rows = lax.dynamic_slice_in_dim(norm_sums[:, :D], data_rank * enc_share, enc_share, 1)
    dec_norm_rows = lax.dynamic_slice_in_dim(norm_sums[:, D:], data_rank * dec_share, dec_share, 1)
    local_sum = jnp.sum(enc_sum_rows * enc_sum_rows) + jnp.sum(dec_sum_rows * dec_sum_rows)
    squares = sum_everywhere(jnp.full((8, 128), local_sum))[0, 0] + jnp.sum(norm_sums * norm_sums)
    (qkv_rows, out_rows), wide_slots = lax.optimization_barrier(((qkv_rows, out_rows), wide_slots))
    late_slots = owned({enc_slots[0]: qkv_rows, enc_slots[1]: out_rows, enc_slots[4]: bridge_rows})
    data_rank = lax.axis_index("dp")

    def is_rank(*slots):
        return functools.reduce(jnp.logical_or, [data_rank == slot for slot in slots])

    lower_row = (jnp.arange(wide_slots.shape[0], dtype=jnp.int32) % enc_rows >= dec_rows)[:, None]
    shifted = jnp.where(
        lower_row, jnp.roll(wide_slots, half_width, axis=1), wide_slots
    )
    grad_slots = jnp.where(
        is_rank(*enc_slots[2:4]),
        wide_slots,
        jnp.where(is_rank(*dec_slots), shifted, late_slots),
    )
    grad_norm = jnp.sqrt(squares)
    factor = clip_bound * lax.rsqrt(squares + 1e-06)
    enc_grad = enc_sum_rows * factor
    dec_grad = dec_sum_rows * factor
    enc_norm_grad = enc_norm_rows * factor
    dec_norm_grad = dec_norm_rows * factor
    dec_shift_grad = dec_norm_grad[3]
    enc_moment_new = momentum_keep * enc_moment + enc_grad
    dec_moment_new = momentum_keep * dec_moment + dec_grad
    enc_norm_moment_new = momentum_keep * enc_norm_moment + enc_norm_grad
    dec_norm_moment_new = momentum_keep * dec_norm_moment + dec_norm_grad
    own = (
        momentum_keep * old_slots.astype(jnp.float32)
        + factor * grad_slots.astype(jnp.float32)
    ).astype(jnp.bfloat16)
    low_blocks, high_blocks = gram_sum(
        lax.dot_general(own, own, (((1,), (1,)), ((), ())), preferred_element_type=jnp.float32)
    )
    orthogonal = newton(low_blocks, high_blocks, own, is_rank(*dec_slots), enc_rows, dec_rows)
    rows_back = lax.all_to_all(
        orthogonal.reshape(data_ranks, enc_rows, slot_width), "dp", 0, 0
    ).astype(jnp.float32)
    enc_results, dec_results = unslot(rows_back, enc_widths, dec_widths, dec_rows)
    enc_master_new = apply_step(enc_master, enc_results, enc_widths, D, rate_enc, model_ranks)
    dec_master_new = apply_step(dec_master, dec_results, dec_widths, DD, rate_dec, model_ranks)
    enc_norms_new = enc_norms - rate_norm * enc_norm_moment_new
    dec_norms_new = dec_norms - rate_norm * dec_norm_moment_new
    return (
        decoded,
        input_grad,
        enc_grad,
        dec_grad,
        enc_norm_grad,
        dec_norm_grad,
        dec_shift_grad,
        enc_moment_new,
        dec_moment_new,
        enc_norm_moment_new,
        dec_norm_moment_new,
        enc_master_new,
        dec_master_new,
        enc_norms_new,
        dec_norms_new,
        enc_master_new.astype(jnp.bfloat16),
        dec_master_new.astype(jnp.bfloat16),
        enc_norms_new.astype(jnp.bfloat16),
        dec_norms_new.astype(jnp.bfloat16),
        grad_norm,
    )


def solution(mesh):
    return jax.shard_map(
        local,
        mesh=mesh,
        in_specs=(
            P("dp", None),
            P("dp", None),
            P("dp", None),
            P("dp", "mp"),
            P("dp", "mp"),
            P(None, "dp"),
            P(None, "dp"),
            P("dp", "mp"),
            P("dp", "mp"),
            P(None, "dp"),
            P(None, "dp"),
        ),
        out_specs=(
            P("dp", None),
            P("dp", None),
            P("dp", "mp"),
            P("dp", "mp"),
            P(None, "dp"),
            P(None, "dp"),
            P("dp"),
            P("dp", "mp"),
            P("dp", "mp"),
            P(None, "dp"),
            P(None, "dp"),
            P("dp", "mp"),
            P("dp", "mp"),
            P(None, "dp"),
            P(None, "dp"),
            P("dp", "mp"),
            P("dp", "mp"),
            P(None, "dp"),
            P(None, "dp"),
            P(),
        ),
        check_vma=False,
    )
```

```python
import functools
import math

import jax
import jax.numpy as jnp
from jax import lax
from jax.experimental import pallas as pl
from jax.experimental.pallas import tpu as pltpu
from jax.sharding import PartitionSpec as P

D = 1024
HD = 64
FF = 4096
DD = 512
DHD = 32
DFF = 2048
NS_STEPS = 5


highest = lax.Precision.HIGHEST
ln_eps = 1e-06
masked_score = -1e30
newton_first = 3.4445
newton_second = -4.775
newton_third = 2.0315
momentum_keep = 0.5
clip_bound = 100.0
rate_enc = 0.2
rate_dec = 0.3
rate_norm = 1.0
decay_rate = 0.01
kernel_vmem = 32 * 1024 * 1024
newton_vmem = 48 * 1024 * 1024
grads_vmem = 58 * 1024 * 1024


def shortened(array):

    def short(part):
        return part.astype(jnp.bfloat16) if part.dtype == jnp.float32 else part

    return jax.tree.map(short, array)


def pair_swap(array, axis, bit):
    size = lax.axis_size(axis)
    return lax.ppermute(array, axis, [(rank, rank ^ bit) for rank in range(size)])


def core_swap(array):
    return pair_swap(array, "mp", 1)


def far_swap(array):
    return pair_swap(array, "mp", 2)


def far_sum(chip_term):
    half = chip_term.astype(jnp.bfloat16)
    return half.astype(jnp.float32) + far_swap(half).astype(jnp.float32)


def chip_sum(own_term, other_term):
    return own_term + core_swap(other_term.astype(jnp.bfloat16)).astype(jnp.float32)


def shared(own_parts):
    return [part for own in own_parts for part in (own, core_swap(own))]


def paired(parts):
    return list(zip(parts[::2], parts[1::2]))


def times(left, right):
    return jnp.dot(left, right, preferred_element_type=jnp.float32)


def times_turned(left, right):
    return jnp.einsum("tf,df->td", left, right, preferred_element_type=jnp.float32)


def gather_small(array):
    rank = lax.axis_index("dp")
    gathered = array[None]
    bit = 1
    while bit < lax.axis_size("dp"):
        other = pair_swap(gathered, "dp", bit)
        lower = (rank & bit) == 0
        gathered = jnp.concatenate(
            [jnp.where(lower, gathered, other), jnp.where(lower, other, gathered)], axis=0
        )
        bit *= 2
    return gathered


def assemble_kernel(rank_ref, *refs):
    whole_ref = refs[-1]
    rows = refs[0].shape[0]
    for bit, part_ref in enumerate(refs[:-1]):
        place = pl.multiple_of((rank_ref[0] ^ bit) * rows, rows)
        whole_ref[pl.ds(place, rows), :] = part_ref[...]


def assemble(parts, place):
    rows, columns = parts[0].shape
    spec = pl.BlockSpec(memory_space=pltpu.VMEM)
    return pl.pallas_call(
        assemble_kernel,
        in_specs=[pl.BlockSpec(memory_space=pltpu.SMEM)] + [spec] * len(parts),
        out_specs=spec,
        out_shape=jax.ShapeDtypeStruct((len(parts) * rows, columns), parts[0].dtype),
        compiler_params=pltpu.CompilerParams(vmem_limit_bytes=grads_vmem),
        cost_estimate=pl.CostEstimate(
            flops=0, bytes_accessed=4 * len(parts) * rows * columns, transcendentals=0
        ),
        name="assemble",
    )(place.reshape(1), *parts)


class Gather:
    def __init__(self, array):
        self.general = lax.axis_size("dp") != 8
        if self.general:
            self.whole = lax.all_gather(array, "dp", axis=0, tiled=True)
            self.lined = [array]
        else:
            self.lined = [array] + [pair_swap(array, "dp", 2 * bit) for bit in (1, 2, 3)]
            self.crossed = None

    def turn(self, values):
        if self.general:
            return values
        values, self.lined = lax.optimization_barrier((values, self.lined))
        self.cross()
        return values

    def cross(self):
        self.crossed = [pair_swap(part, "dp", 1) for part in self.lined]

    def result(self):
        if self.general:
            return self.whole
        if self.crossed is None:
            self.cross()
        parts = [part for pair in zip(self.lined, self.crossed) for part in pair]
        return assemble(parts, lax.axis_index("dp"))


def collect_values(slots):
    ranks = lax.axis_size("dp")
    rank = lax.axis_index("dp")
    width = max(rows.shape[1] for rows in slots.values())
    padded = {
        owner: jnp.pad(rows.astype(jnp.bfloat16), ((0, 0), (0, width - rows.shape[1])))
        for owner, rows in slots.items()
    }
    values = []
    for bit in range(ranks):
        value = None
        for owner, rows in padded.items():
            value = rows if value is None else jnp.where(rank ^ bit == owner, rows, value)
        values.append(value)
    return values


def collect_parts(values, owners):
    return values[:1] + [
        lax.ppermute(value, "dp", [(owner ^ bit, owner) for owner in owners])
        for bit, value in enumerate(values)
        if bit
    ]


def cross_pair(even_rows, odd_rows):
    even = lax.axis_index("dp") % 2 == 0
    kept = jnp.where(even, even_rows, odd_rows)
    return kept, pair_swap(jnp.where(even, odd_rows, even_rows), "dp", 1)


def line_pair(kept, crossed, owners):
    even = lax.axis_index("dp") % 2 == 0
    lined = jnp.concatenate(
        [jnp.where(even, kept, crossed), jnp.where(even, crossed, kept)], axis=0
    )
    return [lined] + [
        lax.ppermute(lined, "dp", [(owner ^ (2 * bit), owner) for owner in owners])
        for bit in range(1, lax.axis_size("dp") // 2)
    ]


def after(value, anchor):
    return lax.optimization_barrier((value, anchor))[0]


def fold(kept, received):
    return (kept.astype(jnp.float32) + received.astype(jnp.float32)).astype(jnp.bfloat16)


def split_rows(array, place):
    half = array.shape[0] // 2
    return (
        lax.dynamic_slice_in_dim(array, (1 - place) * half, half, 0),
        lax.dynamic_slice_in_dim(array, place * half, half, 0),
    )


class Scatter:
    def __init__(self, groups):
        self.phase = 0
        self.general = lax.axis_size("dp") != 8
        self.rank = lax.axis_index("dp")
        self.sent = self.kept = self.received = None
        if self.general:
            whole = jnp.concatenate(
                [
                    jnp.einsum(
                        "td,tf->df",
                        jnp.concatenate(lefts, axis=0),
                        jnp.concatenate(rights, axis=0),
                        preferred_element_type=jnp.float32,
                    ).astype(jnp.bfloat16)
                    for lefts, rights in groups
                ],
                axis=1,
            )
            self.total = lax.psum_scatter(whole, "dp", scatter_dimension=0, tiled=True)
        else:
            self.sent, self.kept = weight_grads(groups, self.rank % 2)

    def send(self):
        if not self.general:
            self.received = pair_swap(self.sent, "dp", 1 << self.phase)

    def fold(self):
        if not self.general:
            place = self.rank // 2 % 2 if self.phase == 0 else self.rank // 4
            self.sent, self.kept = split_rows(fold(self.kept, self.received), place)
            self.phase += 1

    def result(self):
        if self.general:
            return self.total.astype(jnp.float32)
        return self.kept.astype(jnp.float32) + self.received.astype(jnp.float32)


class HopSum:
    def __init__(self, value):
        self.value = value
        self.hops = [
            (axis, 1 << bit)
            for axis in ("mp", "dp")
            for bit in range(lax.axis_size(axis).bit_length() - 1)
        ]

    def step(self, count):
        for axis, bit in self.hops[:count]:
            self.value = self.value + pair_swap(self.value, axis, bit)
        self.hops = self.hops[count:]

    def finish(self):
        self.step(len(self.hops))
        return self.value


def normalize(values):
    center = values - jnp.mean(values, axis=-1, keepdims=True)
    inverse = lax.rsqrt(jnp.mean(center * center, axis=-1, keepdims=True) + ln_eps)
    return center * inverse, inverse


def normalize_back(normal, inverse, gain_row, out_grad):
    scaled = out_grad * gain_row
    mean_grad = jnp.mean(scaled, axis=-1, keepdims=True)
    mean_dot = jnp.mean(scaled * normal, axis=-1, keepdims=True)
    return inverse * (scaled - mean_grad - normal * mean_dot)


def gelu_and_slope(hidden):
    spread = 0.5 + 0.5 * lax.erf(hidden * math.sqrt(0.5))
    density = jnp.exp(-0.5 * hidden * hidden) * (1.0 / math.sqrt(2.0 * math.pi))
    return hidden * spread, spread + hidden * density


def swap_halves(array, chunk_rows, core):
    parts = array.reshape((-1, 2, chunk_rows // 2) + array.shape[1:])
    return jnp.where(core == 0, parts, parts[:, ::-1]).reshape(array.shape)


def segments_of(lengths, row_count):
    item_ends = jnp.cumsum(lengths)
    position = jnp.arange(row_count, dtype=jnp.int32)
    segment = jnp.sum((position[:, None] >= item_ends[None, :]).astype(jnp.int32), axis=1)
    live_mask = (position < item_ends[-1]).astype(jnp.float32)
    return (segment, live_mask)


def split_columns(whole_cols, widths):
    pieces = []
    start_col = 0
    for piece_width in widths:
        pieces.append(whole_cols[:, start_col : start_col + piece_width])
        start_col += piece_width
    return pieces


def head_mask(head, head_width, inner_width):
    lane = lax.broadcasted_iota(jnp.int32, (1, inner_width), 1)
    inside = jnp.logical_and(lane >= head * head_width, lane < (head + 1) * head_width)
    return jnp.where(inside, 1.0, 0.0)


def masked_rows(rows, head, head_width):
    mask = head_mask(head, head_width, rows.shape[1])
    return (rows.astype(jnp.float32) * mask).astype(jnp.bfloat16)


def last_dims(left, right):
    return lax.dot_general(
        left, right, (((1,), (1,)), ((), ())), preferred_element_type=jnp.float32
    )


def segment_bias(key_segment_ref, query_segment_ref):
    return jnp.where(key_segment_ref[...] == query_segment_ref[...], 0.0, masked_score)


def joined_columns(refs, first, last):
    return jnp.concatenate([ref[:, first:last] for ref in refs], axis=0)


def attend_forward_kernel(
    head_width, place, count, key_segment_ref, query_segment_ref, *refs
):
    mixed_refs, (own_ref, other_ref, logsum_ref) = refs[:count], refs[count:]
    block_rows = query_segment_ref.shape[0]
    half_rows, inner_width = own_ref.shape
    score_scale = head_width ** (-0.5)
    bias = segment_bias(key_segment_ref, query_segment_ref)
    if count == 1:
        rows = mixed_refs[0][place * block_rows : (place + 1) * block_rows, :inner_width]
    else:
        rows = joined_columns(mixed_refs[2 * place : 2 * place + 2], 0, inner_width)
    keys = joined_columns(mixed_refs, inner_width, 2 * inner_width)
    values = joined_columns(mixed_refs, 2 * inner_width, 3 * inner_width)
    total_out = jnp.zeros((block_rows, inner_width), jnp.float32)
    logsums = []
    for head in range(inner_width // head_width):
        scores = last_dims(masked_rows(rows, head, head_width), keys) * score_scale + bias
        top = jnp.max(scores, axis=1, keepdims=True)
        shifted = jnp.exp(scores - top)
        total = jnp.sum(shifted, axis=1, keepdims=True)
        part = times(shifted.astype(jnp.bfloat16), values)
        total_out += part * (head_mask(head, head_width, inner_width) / total)
        logsums.append(jnp.broadcast_to(top + jnp.log(total), (block_rows, 128)))
    own_ref[...] = total_out[:half_rows].astype(jnp.bfloat16)
    other_ref[...] = total_out[half_rows:].astype(jnp.bfloat16)
    lane = lax.broadcasted_iota(jnp.int32, (block_rows, 128), 1)
    stacked = logsums[0]
    for head in range(1, len(logsums)):
        stacked = jnp.where(lane == head, logsums[head], stacked)
    logsum_ref[...] = stacked.T[: len(logsums), :]


def attend_forward(mixed, segment, place, head_width, block_rows):
    row_count = segment.shape[0]
    inner_width = mixed[0].shape[1] // 3
    head_count = inner_width // head_width
    whole = pl.BlockSpec(memory_space=pltpu.VMEM)
    half = jax.ShapeDtypeStruct((block_rows // 2, inner_width), jnp.bfloat16)
    return pl.pallas_call(
        functools.partial(attend_forward_kernel, head_width, place, len(mixed)),
        in_specs=[whole] * (2 + len(mixed)),
        out_specs=[whole] * 3,
        out_shape=[half, half, jax.ShapeDtypeStruct((head_count, block_rows), jnp.float32)],
        compiler_params=pltpu.CompilerParams(vmem_limit_bytes=kernel_vmem),
        cost_estimate=pl.CostEstimate(
            flops=4 * block_rows * row_count * inner_width * head_count,
            bytes_accessed=8 * row_count * inner_width,
            transcendentals=block_rows * row_count * head_count,
        ),
        name="attend_forward",
    )(
        segment.reshape(1, row_count),
        segment[place * block_rows : (place + 1) * block_rows].reshape(block_rows, 1),
        *mixed,
    )


def attend_backward_kernel(head_width, count, key_segment_ref, query_segment_ref, *refs):
    grad_refs, logsum_refs, refs = refs[:4], refs[4:6], refs[6:]
    mixed_refs, out_refs, refs = refs[:count], refs[count : count + 4], refs[count + 4 :]
    turned_ref, grad_ref, query_ref, bias_ref, query_grad_ref, key_total_ref, value_total_ref = refs
    row_count, inner_width = grad_ref.shape
    part_rows = row_count // 4
    block_rows = row_count // 2
    score_scale = head_width ** (-0.5)
    keys = joined_columns(mixed_refs, inner_width, 2 * inner_width)
    values = joined_columns(mixed_refs, 2 * inner_width, 3 * inner_width)
    turned_ref[...] = keys.astype(jnp.float32).T.astype(jnp.bfloat16)
    for k in range(4):
        grad_ref[k * part_rows : (k + 1) * part_rows, :] = grad_refs[k][...]
    query_ref[...] = joined_columns(mixed_refs, 0, inner_width)
    key_total_ref[...] = jnp.zeros_like(key_total_ref)
    value_total_ref[...] = jnp.zeros_like(value_total_ref)
    for block in range(2):
        bias_ref[block] = jnp.where(
            key_segment_ref[...]
            == query_segment_ref[:, block * block_rows : (block + 1) * block_rows],
            0.0,
            masked_score,
        )

    @pl.loop(0, 2)
    def _(block):
        rows = pl.ds(pl.multiple_of(block * block_rows, block_rows), block_rows)
        parts = []
        for head in range(inner_width // head_width):
            query = masked_rows(query_ref[rows, :], head, head_width)
            grad = masked_rows(grad_ref[rows, :], head, head_width)
            logsum = jnp.where(
                block == 0,
                logsum_refs[0][head : head + 1, :],
                logsum_refs[1][head : head + 1, :],
            )
            scores = last_dims(keys, query) * score_scale + bias_ref[block]
            attention = jnp.exp(scores - logsum)
            weighted = attention * last_dims(values, grad)
            row_dot = jnp.sum(weighted, axis=0, keepdims=True)
            score_grad = (weighted - attention * row_dot).astype(jnp.bfloat16)
            value_total_ref[...] += times(attention.astype(jnp.bfloat16), grad)
            key_total_ref[...] += times(score_grad, query)
            parts.append(
                times(turned_ref[head * head_width : (head + 1) * head_width, :], score_grad)
            )
        query_grad_ref[rows, :] = (jnp.concatenate(parts, axis=0) * score_scale).T

    for k, out_ref in enumerate(out_refs):
        rows = slice(k * part_rows, (k + 1) * part_rows)
        out_ref[:, :inner_width] = query_grad_ref[rows, :].astype(jnp.bfloat16)
        out_ref[:, inner_width : 2 * inner_width] = (key_total_ref[rows, :] * score_scale).astype(
            jnp.bfloat16
        )
        out_ref[:, 2 * inner_width :] = value_total_ref[rows, :].astype(jnp.bfloat16)


def attend_backward(heads_grads, mixed, logsums, segment, head_width):
    row_count = segment.shape[0]
    part_rows, inner_width = heads_grads[0].shape
    head_count = inner_width // head_width
    whole = pl.BlockSpec(memory_space=pltpu.VMEM)
    part = jax.ShapeDtypeStruct((part_rows, 3 * inner_width), jnp.bfloat16)
    return pl.pallas_call(
        functools.partial(attend_backward_kernel, head_width, len(mixed)),
        in_specs=[whole] * (8 + len(mixed)),
        out_specs=[whole] * 4,
        out_shape=[part] * 4,
        scratch_shapes=[
            pltpu.VMEM((inner_width, row_count), jnp.bfloat16),
            pltpu.VMEM((row_count, inner_width), jnp.bfloat16),
            pltpu.VMEM((row_count, inner_width), jnp.bfloat16),
            pltpu.VMEM((2, row_count, row_count // 2), jnp.float32),
            pltpu.VMEM((row_count, inner_width), jnp.float32),
            pltpu.VMEM((row_count, inner_width), jnp.float32),
            pltpu.VMEM((row_count, inner_width), jnp.float32),
        ],
        compiler_params=pltpu.CompilerParams(vmem_limit_bytes=kernel_vmem),
        cost_estimate=pl.CostEstimate(
            flops=10 * row_count * row_count * inner_width * head_count,
            bytes_accessed=14 * row_count * inner_width,
            transcendentals=row_count * row_count * head_count,
        ),
        name="attend_backward",
    )(
        segment.reshape(row_count, 1),
        segment.reshape(1, row_count),
        *heads_grads,
        *logsums,
        *mixed,
    )


def block_forward(own_chunks, rows, segment, pieces, norm_values, head_width, hook):
    qkv_proj, out_proj = pieces[:2]
    mixed = [times(part, qkv_proj).astype(jnp.bfloat16) for part in rows]
    block_rows = segment.shape[0] // len(own_chunks)
    heads, logsums, middles = [], [], []
    for place, own in enumerate(own_chunks):
        own_heads, other_heads, logsum = attend_forward(
            mixed, segment, place, head_width, block_rows
        )
        heads += [own_heads, other_heads]
        logsums.append(logsum)
        chip_term = chip_sum(
            times_turned(own_heads, out_proj), times_turned(other_heads, out_proj)
        )
        middles.append(own + far_sum(chip_term))
    middles = hook("middle", middles)
    up_proj, down_proj = pieces[2:4]
    seconds, chip_terms, ups, activated, slopes = [], [], [], [], []
    for middle in middles:
        normal, inverse = normalize(middle)
        parts = shared([(normal * norm_values[2] + norm_values[3]).astype(jnp.bfloat16)])
        partials = []
        for part in parts:
            value, slope = gelu_and_slope(times(part, up_proj))
            value = value.astype(jnp.bfloat16)
            partials.append(times_turned(value, down_proj))
            activated.append(value)
            slopes.append(slope)
        ups += parts
        chip_terms.append(chip_sum(*partials))
        seconds.append((normal, inverse))
    return middles, chip_terms, (rows, mixed, heads, logsums, seconds, ups, activated, slopes)


def block_backward(
    own_grads, half_rows, saved, firsts, pieces, norm_values, segment, head_width, hook
):
    rows, mixed, heads, logsums, seconds, ups, activated, slopes = saved
    qkv_proj, out_proj, up_proj, down_proj = pieces
    down_group = (half_rows, activated)
    half_rows = hook("start", half_rows, down_group)
    hidden_rows = [
        (times(half, down_proj) * slope).astype(jnp.bfloat16)
        for half, slope in zip(half_rows, slopes)
    ]
    chip_terms = [
        chip_sum(times_turned(own, up_proj), times_turned(other, up_proj))
        for own, other in paired(hidden_rows)
    ]
    up_group = (ups, hidden_rows)
    normed_grads = hook("sums", [far_sum(chip_term) for chip_term in chip_terms], up_group)
    middle_grads, gain_two, shift_two = [], 0.0, 0.0
    for own_grad, chip_term, normed_grad, (normal, inverse) in zip(
        own_grads, chip_terms, normed_grads, seconds
    ):
        gain_two = gain_two + jnp.sum(chip_term * normal, axis=0)
        shift_two = shift_two + jnp.sum(chip_term, axis=0)
        middle_grads.append(
            own_grad + normalize_back(normal, inverse, norm_values[2], normed_grad)
        )
    middle_rows = shared([grad.astype(jnp.bfloat16) for grad in middle_grads])
    out_group = (middle_rows, heads)
    middle_rows = hook("middle", middle_rows, out_group)
    heads_grads = [times(part, out_proj).astype(jnp.bfloat16) for part in middle_rows]
    mixed_grads = attend_backward(heads_grads, mixed, logsums, segment, head_width)
    qkv_group = (rows, mixed_grads)
    mixed_grads = hook("mixed", mixed_grads, qkv_group)
    chip_terms = [
        chip_sum(times_turned(own, qkv_proj), times_turned(other, qkv_proj))
        for own, other in paired(mixed_grads)
    ]
    gain_one, shift_one = 0.0, 0.0
    for chip_term, (normal, _) in zip(chip_terms, firsts):
        gain_one = gain_one + jnp.sum(chip_term * normal, axis=0)
        shift_one = shift_one + jnp.sum(chip_term, axis=0)
    norm_grads = jnp.stack([gain_one, shift_one, gain_two, shift_two])
    groups = [qkv_group, out_group, up_group, down_group]
    return chip_terms, middle_grads, groups, norm_grads


def block_input_grads(far_sums, middle_grads, firsts, norm_values):
    return [
        middle_grad + normalize_back(normal, inverse, norm_values[0], normed_grad)
        for middle_grad, normed_grad, (normal, inverse) in zip(middle_grads, far_sums, firsts)
    ]


def row_pieces(refs, count):
    if len(refs) == count:
        return [ref[...] for ref in refs]
    rows = refs[0].shape[0] // count
    return [refs[0][k * rows : (k + 1) * rows, :] for k in range(count)]


def weight_grads_kernel(counts, parity_ref, *refs):
    sent_ref, kept_ref = refs[-2:]
    even = parity_ref[0] == 0
    place, column = 0, 0
    for left_count, right_count in counts:
        count = max(left_count, right_count)
        lefts = row_pieces(refs[place : place + left_count], count)
        place += left_count
        rights = row_pieces(refs[place : place + right_count], count)
        place += right_count
        total = 0.0
        for left, right in zip(lefts, rights):
            total = total + lax.dot_general(
                left, right, (((0,), (0,)), ((), ())), preferred_element_type=jnp.float32
            )
        half = total.shape[0] // 2
        columns = slice(column, column + total.shape[1])
        upper, lower = total[:half], total[half:]
        sent_ref[:, columns] = jnp.where(even, lower, upper).astype(jnp.bfloat16)
        kept_ref[:, columns] = jnp.where(even, upper, lower).astype(jnp.bfloat16)
        column += total.shape[1]


def weight_grads(groups, parity):
    width = groups[0][0][0].shape[1]
    specs, operands, flops = [], [], 0
    for lefts, rights in groups:
        for left in lefts:
            specs.append(
                pl.BlockSpec((left.shape[0], width // 4), lambda i: (0, i % 2 * 2 + i // 2))
            )
            operands.append(left)
        for right in rights:
            specs.append(pl.BlockSpec(right.shape, lambda i: (0, 0)))
            operands.append(right)
            flops += 2 * width * right.shape[0] * right.shape[1]
    columns = sum(rights[0].shape[1] for _, rights in groups)
    half = jax.ShapeDtypeStruct((width // 2, columns), jnp.bfloat16)
    return pl.pallas_call(
        functools.partial(
            weight_grads_kernel, [(len(lefts), len(rights)) for lefts, rights in groups]
        ),
        grid=(4,),
        in_specs=[pl.BlockSpec(memory_space=pltpu.SMEM)] + specs,
        out_specs=[pl.BlockSpec((width // 8, columns), lambda i: (i, 0))] * 2,
        out_shape=[half, half],
        compiler_params=pltpu.CompilerParams(
            dimension_semantics=("arbitrary",), vmem_limit_bytes=grads_vmem
        ),
        cost_estimate=pl.CostEstimate(
            flops=flops,
            bytes_accessed=2 * sum(operand.size for operand in operands) + 2 * width * columns,
            transcendentals=0,
        ),
        name="weight_grads",
    )(parity.reshape(1), *operands)


low_set = ((0, 0), (0, 1), (0, 2), (0, 3), (1, 1))
high_set = ((2, 2), (2, 3), (3, 3), (1, 2), (1, 3))


def newton_kernel(
    enc_rows, dec_rows, paired_ref, low_ref, high_ref, own_ref, out_ref, gram_ref, total_ref,
    mix_ref, gram_half_ref, total_half_ref,
):
    size = gram_ref.shape[0]
    block = size // 4
    tile = size // 2

    def in_upper(axis, count, start):
        shape = (count, 1) if axis == 0 else (1, count)
        place = start + lax.broadcasted_iota(jnp.int32, shape, axis)
        return place % enc_rows < dec_rows

    row = lax.broadcasted_iota(jnp.int32, (block, block), 0)
    column = lax.broadcasted_iota(jnp.int32, (block, block), 1)
    upper_trace, whole_trace = 0.0, 0.0
    for places, blocks_ref in ((low_set, low_ref), (high_set, high_ref)):
        for k, (i, j) in enumerate(places):
            value = blocks_ref[k * block : (k + 1) * block, :]
            gram_ref[i * block : (i + 1) * block, j * block : (j + 1) * block] = value
            if i != j:
                gram_ref[j * block : (j + 1) * block, i * block : (i + 1) * block] = value.T
            else:
                diagonal = jnp.where(row == column, value, 0.0)
                whole_trace += jnp.sum(diagonal)
                upper_trace += jnp.sum(
                    jnp.where(in_upper(0, block, i * block), diagonal, 0.0)
                )
    paired = paired_ref[0] == 1
    upper_scale = 1.0 / (jnp.sqrt(jnp.where(paired, upper_trace, whole_trace)) + 1e-07)
    lower_scale = 1.0 / (
        jnp.sqrt(jnp.where(paired, whole_trace - upper_trace, whole_trace)) + 1e-07
    )
    column_scale = jnp.where(in_upper(1, size, 0), upper_scale, lower_scale)

    def rows_of(step):
        return pl.ds(pl.multiple_of(step * tile, tile), tile)

    def times(left, right):
        return jnp.dot(left, right, preferred_element_type=jnp.float32)

    @pl.loop(0, size // tile)
    def _(step):
        rows = rows_of(step)
        row_scale = jnp.where(in_upper(0, tile, step * tile), upper_scale, lower_scale)
        scaled = gram_ref[rows, :] * row_scale * column_scale
        gram_ref[rows, :] = scaled
        gram_half_ref[0, rows, :] = scaled.astype(jnp.bfloat16)

    for newton_step in range(NS_STEPS):
        now, later = newton_step % 2, (newton_step + 1) % 2

        @pl.loop(0, size // tile)
        def _(step):
            rows = rows_of(step)
            square = times(gram_half_ref[now, rows, :], gram_half_ref[now])
            mix = newton_second * gram_ref[rows, :] + newton_third * square
            mix_ref[rows, :] = mix.astype(jnp.bfloat16)
            if newton_step == 0:
                same = lax.broadcasted_iota(
                    jnp.int32, (tile, size), 0
                ) + step * tile == lax.broadcasted_iota(jnp.int32, (tile, size), 1)
                total = jnp.where(same, newton_first, 0.0) + mix
                total_ref[rows, :] = total
                total_half_ref[later, rows, :] = total.astype(jnp.bfloat16)

        @pl.loop(0, size // tile)
        def _(step):
            rows = rows_of(step)
            mix = mix_ref[rows, :]
            if newton_step > 0:
                total = newton_first * total_ref[rows, :] + times(mix, total_half_ref[now])
                if newton_step == NS_STEPS - 1:
                    out_ref[rows, :] = times(
                        (total * column_scale).astype(jnp.bfloat16), own_ref[...]
                    ).astype(jnp.bfloat16)
                else:
                    total_ref[rows, :] = total
                    total_half_ref[later, rows, :] = total.astype(jnp.bfloat16)
            if newton_step < NS_STEPS - 1:
                left = newton_first * gram_ref[rows, :] + times(mix, gram_half_ref[now])
                gram = newton_first * left + times(left.astype(jnp.bfloat16), mix_ref[...])
                gram_ref[rows, :] = gram
                gram_half_ref[later, rows, :] = gram.astype(jnp.bfloat16)


def newton(low_blocks, high_blocks, own, paired, enc_rows, dec_rows):
    size, width = own.shape
    whole = pl.BlockSpec(memory_space=pltpu.VMEM)
    return pl.pallas_call(
        functools.partial(newton_kernel, enc_rows, dec_rows),
        in_specs=[pl.BlockSpec(memory_space=pltpu.SMEM)] + [whole] * 3,
        out_specs=whole,
        out_shape=jax.ShapeDtypeStruct((size, width), jnp.bfloat16),
        scratch_shapes=[
            pltpu.VMEM((size, size), jnp.float32),
            pltpu.VMEM((size, size), jnp.float32),
            pltpu.VMEM((size, size), jnp.bfloat16),
            pltpu.VMEM((2, size, size), jnp.bfloat16),
            pltpu.VMEM((2, size, size), jnp.bfloat16),
        ],
        compiler_params=pltpu.CompilerParams(vmem_limit_bytes=newton_vmem),
        cost_estimate=pl.CostEstimate(
            flops=36 * size * size * size, bytes_accessed=20 * size * size, transcendentals=0
        ),
        name="newton",
    )(paired.astype(jnp.int32).reshape(1), low_blocks, high_blocks, own)


def gram_sum(gram):
    size = gram.shape[0] // 4

    def packed(places):
        return jnp.concatenate(
            [gram[i * size : (i + 1) * size, j * size : (j + 1) * size] for i, j in places],
            axis=0,
        )

    lower_core = lax.axis_index("mp") % 2 == 0
    low_blocks, high_blocks = packed(low_set), packed(high_set)
    own = jnp.where(lower_core, low_blocks, high_blocks)
    own = own + core_swap(jnp.where(lower_core, high_blocks, low_blocks))
    own = own + far_swap(own)
    other = core_swap(own)
    return jnp.where(lower_core, own, other), jnp.where(lower_core, other, own)


enc_slots = (2, 5, 3, 4, 6)
dec_slots = (0, 7)


def slot_rows(enc_rows_half, dec_rows_half, enc_widths, dec_widths, slot_width, data_ranks):
    enc_parts = split_columns(enc_rows_half, enc_widths)
    dec_parts = split_columns(dec_rows_half, dec_widths)
    half_width = slot_width // 2

    def widened(part, width):
        return jnp.pad(part, ((0, 0), (0, width - part.shape[1])))

    empty = jnp.zeros((enc_rows_half.shape[0], slot_width), enc_rows_half.dtype)
    slots = [empty] * data_ranks
    for part, slot in zip(enc_parts, enc_slots):
        slots[slot] = widened(part, slot_width)
    for place, slot in enumerate(dec_slots):
        upper = jnp.pad(widened(dec_parts[2 * place], half_width), ((0, 0), (0, half_width)))
        lower = jnp.pad(widened(dec_parts[2 * place + 1], half_width), ((0, 0), (half_width, 0)))
        slots[slot] = jnp.concatenate([upper, lower], axis=0)
    return jnp.stack(slots)


def unslot(rows_back, enc_widths, dec_widths, dec_rows):
    slot_width = rows_back.shape[2]
    enc_results = [rows_back[slot][:, :width] for slot, width in zip(enc_slots, enc_widths)]
    dec_results = []
    for place, width in enumerate(dec_widths):
        slot = rows_back[dec_slots[place // 2]]
        odd = place % 2
        dec_results.append(
            slot[
                odd * dec_rows : (odd + 1) * dec_rows,
                odd * (slot_width // 2) : odd * (slot_width // 2) + width,
            ]
        )
    return enc_results, dec_results


def apply_step(master, ortho_rows, widths, model_width, rate, model_ranks):
    steps_all = [
        orthogonal * (0.2 * math.sqrt(max(model_width, piece_width * model_ranks)))
        for orthogonal, piece_width in zip(ortho_rows, widths)
    ]
    return master * (1.0 - rate * decay_rate) - rate * jnp.concatenate(steps_all, axis=1)


def local(
    patches,
    cotangent,
    item_lengths,
    enc_master,
    dec_master,
    enc_norms,
    dec_norms,
    enc_moment,
    dec_moment,
    enc_norm_moment,
    dec_norm_moment,
):
    model_ranks = lax.axis_size("mp")
    data_ranks = lax.axis_size("dp")
    enc_widths = [
        3 * D // model_ranks,
        D // model_ranks,
        FF // model_ranks,
        FF // model_ranks,
        DD // model_ranks,
    ]
    dec_widths = [3 * DD // model_ranks, DD // model_ranks, DFF // model_ranks, DFF // model_ranks]
    first_cols = enc_widths[0] + enc_widths[1]
    norm_parts = gather_small(
        jnp.concatenate([enc_norms, dec_norms], axis=1).astype(jnp.bfloat16)
    ).astype(jnp.float32)
    enc_share, dec_share = enc_norms.shape[1], dec_norms.shape[1]
    enc_norm_values = jnp.moveaxis(norm_parts[:, :, :enc_share], 0, 1).reshape(4, D)
    dec_norm_values = jnp.moveaxis(norm_parts[:, :, enc_share:], 0, 1).reshape(4, DD)
    enc_half = enc_master.astype(jnp.bfloat16)
    first_gather = Gather(enc_half[:, :first_cols])
    rest_low = lax.all_gather(
        after(enc_half[:, first_cols:], first_gather.lined), "dp", axis=0, tiled=True
    )
    dec_low = lax.all_gather(
        after(dec_master.astype(jnp.bfloat16), first_gather.lined), "dp", axis=0, tiled=True
    )
    enc_pieces = split_columns(first_gather.result(), enc_widths[:2])
    dec_pieces = split_columns(dec_low, dec_widths)
    model_rank = lax.axis_index("mp")
    core = model_rank % 2
    upper_chip = model_rank // 2
    row_count = patches.shape[0]
    enc_rows = enc_master.shape[0]
    dec_rows = dec_master.shape[0]
    chunk_count = 2
    chunk_rows = row_count // chunk_count
    own_count = chunk_rows // 2
    segment, live_mask = segments_of(item_lengths[0], row_count)
    segment = swap_halves(segment, chunk_rows, core)
    live_mask = swap_halves(live_mask, chunk_rows, core)
    inputs = swap_halves(patches, chunk_rows, core)
    upstream = swap_halves(cotangent, chunk_rows, core) * live_mask.astype(jnp.bfloat16)[:, None]

    slot_width = max(enc_widths)

    def to_owners(enc_part, dec_part):
        slots = slot_rows(
            enc_part.astype(jnp.bfloat16),
            dec_part.astype(jnp.bfloat16),
            enc_widths,
            dec_widths,
            slot_width,
            data_ranks,
        )
        moved = lax.all_to_all(slots, "dp", 0, 0)
        return moved.reshape(-1, slot_width)

    input_normal, input_inverse = normalize(inputs.astype(jnp.float32))
    own_places = [slice(k * chunk_rows, k * chunk_rows + own_count) for k in range(chunk_count)]
    enc_firsts = [(input_normal[place], input_inverse[place]) for place in own_places]
    enc_rows_in = [
        (input_normal * enc_norm_values[0] + enc_norm_values[1]).astype(jnp.bfloat16)
    ]
    late_pieces = {}

    def enc_forward_hook(name, values):
        if name == "middle":
            enc_pieces.extend(split_columns(rest_low, enc_widths[2:]))
            late_pieces["bridge"] = whole_bridge(enc_pieces[4])
        return values

    def whole_bridge(bridge):
        bridge_far = far_swap(bridge)
        bridge_pair = jnp.where(
            upper_chip == 0, jnp.stack([bridge, bridge_far]), jnp.stack([bridge_far, bridge])
        )
        pair_other = core_swap(bridge_pair)
        bridge_all = jnp.stack(
            [
                jnp.where(core == 0, bridge_pair, pair_other),
                jnp.where(core == 0, pair_other, bridge_pair),
            ],
            axis=1,
        )
        share_width = bridge.shape[1]
        return jnp.moveaxis(bridge_all.reshape(-1, D, share_width), 0, 1).reshape(D, DD)

    enc_middles, enc_terms, enc_saved = block_forward(
        [inputs[place].astype(jnp.float32) for place in own_places],
        enc_rows_in,
        segment,
        enc_pieces,
        enc_norm_values,
        HD,
        enc_forward_hook,
    )
    bridge_all = late_pieces["bridge"]
    encoded_own = [
        (middle + far_sum(term)).astype(jnp.bfloat16)
        for middle, term in zip(enc_middles, enc_terms)
    ]
    decoder_in = [
        times(chunk, bridge_all).astype(jnp.bfloat16).astype(jnp.float32) for chunk in encoded_own
    ]
    encoded_rows = shared(encoded_own)
    dec_firsts = [normalize(chunk) for chunk in decoder_in]
    dec_rows_in = shared(
        [
            (normal * dec_norm_values[0] + dec_norm_values[1]).astype(jnp.bfloat16)
            for normal, _ in dec_firsts
        ]
    )
    dec_outs, dec_out_terms, dec_saved = block_forward(
        decoder_in,
        dec_rows_in,
        segment,
        dec_pieces,
        dec_norm_values,
        DHD,
        lambda name, values: values,
    )
    old_enc, old_dec, _ = lax.optimization_barrier((enc_moment, dec_moment, encoded_own[0]))
    old_slots = to_owners(old_enc, old_dec)
    upstream_rows = [
        upstream[k * own_count : (k + 1) * own_count] for k in range(2 * chunk_count)
    ]
    dec_terms, dec_middles, dec_groups, dec_norm_grads = block_backward(
        [half.astype(jnp.float32) for half in upstream_rows[::2]],
        upstream_rows,
        dec_saved,
        dec_firsts,
        dec_pieces,
        dec_norm_values,
        segment,
        DHD,
        lambda name, values, group: values,
    )
    dec_scatter = Scatter(dec_groups)
    dec_far_sums, dec_scatter.sent = lax.optimization_barrier(
        ([far_sum(term) for term in dec_terms], dec_scatter.sent)
    )
    dec_scatter.send()
    dec_in_grads = block_input_grads(dec_far_sums, dec_middles, dec_firsts, dec_norm_values)
    bridge_rows_in = shared([grad.astype(jnp.bfloat16) for grad in dec_in_grads])
    bridge_rows_in, old_slots = lax.optimization_barrier((bridge_rows_in, old_slots))
    encoded_grads = [times_turned(part, bridge_all) for part in bridge_rows_in]
    share_width = enc_widths[4]
    bridge_in_grad = [
        lax.dynamic_slice_in_dim(part, model_rank * share_width, share_width, 1)
        for part in bridge_rows_in
    ]
    scatters = {}

    def joined(values, *background):
        values, received = lax.optimization_barrier(
            (values, [scatter.received for scatter in background])
        )
        for scatter, piece in zip(background, received):
            scatter.received = piece
            scatter.fold()
        return values

    def enc_hook(name, values, group):
        if name == "start":
            scatters["down"] = Scatter([group, (encoded_rows, bridge_in_grad)])
            scatters["down"].send()
        if name == "sums":
            values = joined(values, dec_scatter)
            dec_scatter.send()
            scatters["up"] = Scatter([group])
            values, scatters["up"].sent = lax.optimization_barrier((values, scatters["up"].sent))
            scatters["up"].send()
        if name == "middle":
            values = joined(values, dec_scatter, scatters["down"])
            dec_scatter.send()
            scatters["down"].send()
            scatters["out"] = group
        if name == "mixed":
            late = scatters["late"] = Scatter([group, scatters["out"]])
            late.send()
            values = after(values, late.sent)
            values, dec_scatter.received = joined(
                (values, dec_scatter.received), scatters["down"], scatters["up"]
            )
            scatters["up"].send()
            scatters["down"].send()
        return values

    enc_back_terms, enc_middle_grads, _, enc_norm_grads = block_backward(
        encoded_grads[::2],
        [grad.astype(jnp.bfloat16) for grad in encoded_grads],
        enc_saved,
        enc_firsts,
        enc_pieces[:4],
        enc_norm_values,
        segment,
        HD,
        enc_hook,
    )
    late, up, down = (scatters[name] for name in ("late", "up", "down"))
    norm_hops = HopSum(jnp.concatenate([enc_norm_grads, dec_norm_grads], axis=1))
    norm_hops.step(2)
    enc_back_terms, norm_hops.value, down.received = joined(
        (enc_back_terms, norm_hops.value, down.received), late, up
    )
    late.send()
    up.send()
    norm_hops.step(1)
    enc_far_sums = [far_sum(term) for term in enc_back_terms]
    dec_sum_rows = dec_scatter.result()
    down_rows, bridge_rows = split_columns(down.result(), enc_widths[3:])
    half_width = slot_width // 2
    half_rows = [
        jnp.pad(part, ((0, 0), (0, half_width - part.shape[1])))
        for part in split_columns(dec_sum_rows, dec_widths)
    ]
    narrow = {
        dec_slots[0]: jnp.concatenate(half_rows[:2], axis=0),
        dec_slots[1]: jnp.concatenate(half_rows[2:], axis=0),
        enc_slots[4]: bridge_rows,
    }
    narrow_parts = collect_parts(collect_values(narrow), narrow)
    norm_hops.value, up.received = joined((norm_hops.value, up.received), late)
    up_rows = up.result()
    up_half, down_half = up_rows.astype(jnp.bfloat16), down_rows.astype(jnp.bfloat16)
    late.sent, up_half, down_half = lax.optimization_barrier((late.sent, up_half, down_half))
    late.send()
    wide_crossed = cross_pair(down_half, up_half)
    norm_hops.step(1)
    late.received, wide_crossed, norm_hops.value, enc_far_sums, narrow_parts = (
        lax.optimization_barrier(
            (late.received, wide_crossed, norm_hops.value, enc_far_sums, narrow_parts)
        )
    )
    qkv_rows, out_rows = split_columns(late.result(), enc_widths[:2])
    out_padded = jnp.pad(out_rows, ((0, 0), (0, enc_widths[0] - enc_widths[1])))
    tail_crossed = cross_pair(qkv_rows.astype(jnp.bfloat16), out_padded.astype(jnp.bfloat16))
    wide_parts = line_pair(*wide_crossed, enc_slots[2:4])
    norm_sums = norm_hops.finish()
    data_rank = lax.axis_index("dp")
    enc_sum_rows = jnp.concatenate([qkv_rows, out_rows, up_rows, down_rows, bridge_rows], axis=1)
    local_sum = jnp.sum(enc_sum_rows * enc_sum_rows) + jnp.sum(dec_sum_rows * dec_sum_rows)
    square_hops = HopSum(jnp.full((8, 128), local_sum))
    squares = square_hops.finish()[0, 0]
    tail_crossed, squares, norm_sums = lax.optimization_barrier((tail_crossed, squares, norm_sums))
    squares = squares + jnp.sum(norm_sums * norm_sums)
    tail_parts = line_pair(*tail_crossed, enc_slots[:2])

    def owned(parts, place):
        whole = assemble(parts, place)
        return jnp.pad(whole, ((0, 0), (0, slot_width - whole.shape[1])))

    late_slots = owned(tail_parts, data_rank // 2)
    wide_slots = owned(wide_parts, data_rank // 2)
    narrow_slots = owned(narrow_parts, data_rank)
    enc_norm_rows = lax.dynamic_slice_in_dim(norm_sums[:, :D], data_rank * enc_share, enc_share, 1)
    dec_norm_rows = lax.dynamic_slice_in_dim(norm_sums[:, D:], data_rank * dec_share, dec_share, 1)
    input_grads = block_input_grads(
        enc_far_sums, enc_middle_grads, enc_firsts, enc_norm_values
    )

    def natural(own_chunks):
        return swap_halves(jnp.concatenate(shared(own_chunks), axis=0), chunk_rows, core)

    dec_out_terms, _ = lax.optimization_barrier((dec_out_terms, late.received))
    decoded = [middle + far_sum(term) for middle, term in zip(dec_outs, dec_out_terms)]
    decoded = natural(decoded)
    input_grad = natural(input_grads)
    data_rank = lax.axis_index("dp")

    def is_rank(*slots):
        return functools.reduce(jnp.logical_or, [data_rank == slot for slot in slots])

    lower_row = (jnp.arange(wide_slots.shape[0], dtype=jnp.int32) % enc_rows >= dec_rows)[:, None]
    shifted = jnp.where(
        jnp.logical_and(lower_row, is_rank(*dec_slots)),
        jnp.roll(narrow_slots, half_width, axis=1),
        narrow_slots,
    )
    grad_slots = jnp.where(
        is_rank(*enc_slots[2:4]),
        wide_slots,
        jnp.where(is_rank(*enc_slots[:2]), late_slots, shifted),
    )
    grad_norm = jnp.sqrt(squares)
    factor = clip_bound * lax.rsqrt(squares + 1e-06)
    enc_grad = enc_sum_rows * factor
    dec_grad = dec_sum_rows * factor
    enc_norm_grad = enc_norm_rows * factor
    dec_norm_grad = dec_norm_rows * factor
    dec_shift_grad = dec_norm_grad[3]
    enc_moment_new = momentum_keep * enc_moment + enc_grad
    dec_moment_new = momentum_keep * dec_moment + dec_grad
    enc_norm_moment_new = momentum_keep * enc_norm_moment + enc_norm_grad
    dec_norm_moment_new = momentum_keep * dec_norm_moment + dec_norm_grad
    own = (
        momentum_keep * old_slots.astype(jnp.float32)
        + factor * grad_slots.astype(jnp.float32)
    ).astype(jnp.bfloat16)
    low_blocks, high_blocks = gram_sum(
        lax.dot_general(own, own, (((1,), (1,)), ((), ())), preferred_element_type=jnp.float32)
    )
    orthogonal = newton(low_blocks, high_blocks, own, is_rank(*dec_slots), enc_rows, dec_rows)
    rows_back = lax.all_to_all(
        orthogonal.reshape(data_ranks, enc_rows, slot_width), "dp", 0, 0
    ).astype(jnp.float32)
    enc_results, dec_results = unslot(rows_back, enc_widths, dec_widths, dec_rows)
    enc_master_new = apply_step(enc_master, enc_results, enc_widths, D, rate_enc, model_ranks)
    dec_master_new = apply_step(dec_master, dec_results, dec_widths, DD, rate_dec, model_ranks)
    enc_norms_new = enc_norms - rate_norm * enc_norm_moment_new
    dec_norms_new = dec_norms - rate_norm * dec_norm_moment_new
    return (
        decoded,
        input_grad,
        enc_grad,
        dec_grad,
        enc_norm_grad,
        dec_norm_grad,
        dec_shift_grad,
        enc_moment_new,
        dec_moment_new,
        enc_norm_moment_new,
        dec_norm_moment_new,
        enc_master_new,
        dec_master_new,
        enc_norms_new,
        dec_norms_new,
        enc_master_new.astype(jnp.bfloat16),
        dec_master_new.astype(jnp.bfloat16),
        enc_norms_new.astype(jnp.bfloat16),
        dec_norms_new.astype(jnp.bfloat16),
        grad_norm,
    )


def solution(mesh):
    return jax.shard_map(
        local,
        mesh=mesh,
        in_specs=(
            P("dp", None),
            P("dp", None),
            P("dp", None),
            P("dp", "mp"),
            P("dp", "mp"),
            P(None, "dp"),
            P(None, "dp"),
            P("dp", "mp"),
            P("dp", "mp"),
            P(None, "dp"),
            P(None, "dp"),
        ),
        out_specs=(
            P("dp", None),
            P("dp", None),
            P("dp", "mp"),
            P("dp", "mp"),
            P(None, "dp"),
            P(None, "dp"),
            P("dp"),
            P("dp", "mp"),
            P("dp", "mp"),
            P(None, "dp"),
            P(None, "dp"),
            P("dp", "mp"),
            P("dp", "mp"),
            P(None, "dp"),
            P(None, "dp"),
            P("dp", "mp"),
            P("dp", "mp"),
            P(None, "dp"),
            P(None, "dp"),
            P(),
        ),
        check_vma=False,
    )
```

```python
import functools
import math

import jax
import jax.numpy as jnp
from jax import lax
from jax.experimental import pallas as pl
from jax.experimental.pallas import tpu as pltpu
from jax.sharding import PartitionSpec as P

D = 1024
HD = 64
FF = 4096
DD = 512
DHD = 32
DFF = 2048
NS_STEPS = 5


highest = lax.Precision.HIGHEST
ln_eps = 1e-06
masked_score = -1e30
newton_first = 3.4445
newton_second = -4.775
newton_third = 2.0315
momentum_keep = 0.5
clip_bound = 100.0
rate_enc = 0.2
rate_dec = 0.3
rate_norm = 1.0
decay_rate = 0.01
kernel_vmem = 32 * 1024 * 1024
newton_vmem = 48 * 1024 * 1024
grads_vmem = 58 * 1024 * 1024


def shortened(array):

    def short(part):
        return part.astype(jnp.bfloat16) if part.dtype == jnp.float32 else part

    return jax.tree.map(short, array)


def pair_swap(array, axis, bit):
    size = lax.axis_size(axis)
    return lax.ppermute(array, axis, [(rank, rank ^ bit) for rank in range(size)])


def core_swap(array):
    return pair_swap(array, "mp", 1)


def far_swap(array):
    return pair_swap(array, "mp", 2)


def far_sum(chip_term):
    half = chip_term.astype(jnp.bfloat16)
    return half.astype(jnp.float32) + far_swap(half).astype(jnp.float32)


def chip_sum(own_term, other_term):
    return own_term + core_swap(other_term.astype(jnp.bfloat16)).astype(jnp.float32)


def shared(own_parts):
    return [part for own in own_parts for part in (own, core_swap(own))]


def paired(parts):
    return list(zip(parts[::2], parts[1::2]))


def times(left, right):
    return jnp.dot(left, right, preferred_element_type=jnp.float32)


def times_turned(left, right):
    return jnp.einsum("tf,df->td", left, right, preferred_element_type=jnp.float32)


def gather_small(array):
    rank = lax.axis_index("dp")
    gathered = array[None]
    bit = 1
    while bit < lax.axis_size("dp"):
        other = pair_swap(gathered, "dp", bit)
        lower = (rank & bit) == 0
        gathered = jnp.concatenate(
            [jnp.where(lower, gathered, other), jnp.where(lower, other, gathered)], axis=0
        )
        bit *= 2
    return gathered


def assemble_kernel(rank_ref, *refs):
    whole_ref = refs[-1]
    rows = refs[0].shape[0]
    for bit, part_ref in enumerate(refs[:-1]):
        place = pl.multiple_of((rank_ref[0] ^ bit) * rows, rows)
        whole_ref[pl.ds(place, rows), :] = part_ref[...]


def assemble(parts, place):
    rows, columns = parts[0].shape
    spec = pl.BlockSpec(memory_space=pltpu.VMEM)
    return pl.pallas_call(
        assemble_kernel,
        in_specs=[pl.BlockSpec(memory_space=pltpu.SMEM)] + [spec] * len(parts),
        out_specs=spec,
        out_shape=jax.ShapeDtypeStruct((len(parts) * rows, columns), parts[0].dtype),
        compiler_params=pltpu.CompilerParams(vmem_limit_bytes=grads_vmem),
        cost_estimate=pl.CostEstimate(
            flops=0, bytes_accessed=4 * len(parts) * rows * columns, transcendentals=0
        ),
        name="assemble",
    )(place.reshape(1), *parts)


class Gather:
    def __init__(self, array):
        self.general = lax.axis_size("dp") != 8
        if self.general:
            self.whole = lax.all_gather(array, "dp", axis=0, tiled=True)
            self.lined = [array]
        else:
            self.lined = [array] + [pair_swap(array, "dp", 2 * bit) for bit in (1, 2, 3)]
            self.crossed = None

    def turn(self, values):
        if self.general:
            return values
        values, self.lined = lax.optimization_barrier((values, self.lined))
        self.cross()
        return values

    def cross(self):
        self.crossed = [pair_swap(part, "dp", 1) for part in self.lined]

    def result(self):
        if self.general:
            return self.whole
        if self.crossed is None:
            self.cross()
        parts = [part for pair in zip(self.lined, self.crossed) for part in pair]
        return assemble(parts, lax.axis_index("dp"))


def collect_values(slots):
    ranks = lax.axis_size("dp")
    rank = lax.axis_index("dp")
    width = max(rows.shape[1] for rows in slots.values())
    padded = {
        owner: jnp.pad(rows.astype(jnp.bfloat16), ((0, 0), (0, width - rows.shape[1])))
        for owner, rows in slots.items()
    }
    values = []
    for bit in range(ranks):
        value = None
        for owner, rows in padded.items():
            value = rows if value is None else jnp.where(rank ^ bit == owner, rows, value)
        values.append(value)
    return values


def collect_parts(values, owners):
    return values[:1] + [
        lax.ppermute(value, "dp", [(owner ^ bit, owner) for owner in owners])
        for bit, value in enumerate(values)
        if bit
    ]


def cross_pair(even_rows, odd_rows):
    even = lax.axis_index("dp") % 2 == 0
    kept = jnp.where(even, even_rows, odd_rows)
    return kept, pair_swap(jnp.where(even, odd_rows, even_rows), "dp", 1)


def line_pair(kept, crossed, owners):
    even = lax.axis_index("dp") % 2 == 0
    lined = jnp.concatenate(
        [jnp.where(even, kept, crossed), jnp.where(even, crossed, kept)], axis=0
    )
    return [lined] + [
        lax.ppermute(lined, "dp", [(owner ^ (2 * bit), owner) for owner in owners])
        for bit in range(1, lax.axis_size("dp") // 2)
    ]


def after(value, anchor):
    return lax.optimization_barrier((value, anchor))[0]


def fold(kept, received):
    return (kept.astype(jnp.float32) + received.astype(jnp.float32)).astype(jnp.bfloat16)


def split_rows(array, place):
    half = array.shape[0] // 2
    return (
        lax.dynamic_slice_in_dim(array, (1 - place) * half, half, 0),
        lax.dynamic_slice_in_dim(array, place * half, half, 0),
    )


class Scatter:
    def __init__(self, groups):
        self.phase = 0
        self.general = lax.axis_size("dp") != 8
        self.rank = lax.axis_index("dp")
        self.sent = self.kept = self.received = None
        if self.general:
            whole = jnp.concatenate(
                [
                    jnp.einsum(
                        "td,tf->df",
                        jnp.concatenate(lefts, axis=0),
                        jnp.concatenate(rights, axis=0),
                        preferred_element_type=jnp.float32,
                    ).astype(jnp.bfloat16)
                    for lefts, rights in groups
                ],
                axis=1,
            )
            self.total = lax.psum_scatter(whole, "dp", scatter_dimension=0, tiled=True)
        else:
            self.sent, self.kept = weight_grads(groups, self.rank % 2)

    def send(self):
        if not self.general:
            self.received = pair_swap(self.sent, "dp", 1 << self.phase)

    def fold(self):
        if not self.general:
            place = self.rank // 2 % 2 if self.phase == 0 else self.rank // 4
            self.sent, self.kept = split_rows(fold(self.kept, self.received), place)
            self.phase += 1

    def result(self):
        if self.general:
            return self.total.astype(jnp.float32)
        return self.kept.astype(jnp.float32) + self.received.astype(jnp.float32)


class HopSum:
    def __init__(self, value):
        self.value = value
        self.hops = [
            (axis, 1 << bit)
            for axis in ("mp", "dp")
            for bit in range(lax.axis_size(axis).bit_length() - 1)
        ]

    def step(self, count):
        for axis, bit in self.hops[:count]:
            self.value = self.value + pair_swap(self.value, axis, bit)
        self.hops = self.hops[count:]

    def finish(self):
        self.step(len(self.hops))
        return self.value


def normalize(values):
    center = values - jnp.mean(values, axis=-1, keepdims=True)
    inverse = lax.rsqrt(jnp.mean(center * center, axis=-1, keepdims=True) + ln_eps)
    return center * inverse, inverse


def normalize_back(normal, inverse, gain_row, out_grad):
    scaled = out_grad * gain_row
    mean_grad = jnp.mean(scaled, axis=-1, keepdims=True)
    mean_dot = jnp.mean(scaled * normal, axis=-1, keepdims=True)
    return inverse * (scaled - mean_grad - normal * mean_dot)


def gelu_and_slope(hidden):
    spread = 0.5 + 0.5 * lax.erf(hidden * math.sqrt(0.5))
    density = jnp.exp(-0.5 * hidden * hidden) * (1.0 / math.sqrt(2.0 * math.pi))
    return hidden * spread, spread + hidden * density


def swap_halves(array, chunk_rows, core):
    parts = array.reshape((-1, 2, chunk_rows // 2) + array.shape[1:])
    return jnp.where(core == 0, parts, parts[:, ::-1]).reshape(array.shape)


def segments_of(lengths, row_count):
    item_ends = jnp.cumsum(lengths)
    position = jnp.arange(row_count, dtype=jnp.int32)
    segment = jnp.sum((position[:, None] >= item_ends[None, :]).astype(jnp.int32), axis=1)
    live_mask = (position < item_ends[-1]).astype(jnp.float32)
    return (segment, live_mask)


def split_columns(whole_cols, widths):
    pieces = []
    start_col = 0
    for piece_width in widths:
        pieces.append(whole_cols[:, start_col : start_col + piece_width])
        start_col += piece_width
    return pieces


def head_mask(head, head_width, inner_width):
    lane = lax.broadcasted_iota(jnp.int32, (1, inner_width), 1)
    inside = jnp.logical_and(lane >= head * head_width, lane < (head + 1) * head_width)
    return jnp.where(inside, 1.0, 0.0)


def masked_rows(rows, head, head_width):
    mask = head_mask(head, head_width, rows.shape[1])
    return (rows.astype(jnp.float32) * mask).astype(jnp.bfloat16)


def last_dims(left, right):
    return lax.dot_general(
        left, right, (((1,), (1,)), ((), ())), preferred_element_type=jnp.float32
    )


def segment_bias(key_segment_ref, query_segment_ref):
    return jnp.where(key_segment_ref[...] == query_segment_ref[...], 0.0, masked_score)


def joined_columns(refs, first, last):
    return jnp.concatenate([ref[:, first:last] for ref in refs], axis=0)


def attend_forward_kernel(
    head_width, place, count, key_segment_ref, query_segment_ref, *refs
):
    mixed_refs, (own_ref, other_ref, logsum_ref) = refs[:count], refs[count:]
    block_rows = query_segment_ref.shape[0]
    half_rows, inner_width = own_ref.shape
    score_scale = head_width ** (-0.5)
    bias = segment_bias(key_segment_ref, query_segment_ref)
    if count == 1:
        rows = mixed_refs[0][place * block_rows : (place + 1) * block_rows, :inner_width]
    else:
        rows = joined_columns(mixed_refs[2 * place : 2 * place + 2], 0, inner_width)
    keys = joined_columns(mixed_refs, inner_width, 2 * inner_width)
    values = joined_columns(mixed_refs, 2 * inner_width, 3 * inner_width)
    total_out = jnp.zeros((block_rows, inner_width), jnp.float32)
    logsums = []
    for head in range(inner_width // head_width):
        scores = last_dims(masked_rows(rows, head, head_width), keys) * score_scale + bias
        top = jnp.max(scores, axis=1, keepdims=True)
        shifted = jnp.exp(scores - top)
        total = jnp.sum(shifted, axis=1, keepdims=True)
        part = times(shifted.astype(jnp.bfloat16), values)
        total_out += part * (head_mask(head, head_width, inner_width) / total)
        logsums.append(jnp.broadcast_to(top + jnp.log(total), (block_rows, 128)))
    own_ref[...] = total_out[:half_rows].astype(jnp.bfloat16)
    other_ref[...] = total_out[half_rows:].astype(jnp.bfloat16)
    lane = lax.broadcasted_iota(jnp.int32, (block_rows, 128), 1)
    stacked = logsums[0]
    for head in range(1, len(logsums)):
        stacked = jnp.where(lane == head, logsums[head], stacked)
    logsum_ref[...] = stacked.T[: len(logsums), :]


def attend_forward(mixed, segment, place, head_width, block_rows):
    row_count = segment.shape[0]
    inner_width = mixed[0].shape[1] // 3
    head_count = inner_width // head_width
    whole = pl.BlockSpec(memory_space=pltpu.VMEM)
    half = jax.ShapeDtypeStruct((block_rows // 2, inner_width), jnp.bfloat16)
    return pl.pallas_call(
        functools.partial(attend_forward_kernel, head_width, place, len(mixed)),
        in_specs=[whole] * (2 + len(mixed)),
        out_specs=[whole] * 3,
        out_shape=[half, half, jax.ShapeDtypeStruct((head_count, block_rows), jnp.float32)],
        compiler_params=pltpu.CompilerParams(vmem_limit_bytes=kernel_vmem),
        cost_estimate=pl.CostEstimate(
            flops=4 * block_rows * row_count * inner_width * head_count,
            bytes_accessed=8 * row_count * inner_width,
            transcendentals=block_rows * row_count * head_count,
        ),
        name="attend_forward",
    )(
        segment.reshape(1, row_count),
        segment[place * block_rows : (place + 1) * block_rows].reshape(block_rows, 1),
        *mixed,
    )


def attend_backward_kernel(head_width, count, key_segment_ref, query_segment_ref, *refs):
    grad_refs, logsum_refs, refs = refs[:4], refs[4:6], refs[6:]
    mixed_refs, out_refs, refs = refs[:count], refs[count : count + 4], refs[count + 4 :]
    turned_ref, grad_ref, query_ref, bias_ref, query_grad_ref, key_total_ref, value_total_ref = refs
    row_count, inner_width = grad_ref.shape
    part_rows = row_count // 4
    block_rows = row_count // 2
    score_scale = head_width ** (-0.5)
    keys = joined_columns(mixed_refs, inner_width, 2 * inner_width)
    values = joined_columns(mixed_refs, 2 * inner_width, 3 * inner_width)
    turned_ref[...] = keys.astype(jnp.float32).T.astype(jnp.bfloat16)
    for k in range(4):
        grad_ref[k * part_rows : (k + 1) * part_rows, :] = grad_refs[k][...]
    query_ref[...] = joined_columns(mixed_refs, 0, inner_width)
    key_total_ref[...] = jnp.zeros_like(key_total_ref)
    value_total_ref[...] = jnp.zeros_like(value_total_ref)
    for block in range(2):
        bias_ref[block] = jnp.where(
            key_segment_ref[...]
            == query_segment_ref[:, block * block_rows : (block + 1) * block_rows],
            0.0,
            masked_score,
        )

    @pl.loop(0, 2)
    def _(block):
        rows = pl.ds(pl.multiple_of(block * block_rows, block_rows), block_rows)
        parts = []
        for head in range(inner_width // head_width):
            query = masked_rows(query_ref[rows, :], head, head_width)
            grad = masked_rows(grad_ref[rows, :], head, head_width)
            logsum = jnp.where(
                block == 0,
                logsum_refs[0][head : head + 1, :],
                logsum_refs[1][head : head + 1, :],
            )
            scores = last_dims(keys, query) * score_scale + bias_ref[block]
            attention = jnp.exp(scores - logsum)
            weighted = attention * last_dims(values, grad)
            row_dot = jnp.sum(weighted, axis=0, keepdims=True)
            score_grad = (weighted - attention * row_dot).astype(jnp.bfloat16)
            value_total_ref[...] += times(attention.astype(jnp.bfloat16), grad)
            key_total_ref[...] += times(score_grad, query)
            parts.append(
                times(turned_ref[head * head_width : (head + 1) * head_width, :], score_grad)
            )
        query_grad_ref[rows, :] = (jnp.concatenate(parts, axis=0) * score_scale).T

    for k, out_ref in enumerate(out_refs):
        rows = slice(k * part_rows, (k + 1) * part_rows)
        out_ref[:, :inner_width] = query_grad_ref[rows, :].astype(jnp.bfloat16)
        out_ref[:, inner_width : 2 * inner_width] = (key_total_ref[rows, :] * score_scale).astype(
            jnp.bfloat16
        )
        out_ref[:, 2 * inner_width :] = value_total_ref[rows, :].astype(jnp.bfloat16)


def attend_backward(heads_grads, mixed, logsums, segment, head_width):
    row_count = segment.shape[0]
    part_rows, inner_width = heads_grads[0].shape
    head_count = inner_width // head_width
    whole = pl.BlockSpec(memory_space=pltpu.VMEM)
    part = jax.ShapeDtypeStruct((part_rows, 3 * inner_width), jnp.bfloat16)
    return pl.pallas_call(
        functools.partial(attend_backward_kernel, head_width, len(mixed)),
        in_specs=[whole] * (8 + len(mixed)),
        out_specs=[whole] * 4,
        out_shape=[part] * 4,
        scratch_shapes=[
            pltpu.VMEM((inner_width, row_count), jnp.bfloat16),
            pltpu.VMEM((row_count, inner_width), jnp.bfloat16),
            pltpu.VMEM((row_count, inner_width), jnp.bfloat16),
            pltpu.VMEM((2, row_count, row_count // 2), jnp.float32),
            pltpu.VMEM((row_count, inner_width), jnp.float32),
            pltpu.VMEM((row_count, inner_width), jnp.float32),
            pltpu.VMEM((row_count, inner_width), jnp.float32),
        ],
        compiler_params=pltpu.CompilerParams(vmem_limit_bytes=kernel_vmem),
        cost_estimate=pl.CostEstimate(
            flops=10 * row_count * row_count * inner_width * head_count,
            bytes_accessed=14 * row_count * inner_width,
            transcendentals=row_count * row_count * head_count,
        ),
        name="attend_backward",
    )(
        segment.reshape(row_count, 1),
        segment.reshape(1, row_count),
        *heads_grads,
        *logsums,
        *mixed,
    )


def block_forward(own_chunks, rows, segment, pieces, norm_values, head_width, hook):
    qkv_proj, out_proj = pieces[:2]
    mixed = [times(part, qkv_proj).astype(jnp.bfloat16) for part in rows]
    block_rows = segment.shape[0] // len(own_chunks)
    heads, logsums, middles = [], [], []
    for place, own in enumerate(own_chunks):
        own_heads, other_heads, logsum = attend_forward(
            mixed, segment, place, head_width, block_rows
        )
        heads += [own_heads, other_heads]
        logsums.append(logsum)
        chip_term = chip_sum(
            times_turned(own_heads, out_proj), times_turned(other_heads, out_proj)
        )
        middles.append(own + far_sum(chip_term))
    middles = hook("middle", middles)
    up_proj, down_proj = pieces[2:4]
    seconds, chip_terms, ups, activated, slopes = [], [], [], [], []
    for middle in middles:
        normal, inverse = normalize(middle)
        parts = shared([(normal * norm_values[2] + norm_values[3]).astype(jnp.bfloat16)])
        partials = []
        for part in parts:
            value, slope = gelu_and_slope(times(part, up_proj))
            value = value.astype(jnp.bfloat16)
            partials.append(times_turned(value, down_proj))
            activated.append(value)
            slopes.append(slope)
        ups += parts
        chip_terms.append(chip_sum(*partials))
        seconds.append((normal, inverse))
    return middles, chip_terms, (rows, mixed, heads, logsums, seconds, ups, activated, slopes)


def block_backward(
    own_grads, half_rows, saved, firsts, pieces, norm_values, segment, head_width, hook
):
    rows, mixed, heads, logsums, seconds, ups, activated, slopes = saved
    qkv_proj, out_proj, up_proj, down_proj = pieces
    down_group = (half_rows, activated)
    half_rows = hook("start", half_rows, down_group)
    hidden_rows = [
        (times(half, down_proj) * slope).astype(jnp.bfloat16)
        for half, slope in zip(half_rows, slopes)
    ]
    chip_terms = [
        chip_sum(times_turned(own, up_proj), times_turned(other, up_proj))
        for own, other in paired(hidden_rows)
    ]
    up_group = (ups, hidden_rows)
    normed_grads = hook("sums", [far_sum(chip_term) for chip_term in chip_terms], up_group)
    middle_grads, gain_two, shift_two = [], 0.0, 0.0
    for own_grad, chip_term, normed_grad, (normal, inverse) in zip(
        own_grads, chip_terms, normed_grads, seconds
    ):
        gain_two = gain_two + jnp.sum(chip_term * normal, axis=0)
        shift_two = shift_two + jnp.sum(chip_term, axis=0)
        middle_grads.append(
            own_grad + normalize_back(normal, inverse, norm_values[2], normed_grad)
        )
    middle_rows = shared([grad.astype(jnp.bfloat16) for grad in middle_grads])
    out_group = (middle_rows, heads)
    middle_rows = hook("middle", middle_rows, out_group)
    heads_grads = [times(part, out_proj).astype(jnp.bfloat16) for part in middle_rows]
    heads_grads = hook("heads", heads_grads, None)
    mixed_grads = attend_backward(heads_grads, mixed, logsums, segment, head_width)
    qkv_group = (rows, mixed_grads)
    mixed_grads = hook("mixed", mixed_grads, qkv_group)
    chip_terms = [
        chip_sum(times_turned(own, qkv_proj), times_turned(other, qkv_proj))
        for own, other in paired(mixed_grads)
    ]
    gain_one, shift_one = 0.0, 0.0
    for chip_term, (normal, _) in zip(chip_terms, firsts):
        gain_one = gain_one + jnp.sum(chip_term * normal, axis=0)
        shift_one = shift_one + jnp.sum(chip_term, axis=0)
    norm_grads = jnp.stack([gain_one, shift_one, gain_two, shift_two])
    groups = [qkv_group, out_group, up_group, down_group]
    return chip_terms, middle_grads, groups, norm_grads


def block_input_grads(far_sums, middle_grads, firsts, norm_values):
    return [
        middle_grad + normalize_back(normal, inverse, norm_values[0], normed_grad)
        for middle_grad, normed_grad, (normal, inverse) in zip(middle_grads, far_sums, firsts)
    ]


def row_pieces(refs, count):
    if len(refs) == count:
        return [ref[...] for ref in refs]
    rows = refs[0].shape[0] // count
    return [refs[0][k * rows : (k + 1) * rows, :] for k in range(count)]


def weight_grads_kernel(counts, parity_ref, *refs):
    sent_ref, kept_ref = refs[-2:]
    even = parity_ref[0] == 0
    place, column = 0, 0
    for left_count, right_count in counts:
        count = max(left_count, right_count)
        lefts = row_pieces(refs[place : place + left_count], count)
        place += left_count
        rights = row_pieces(refs[place : place + right_count], count)
        place += right_count
        total = 0.0
        for left, right in zip(lefts, rights):
            total = total + lax.dot_general(
                left, right, (((0,), (0,)), ((), ())), preferred_element_type=jnp.float32
            )
        half = total.shape[0] // 2
        columns = slice(column, column + total.shape[1])
        upper, lower = total[:half], total[half:]
        sent_ref[:, columns] = jnp.where(even, lower, upper).astype(jnp.bfloat16)
        kept_ref[:, columns] = jnp.where(even, upper, lower).astype(jnp.bfloat16)
        column += total.shape[1]


def weight_grads(groups, parity):
    width = groups[0][0][0].shape[1]
    specs, operands, flops = [], [], 0
    for lefts, rights in groups:
        for left in lefts:
            specs.append(
                pl.BlockSpec((left.shape[0], width // 4), lambda i: (0, i % 2 * 2 + i // 2))
            )
            operands.append(left)
        for right in rights:
            specs.append(pl.BlockSpec(right.shape, lambda i: (0, 0)))
            operands.append(right)
            flops += 2 * width * right.shape[0] * right.shape[1]
    columns = sum(rights[0].shape[1] for _, rights in groups)
    half = jax.ShapeDtypeStruct((width // 2, columns), jnp.bfloat16)
    return pl.pallas_call(
        functools.partial(
            weight_grads_kernel, [(len(lefts), len(rights)) for lefts, rights in groups]
        ),
        grid=(4,),
        in_specs=[pl.BlockSpec(memory_space=pltpu.SMEM)] + specs,
        out_specs=[pl.BlockSpec((width // 8, columns), lambda i: (i, 0))] * 2,
        out_shape=[half, half],
        compiler_params=pltpu.CompilerParams(
            dimension_semantics=("arbitrary",), vmem_limit_bytes=grads_vmem
        ),
        cost_estimate=pl.CostEstimate(
            flops=flops,
            bytes_accessed=2 * sum(operand.size for operand in operands) + 2 * width * columns,
            transcendentals=0,
        ),
        name="weight_grads",
    )(parity.reshape(1), *operands)


low_set = ((0, 0), (0, 1), (0, 2), (0, 3), (1, 1))
high_set = ((2, 2), (2, 3), (3, 3), (1, 2), (1, 3))


def newton_kernel(
    enc_rows, dec_rows, paired_ref, low_ref, high_ref, own_ref, out_ref, gram_ref, total_ref,
    mix_ref, gram_half_ref, total_half_ref,
):
    size = gram_ref.shape[0]
    block = size // 4
    tile = size // 2

    def in_upper(axis, count, start):
        shape = (count, 1) if axis == 0 else (1, count)
        place = start + lax.broadcasted_iota(jnp.int32, shape, axis)
        return place % enc_rows < dec_rows

    row = lax.broadcasted_iota(jnp.int32, (block, block), 0)
    column = lax.broadcasted_iota(jnp.int32, (block, block), 1)
    upper_trace, whole_trace = 0.0, 0.0
    for places, blocks_ref in ((low_set, low_ref), (high_set, high_ref)):
        for k, (i, j) in enumerate(places):
            value = blocks_ref[k * block : (k + 1) * block, :]
            gram_ref[i * block : (i + 1) * block, j * block : (j + 1) * block] = value
            if i != j:
                gram_ref[j * block : (j + 1) * block, i * block : (i + 1) * block] = value.T
            else:
                diagonal = jnp.where(row == column, value, 0.0)
                whole_trace += jnp.sum(diagonal)
                upper_trace += jnp.sum(
                    jnp.where(in_upper(0, block, i * block), diagonal, 0.0)
                )
    paired = paired_ref[0] == 1
    upper_scale = 1.0 / (jnp.sqrt(jnp.where(paired, upper_trace, whole_trace)) + 1e-07)
    lower_scale = 1.0 / (
        jnp.sqrt(jnp.where(paired, whole_trace - upper_trace, whole_trace)) + 1e-07
    )
    column_scale = jnp.where(in_upper(1, size, 0), upper_scale, lower_scale)

    def rows_of(step):
        return slice(step * tile, (step + 1) * tile)

    for step in range(size // tile):
        rows = rows_of(step)
        row_scale = jnp.where(in_upper(0, tile, step * tile), upper_scale, lower_scale)
        scaled = gram_ref[rows, :] * row_scale * column_scale
        gram_ref[rows, :] = scaled
        gram_half_ref[0, rows, :] = scaled.astype(jnp.bfloat16)

    for newton_step in range(NS_STEPS):
        now, later = newton_step % 2, (newton_step + 1) % 2

        for step in range(size // tile):
            rows = rows_of(step)
            square = times(gram_half_ref[now, rows, :], gram_half_ref[now])
            mix = newton_second * gram_ref[rows, :] + newton_third * square
            mix_ref[rows, :] = mix.astype(jnp.bfloat16)
            if newton_step == 0:
                same = lax.broadcasted_iota(
                    jnp.int32, (tile, size), 0
                ) + step * tile == lax.broadcasted_iota(jnp.int32, (tile, size), 1)
                total = jnp.where(same, newton_first, 0.0) + mix
                total_ref[rows, :] = total
                total_half_ref[later, rows, :] = total.astype(jnp.bfloat16)

        for step in range(size // tile):
            rows = rows_of(step)
            mix = mix_ref[rows, :]
            if newton_step > 0:
                total = newton_first * total_ref[rows, :] + times(mix, total_half_ref[now])
                if newton_step == NS_STEPS - 1:
                    out_ref[rows, :] = times(
                        (total * column_scale).astype(jnp.bfloat16), own_ref[...]
                    ).astype(jnp.bfloat16)
                else:
                    total_ref[rows, :] = total
                    total_half_ref[later, rows, :] = total.astype(jnp.bfloat16)
            if newton_step < NS_STEPS - 1:
                left = newton_first * gram_ref[rows, :] + times(mix, gram_half_ref[now])
                gram = newton_first * left + times(left.astype(jnp.bfloat16), mix_ref[...])
                gram_ref[rows, :] = gram
                gram_half_ref[later, rows, :] = gram.astype(jnp.bfloat16)


def newton(low_blocks, high_blocks, own, paired, enc_rows, dec_rows):
    size, width = own.shape
    whole = pl.BlockSpec(memory_space=pltpu.VMEM)
    return pl.pallas_call(
        functools.partial(newton_kernel, enc_rows, dec_rows),
        in_specs=[pl.BlockSpec(memory_space=pltpu.SMEM)] + [whole] * 3,
        out_specs=whole,
        out_shape=jax.ShapeDtypeStruct((size, width), jnp.bfloat16),
        scratch_shapes=[
            pltpu.VMEM((size, size), jnp.float32),
            pltpu.VMEM((size, size), jnp.float32),
            pltpu.VMEM((size, size), jnp.bfloat16),
            pltpu.VMEM((2, size, size), jnp.bfloat16),
            pltpu.VMEM((2, size, size), jnp.bfloat16),
        ],
        compiler_params=pltpu.CompilerParams(vmem_limit_bytes=newton_vmem),
        cost_estimate=pl.CostEstimate(
            flops=36 * size * size * size, bytes_accessed=20 * size * size, transcendentals=0
        ),
        name="newton",
    )(paired.astype(jnp.int32).reshape(1), low_blocks, high_blocks, own)


def gram_sum(gram):
    size = gram.shape[0] // 4

    def packed(places):
        return jnp.concatenate(
            [gram[i * size : (i + 1) * size, j * size : (j + 1) * size] for i, j in places],
            axis=0,
        )

    lower_core = lax.axis_index("mp") % 2 == 0
    low_blocks, high_blocks = packed(low_set), packed(high_set)
    own = jnp.where(lower_core, low_blocks, high_blocks)
    own = own + core_swap(jnp.where(lower_core, high_blocks, low_blocks))
    own = own + far_swap(own)
    other = core_swap(own)
    return jnp.where(lower_core, own, other), jnp.where(lower_core, other, own)


enc_slots = (2, 5, 3, 4, 6)
dec_slots = (0, 7)


def slot_rows(enc_rows_half, dec_rows_half, enc_widths, dec_widths, slot_width, data_ranks):
    enc_parts = split_columns(enc_rows_half, enc_widths)
    dec_parts = split_columns(dec_rows_half, dec_widths)
    half_width = slot_width // 2

    def widened(part, width):
        return jnp.pad(part, ((0, 0), (0, width - part.shape[1])))

    empty = jnp.zeros((enc_rows_half.shape[0], slot_width), enc_rows_half.dtype)
    slots = [empty] * data_ranks
    for part, slot in zip(enc_parts, enc_slots):
        slots[slot] = widened(part, slot_width)
    for place, slot in enumerate(dec_slots):
        upper = jnp.pad(widened(dec_parts[2 * place], half_width), ((0, 0), (0, half_width)))
        lower = jnp.pad(widened(dec_parts[2 * place + 1], half_width), ((0, 0), (half_width, 0)))
        slots[slot] = jnp.concatenate([upper, lower], axis=0)
    return jnp.stack(slots)


def unslot(rows_back, enc_widths, dec_widths, dec_rows):
    slot_width = rows_back.shape[2]
    enc_results = [rows_back[slot][:, :width] for slot, width in zip(enc_slots, enc_widths)]
    dec_results = []
    for place, width in enumerate(dec_widths):
        slot = rows_back[dec_slots[place // 2]]
        odd = place % 2
        dec_results.append(
            slot[
                odd * dec_rows : (odd + 1) * dec_rows,
                odd * (slot_width // 2) : odd * (slot_width // 2) + width,
            ]
        )
    return enc_results, dec_results


def apply_step(master, ortho_rows, widths, model_width, rate, model_ranks):
    steps_all = [
        orthogonal * (0.2 * math.sqrt(max(model_width, piece_width * model_ranks)))
        for orthogonal, piece_width in zip(ortho_rows, widths)
    ]
    return master * (1.0 - rate * decay_rate) - rate * jnp.concatenate(steps_all, axis=1)


def local(
    patches,
    cotangent,
    item_lengths,
    enc_master,
    dec_master,
    enc_norms,
    dec_norms,
    enc_moment,
    dec_moment,
    enc_norm_moment,
    dec_norm_moment,
):
    model_ranks = lax.axis_size("mp")
    data_ranks = lax.axis_size("dp")
    enc_widths = [
        3 * D // model_ranks,
        D // model_ranks,
        FF // model_ranks,
        FF // model_ranks,
        DD // model_ranks,
    ]
    dec_widths = [3 * DD // model_ranks, DD // model_ranks, DFF // model_ranks, DFF // model_ranks]
    first_cols = enc_widths[0] + enc_widths[1]
    norm_parts = gather_small(
        jnp.concatenate([enc_norms, dec_norms], axis=1).astype(jnp.bfloat16)
    ).astype(jnp.float32)
    enc_share, dec_share = enc_norms.shape[1], dec_norms.shape[1]
    enc_norm_values = jnp.moveaxis(norm_parts[:, :, :enc_share], 0, 1).reshape(4, D)
    dec_norm_values = jnp.moveaxis(norm_parts[:, :, enc_share:], 0, 1).reshape(4, DD)
    enc_half = enc_master.astype(jnp.bfloat16)
    first_gather = Gather(enc_half[:, :first_cols])
    rest_low = lax.all_gather(
        after(enc_half[:, first_cols:], first_gather.lined), "dp", axis=0, tiled=True
    )
    dec_low = lax.all_gather(
        after(dec_master.astype(jnp.bfloat16), first_gather.lined), "dp", axis=0, tiled=True
    )
    enc_pieces = split_columns(first_gather.result(), enc_widths[:2])
    dec_pieces = split_columns(dec_low, dec_widths)
    model_rank = lax.axis_index("mp")
    core = model_rank % 2
    upper_chip = model_rank // 2
    row_count = patches.shape[0]
    enc_rows = enc_master.shape[0]
    dec_rows = dec_master.shape[0]
    chunk_count = 2
    chunk_rows = row_count // chunk_count
    own_count = chunk_rows // 2
    segment, live_mask = segments_of(item_lengths[0], row_count)
    segment = swap_halves(segment, chunk_rows, core)
    live_mask = swap_halves(live_mask, chunk_rows, core)
    inputs = swap_halves(patches, chunk_rows, core)
    upstream = swap_halves(cotangent, chunk_rows, core) * live_mask.astype(jnp.bfloat16)[:, None]

    slot_width = max(enc_widths)

    def to_owners(enc_part, dec_part):
        slots = slot_rows(
            enc_part.astype(jnp.bfloat16),
            dec_part.astype(jnp.bfloat16),
            enc_widths,
            dec_widths,
            slot_width,
            data_ranks,
        )
        moved = lax.all_to_all(slots, "dp", 0, 0)
        return moved.reshape(-1, slot_width)

    input_normal, input_inverse = normalize(inputs.astype(jnp.float32))
    own_places = [slice(k * chunk_rows, k * chunk_rows + own_count) for k in range(chunk_count)]
    enc_firsts = [(input_normal[place], input_inverse[place]) for place in own_places]
    enc_rows_in = [
        (input_normal * enc_norm_values[0] + enc_norm_values[1]).astype(jnp.bfloat16)
    ]
    late_pieces = {}

    def enc_forward_hook(name, values):
        if name == "middle":
            enc_pieces.extend(split_columns(rest_low, enc_widths[2:]))
            late_pieces["bridge"] = whole_bridge(enc_pieces[4])
        return values

    def whole_bridge(bridge):
        bridge_far = far_swap(bridge)
        bridge_pair = jnp.where(
            upper_chip == 0, jnp.stack([bridge, bridge_far]), jnp.stack([bridge_far, bridge])
        )
        pair_other = core_swap(bridge_pair)
        bridge_all = jnp.stack(
            [
                jnp.where(core == 0, bridge_pair, pair_other),
                jnp.where(core == 0, pair_other, bridge_pair),
            ],
            axis=1,
        )
        share_width = bridge.shape[1]
        return jnp.moveaxis(bridge_all.reshape(-1, D, share_width), 0, 1).reshape(D, DD)

    enc_middles, enc_terms, enc_saved = block_forward(
        [inputs[place].astype(jnp.float32) for place in own_places],
        enc_rows_in,
        segment,
        enc_pieces,
        enc_norm_values,
        HD,
        enc_forward_hook,
    )
    bridge_all = late_pieces["bridge"]
    encoded_own = [
        (middle + far_sum(term)).astype(jnp.bfloat16)
        for middle, term in zip(enc_middles, enc_terms)
    ]
    decoder_in = [
        times(chunk, bridge_all).astype(jnp.bfloat16).astype(jnp.float32) for chunk in encoded_own
    ]
    encoded_rows = shared(encoded_own)
    dec_firsts = [normalize(chunk) for chunk in decoder_in]
    dec_rows_in = shared(
        [
            (normal * dec_norm_values[0] + dec_norm_values[1]).astype(jnp.bfloat16)
            for normal, _ in dec_firsts
        ]
    )
    dec_outs, dec_out_terms, dec_saved = block_forward(
        decoder_in,
        dec_rows_in,
        segment,
        dec_pieces,
        dec_norm_values,
        DHD,
        lambda name, values: values,
    )
    old_enc, old_dec, _ = lax.optimization_barrier((enc_moment, dec_moment, encoded_own[0]))
    old_slots = to_owners(old_enc, old_dec)
    upstream_rows = [
        upstream[k * own_count : (k + 1) * own_count] for k in range(2 * chunk_count)
    ]
    dec_terms, dec_middles, dec_groups, dec_norm_grads = block_backward(
        [half.astype(jnp.float32) for half in upstream_rows[::2]],
        upstream_rows,
        dec_saved,
        dec_firsts,
        dec_pieces,
        dec_norm_values,
        segment,
        DHD,
        lambda name, values, group: values,
    )
    dec_scatter = Scatter(dec_groups)
    dec_far_sums, dec_scatter.sent = lax.optimization_barrier(
        ([far_sum(term) for term in dec_terms], dec_scatter.sent)
    )
    dec_scatter.send()
    dec_in_grads = block_input_grads(dec_far_sums, dec_middles, dec_firsts, dec_norm_values)
    bridge_rows_in = shared([grad.astype(jnp.bfloat16) for grad in dec_in_grads])
    bridge_rows_in, old_slots = lax.optimization_barrier((bridge_rows_in, old_slots))
    encoded_grads = [times_turned(part, bridge_all) for part in bridge_rows_in]
    share_width = enc_widths[4]
    bridge_in_grad = [
        lax.dynamic_slice_in_dim(part, model_rank * share_width, share_width, 1)
        for part in bridge_rows_in
    ]
    scatters = {}

    def joined(values, *background):
        values, received = lax.optimization_barrier(
            (values, [scatter.received for scatter in background])
        )
        for scatter, piece in zip(background, received):
            scatter.received = piece
            scatter.fold()
        return values

    def enc_hook(name, values, group):
        if name == "start":
            scatters["down"] = Scatter([group, (encoded_rows, bridge_in_grad)])
            scatters["down"].send()
        if name == "sums":
            values = joined(values, dec_scatter)
            dec_scatter.send()
            scatters["up"] = Scatter([group])
            values, scatters["up"].sent = lax.optimization_barrier((values, scatters["up"].sent))
            scatters["up"].send()
        if name == "middle":
            scatters["out"] = group
        if name == "heads":
            values = joined(values, scatters["down"])
            scatters["down"].send()
        if name == "mixed":
            late = scatters["late"] = Scatter([group, scatters["out"]])
            late.send()
            values = after(values, late.sent)
            values = joined(values, scatters["down"], scatters["up"], dec_scatter)
            for scatter in (scatters["up"], scatters["down"], dec_scatter):
                scatter.send()
        return values

    enc_back_terms, enc_middle_grads, _, enc_norm_grads = block_backward(
        encoded_grads[::2],
        [grad.astype(jnp.bfloat16) for grad in encoded_grads],
        enc_saved,
        enc_firsts,
        enc_pieces[:4],
        enc_norm_values,
        segment,
        HD,
        enc_hook,
    )
    late, up, down = (scatters[name] for name in ("late", "up", "down"))
    norm_hops = HopSum(jnp.concatenate([enc_norm_grads, dec_norm_grads], axis=1))
    norm_hops.step(2)
    enc_back_terms, norm_hops.value, down.received, dec_scatter.received = joined(
        (enc_back_terms, norm_hops.value, down.received, dec_scatter.received), late, up
    )
    late.send()
    up.send()
    norm_hops.step(1)
    enc_far_sums = [far_sum(term) for term in enc_back_terms]
    dec_sum_rows = dec_scatter.result()
    down_rows, bridge_rows = split_columns(down.result(), enc_widths[3:])
    half_width = slot_width // 2
    half_rows = [
        jnp.pad(part, ((0, 0), (0, half_width - part.shape[1])))
        for part in split_columns(dec_sum_rows, dec_widths)
    ]
    narrow_rows = [
        jnp.concatenate(half_rows[:2], axis=0),
        jnp.concatenate(half_rows[2:], axis=0),
        bridge_rows,
    ]
    narrow_all = lax.all_gather(
        jnp.concatenate(narrow_rows, axis=1).astype(jnp.bfloat16), "dp", axis=0, tiled=True
    )
    norm_hops.value, up.received = joined((norm_hops.value, up.received), late)
    up_rows = up.result()
    up_half, down_half = up_rows.astype(jnp.bfloat16), down_rows.astype(jnp.bfloat16)
    late.sent, up_half, down_half = lax.optimization_barrier((late.sent, up_half, down_half))
    late.send()
    wide_crossed = cross_pair(down_half, up_half)
    norm_hops.step(1)
    late.received, wide_crossed, norm_hops.value, enc_far_sums = lax.optimization_barrier(
        (late.received, wide_crossed, norm_hops.value, enc_far_sums)
    )
    qkv_rows, out_rows = split_columns(late.result(), enc_widths[:2])
    out_padded = jnp.pad(out_rows, ((0, 0), (0, enc_widths[0] - enc_widths[1])))
    tail_crossed = cross_pair(qkv_rows.astype(jnp.bfloat16), out_padded.astype(jnp.bfloat16))
    wide_parts = line_pair(*wide_crossed, enc_slots[2:4])
    norm_sums = norm_hops.finish()
    data_rank = lax.axis_index("dp")
    enc_sum_rows = jnp.concatenate([qkv_rows, out_rows, up_rows, down_rows, bridge_rows], axis=1)
    local_sum = jnp.sum(enc_sum_rows * enc_sum_rows) + jnp.sum(dec_sum_rows * dec_sum_rows)
    square_hops = HopSum(jnp.full((8, 128), local_sum))
    squares = square_hops.finish()[0, 0]
    tail_crossed, squares, norm_sums = lax.optimization_barrier((tail_crossed, squares, norm_sums))
    squares = squares + jnp.sum(norm_sums * norm_sums)
    tail_parts = line_pair(*tail_crossed, enc_slots[:2])

    def owned(parts, place):
        whole = assemble(parts, place)
        return jnp.pad(whole, ((0, 0), (0, slot_width - whole.shape[1])))

    late_slots = owned(tail_parts, data_rank // 2)
    wide_slots = owned(wide_parts, data_rank // 2)
    dec_parts = [narrow_all[:, k * half_width : (k + 1) * half_width] for k in range(2)]
    bridge_part = jnp.pad(
        narrow_all[:, slot_width:], ((0, 0), (0, half_width - enc_widths[4]))
    )
    narrow_slots = jnp.where(
        data_rank == dec_slots[0],
        dec_parts[0],
        jnp.where(data_rank == dec_slots[1], dec_parts[1], bridge_part),
    )
    narrow_slots = jnp.pad(narrow_slots, ((0, 0), (0, slot_width - half_width)))
    enc_norm_rows = lax.dynamic_slice_in_dim(norm_sums[:, :D], data_rank * enc_share, enc_share, 1)
    dec_norm_rows = lax.dynamic_slice_in_dim(norm_sums[:, D:], data_rank * dec_share, dec_share, 1)
    input_grads = block_input_grads(
        enc_far_sums, enc_middle_grads, enc_firsts, enc_norm_values
    )

    def natural(own_chunks):
        return swap_halves(jnp.concatenate(shared(own_chunks), axis=0), chunk_rows, core)

    dec_out_terms, _ = lax.optimization_barrier((dec_out_terms, late.received))
    decoded = [middle + far_sum(term) for middle, term in zip(dec_outs, dec_out_terms)]
    decoded = natural(decoded)
    input_grad = natural(input_grads)
    data_rank = lax.axis_index("dp")

    def is_rank(*slots):
        return functools.reduce(jnp.logical_or, [data_rank == slot for slot in slots])

    lower_row = (jnp.arange(wide_slots.shape[0], dtype=jnp.int32) % enc_rows >= dec_rows)[:, None]
    shifted = jnp.where(
        jnp.logical_and(lower_row, is_rank(*dec_slots)),
        jnp.roll(narrow_slots, half_width, axis=1),
        narrow_slots,
    )
    grad_slots = jnp.where(
        is_rank(*enc_slots[2:4]),
        wide_slots,
        jnp.where(is_rank(*enc_slots[:2]), late_slots, shifted),
    )
    grad_norm = jnp.sqrt(squares)
    factor = clip_bound * lax.rsqrt(squares + 1e-06)
    enc_grad = enc_sum_rows * factor
    dec_grad = dec_sum_rows * factor
    enc_norm_grad = enc_norm_rows * factor
    dec_norm_grad = dec_norm_rows * factor
    dec_shift_grad = dec_norm_grad[3]
    enc_moment_new = momentum_keep * enc_moment + enc_grad
    dec_moment_new = momentum_keep * dec_moment + dec_grad
    enc_norm_moment_new = momentum_keep * enc_norm_moment + enc_norm_grad
    dec_norm_moment_new = momentum_keep * dec_norm_moment + dec_norm_grad
    own = (
        momentum_keep * old_slots.astype(jnp.float32)
        + factor * grad_slots.astype(jnp.float32)
    ).astype(jnp.bfloat16)
    low_blocks, high_blocks = gram_sum(
        lax.dot_general(own, own, (((1,), (1,)), ((), ())), preferred_element_type=jnp.float32)
    )
    orthogonal = newton(low_blocks, high_blocks, own, is_rank(*dec_slots), enc_rows, dec_rows)
    rows_back = lax.all_to_all(
        orthogonal.reshape(data_ranks, enc_rows, slot_width), "dp", 0, 0
    ).astype(jnp.float32)
    enc_results, dec_results = unslot(rows_back, enc_widths, dec_widths, dec_rows)
    enc_master_new = apply_step(enc_master, enc_results, enc_widths, D, rate_enc, model_ranks)
    dec_master_new = apply_step(dec_master, dec_results, dec_widths, DD, rate_dec, model_ranks)
    enc_norms_new = enc_norms - rate_norm * enc_norm_moment_new
    dec_norms_new = dec_norms - rate_norm * dec_norm_moment_new
    return (
        decoded,
        input_grad,
        enc_grad,
        dec_grad,
        enc_norm_grad,
        dec_norm_grad,
        dec_shift_grad,
        enc_moment_new,
        dec_moment_new,
        enc_norm_moment_new,
        dec_norm_moment_new,
        enc_master_new,
        dec_master_new,
        enc_norms_new,
        dec_norms_new,
        enc_master_new.astype(jnp.bfloat16),
        dec_master_new.astype(jnp.bfloat16),
        enc_norms_new.astype(jnp.bfloat16),
        dec_norms_new.astype(jnp.bfloat16),
        grad_norm,
    )


def solution(mesh):
    return jax.shard_map(
        local,
        mesh=mesh,
        in_specs=(
            P("dp", None),
            P("dp", None),
            P("dp", None),
            P("dp", "mp"),
            P("dp", "mp"),
            P(None, "dp"),
            P(None, "dp"),
            P("dp", "mp"),
            P("dp", "mp"),
            P(None, "dp"),
            P(None, "dp"),
        ),
        out_specs=(
            P("dp", None),
            P("dp", None),
            P("dp", "mp"),
            P("dp", "mp"),
            P(None, "dp"),
            P(None, "dp"),
            P("dp"),
            P("dp", "mp"),
            P("dp", "mp"),
            P(None, "dp"),
            P(None, "dp"),
            P("dp", "mp"),
            P("dp", "mp"),
            P(None, "dp"),
            P(None, "dp"),
            P("dp", "mp"),
            P("dp", "mp"),
            P(None, "dp"),
            P(None, "dp"),
            P(),
        ),
        check_vma=False,
    )
```

```python
import functools
import math

import jax
import jax.numpy as jnp
from jax import lax
from jax.experimental import pallas as pl
from jax.experimental.pallas import tpu as pltpu
from jax.sharding import PartitionSpec as P

D = 1024
HD = 64
FF = 4096
DD = 512
DHD = 32
DFF = 2048
NS_STEPS = 5


highest = lax.Precision.HIGHEST
ln_eps = 1e-06
masked_score = -1e30
newton_first = 3.4445
newton_second = -4.775
newton_third = 2.0315
momentum_keep = 0.5
clip_bound = 100.0
rate_enc = 0.2
rate_dec = 0.3
rate_norm = 1.0
decay_rate = 0.01
kernel_vmem = 32 * 1024 * 1024
newton_vmem = 48 * 1024 * 1024
grads_vmem = 58 * 1024 * 1024


def shortened(array):

    def short(part):
        return part.astype(jnp.bfloat16) if part.dtype == jnp.float32 else part

    return jax.tree.map(short, array)


def pair_swap(array, axis, bit):
    size = lax.axis_size(axis)
    return lax.ppermute(array, axis, [(rank, rank ^ bit) for rank in range(size)])


def core_swap(array):
    return pair_swap(array, "mp", 1)


def far_swap(array):
    return pair_swap(array, "mp", 2)


def far_sum(chip_term):
    half = chip_term.astype(jnp.bfloat16)
    return half.astype(jnp.float32) + far_swap(half).astype(jnp.float32)


def chip_sum(own_term, other_term):
    return own_term + core_swap(other_term.astype(jnp.bfloat16)).astype(jnp.float32)


def shared(own_parts):
    return [part for own in own_parts for part in (own, core_swap(own))]


def paired(parts):
    return list(zip(parts[::2], parts[1::2]))


def times(left, right):
    return jnp.dot(left, right, preferred_element_type=jnp.float32)


def times_turned(left, right):
    return jnp.einsum("tf,df->td", left, right, preferred_element_type=jnp.float32)


def gather_small(array):
    rank = lax.axis_index("dp")
    gathered = array[None]
    bit = 1
    while bit < lax.axis_size("dp"):
        other = pair_swap(gathered, "dp", bit)
        lower = (rank & bit) == 0
        gathered = jnp.concatenate(
            [jnp.where(lower, gathered, other), jnp.where(lower, other, gathered)], axis=0
        )
        bit *= 2
    return gathered


def assemble_kernel(rank_ref, *refs):
    whole_ref = refs[-1]
    rows = refs[0].shape[0]
    for bit, part_ref in enumerate(refs[:-1]):
        place = pl.multiple_of((rank_ref[0] ^ bit) * rows, rows)
        whole_ref[pl.ds(place, rows), :] = part_ref[...]


def assemble(parts, place):
    rows, columns = parts[0].shape
    spec = pl.BlockSpec(memory_space=pltpu.VMEM)
    return pl.pallas_call(
        assemble_kernel,
        in_specs=[pl.BlockSpec(memory_space=pltpu.SMEM)] + [spec] * len(parts),
        out_specs=spec,
        out_shape=jax.ShapeDtypeStruct((len(parts) * rows, columns), parts[0].dtype),
        compiler_params=pltpu.CompilerParams(vmem_limit_bytes=grads_vmem),
        cost_estimate=pl.CostEstimate(
            flops=0, bytes_accessed=4 * len(parts) * rows * columns, transcendentals=0
        ),
        name="assemble",
    )(place.reshape(1), *parts)


class Gather:
    def __init__(self, array):
        self.general = lax.axis_size("dp") != 8
        if self.general:
            self.whole = lax.all_gather(array, "dp", axis=0, tiled=True)
            self.lined = [array]
        else:
            self.lined = [array] + [pair_swap(array, "dp", 2 * bit) for bit in (1, 2, 3)]
            self.crossed = None

    def turn(self, values):
        if self.general:
            return values
        values, self.lined = lax.optimization_barrier((values, self.lined))
        self.cross()
        return values

    def cross(self):
        self.crossed = [pair_swap(part, "dp", 1) for part in self.lined]

    def result(self):
        if self.general:
            return self.whole
        if self.crossed is None:
            self.cross()
        parts = [part for pair in zip(self.lined, self.crossed) for part in pair]
        return assemble(parts, lax.axis_index("dp"))


def collect_values(slots):
    ranks = lax.axis_size("dp")
    rank = lax.axis_index("dp")
    width = max(rows.shape[1] for rows in slots.values())
    padded = {
        owner: jnp.pad(rows.astype(jnp.bfloat16), ((0, 0), (0, width - rows.shape[1])))
        for owner, rows in slots.items()
    }
    values = []
    for bit in range(ranks):
        value = None
        for owner, rows in padded.items():
            value = rows if value is None else jnp.where(rank ^ bit == owner, rows, value)
        values.append(value)
    return values


def collect_parts(values, owners):
    return values[:1] + [
        lax.ppermute(value, "dp", [(owner ^ bit, owner) for owner in owners])
        for bit, value in enumerate(values)
        if bit
    ]


def cross_pair(even_rows, odd_rows):
    even = lax.axis_index("dp") % 2 == 0
    kept = jnp.where(even, even_rows, odd_rows)
    return kept, pair_swap(jnp.where(even, odd_rows, even_rows), "dp", 1)


def line_pair(kept, crossed, owners):
    even = lax.axis_index("dp") % 2 == 0
    lined = jnp.concatenate(
        [jnp.where(even, kept, crossed), jnp.where(even, crossed, kept)], axis=0
    )
    return [lined] + [
        lax.ppermute(lined, "dp", [(owner ^ (2 * bit), owner) for owner in owners])
        for bit in range(1, lax.axis_size("dp") // 2)
    ]


def after(value, anchor):
    return lax.optimization_barrier((value, anchor))[0]


def fold(kept, received):
    return (kept.astype(jnp.float32) + received.astype(jnp.float32)).astype(jnp.bfloat16)


def split_rows(array, place):
    half = array.shape[0] // 2
    return (
        lax.dynamic_slice_in_dim(array, (1 - place) * half, half, 0),
        lax.dynamic_slice_in_dim(array, place * half, half, 0),
    )


class Scatter:
    def __init__(self, groups):
        self.phase = 0
        self.general = lax.axis_size("dp") != 8
        self.rank = lax.axis_index("dp")
        self.sent = self.kept = self.received = None
        if self.general:
            whole = jnp.concatenate(
                [
                    jnp.einsum(
                        "td,tf->df",
                        jnp.concatenate(lefts, axis=0),
                        jnp.concatenate(rights, axis=0),
                        preferred_element_type=jnp.float32,
                    ).astype(jnp.bfloat16)
                    for lefts, rights in groups
                ],
                axis=1,
            )
            self.total = lax.psum_scatter(whole, "dp", scatter_dimension=0, tiled=True)
        else:
            self.sent, self.kept = weight_grads(groups, self.rank % 2)

    def send(self):
        if not self.general:
            self.received = pair_swap(self.sent, "dp", 1 << self.phase)

    def fold(self):
        if not self.general:
            place = self.rank // 2 % 2 if self.phase == 0 else self.rank // 4
            self.sent, self.kept = split_rows(fold(self.kept, self.received), place)
            self.phase += 1

    def result(self):
        if self.general:
            return self.total.astype(jnp.float32)
        return self.kept.astype(jnp.float32) + self.received.astype(jnp.float32)


class HopSum:
    def __init__(self, value):
        self.value = value
        self.hops = [
            (axis, 1 << bit)
            for axis in ("mp", "dp")
            for bit in range(lax.axis_size(axis).bit_length() - 1)
        ]

    def step(self, count):
        for axis, bit in self.hops[:count]:
            self.value = self.value + pair_swap(self.value, axis, bit)
        self.hops = self.hops[count:]

    def finish(self):
        self.step(len(self.hops))
        return self.value


def normalize(values):
    center = values - jnp.mean(values, axis=-1, keepdims=True)
    inverse = lax.rsqrt(jnp.mean(center * center, axis=-1, keepdims=True) + ln_eps)
    return center * inverse, inverse


def normalize_back(normal, inverse, gain_row, out_grad):
    scaled = out_grad * gain_row
    mean_grad = jnp.mean(scaled, axis=-1, keepdims=True)
    mean_dot = jnp.mean(scaled * normal, axis=-1, keepdims=True)
    return inverse * (scaled - mean_grad - normal * mean_dot)


def gelu_and_slope(hidden):
    spread = 0.5 + 0.5 * lax.erf(hidden * math.sqrt(0.5))
    density = jnp.exp(-0.5 * hidden * hidden) * (1.0 / math.sqrt(2.0 * math.pi))
    return hidden * spread, spread + hidden * density


def swap_halves(array, chunk_rows, core):
    parts = array.reshape((-1, 2, chunk_rows // 2) + array.shape[1:])
    return jnp.where(core == 0, parts, parts[:, ::-1]).reshape(array.shape)


def segments_of(lengths, row_count):
    item_ends = jnp.cumsum(lengths)
    position = jnp.arange(row_count, dtype=jnp.int32)
    segment = jnp.sum((position[:, None] >= item_ends[None, :]).astype(jnp.int32), axis=1)
    live_mask = (position < item_ends[-1]).astype(jnp.float32)
    return (segment, live_mask)


def split_columns(whole_cols, widths):
    pieces = []
    start_col = 0
    for piece_width in widths:
        pieces.append(whole_cols[:, start_col : start_col + piece_width])
        start_col += piece_width
    return pieces


def head_mask(head, head_width, inner_width):
    lane = lax.broadcasted_iota(jnp.int32, (1, inner_width), 1)
    inside = jnp.logical_and(lane >= head * head_width, lane < (head + 1) * head_width)
    return jnp.where(inside, 1.0, 0.0)


def masked_rows(rows, head, head_width):
    mask = head_mask(head, head_width, rows.shape[1])
    return (rows.astype(jnp.float32) * mask).astype(jnp.bfloat16)


def last_dims(left, right):
    return lax.dot_general(
        left, right, (((1,), (1,)), ((), ())), preferred_element_type=jnp.float32
    )


def segment_bias(key_segment_ref, query_segment_ref):
    return jnp.where(key_segment_ref[...] == query_segment_ref[...], 0.0, masked_score)


def joined_columns(refs, first, last):
    return jnp.concatenate([ref[:, first:last] for ref in refs], axis=0)


def attend_forward_kernel(
    head_width, place, count, key_segment_ref, query_segment_ref, *refs
):
    mixed_refs, (own_ref, other_ref, logsum_ref) = refs[:count], refs[count:]
    block_rows = query_segment_ref.shape[0]
    half_rows, inner_width = own_ref.shape
    score_scale = head_width ** (-0.5)
    bias = segment_bias(key_segment_ref, query_segment_ref)
    if count == 1:
        rows = mixed_refs[0][place * block_rows : (place + 1) * block_rows, :inner_width]
    else:
        rows = joined_columns(mixed_refs[2 * place : 2 * place + 2], 0, inner_width)
    keys = joined_columns(mixed_refs, inner_width, 2 * inner_width)
    values = joined_columns(mixed_refs, 2 * inner_width, 3 * inner_width)
    total_out = jnp.zeros((block_rows, inner_width), jnp.float32)
    logsums = []
    for head in range(inner_width // head_width):
        scores = last_dims(masked_rows(rows, head, head_width), keys) * score_scale + bias
        top = jnp.max(scores, axis=1, keepdims=True)
        shifted = jnp.exp(scores - top)
        total = jnp.sum(shifted, axis=1, keepdims=True)
        part = times(shifted.astype(jnp.bfloat16), values)
        total_out += part * (head_mask(head, head_width, inner_width) / total)
        logsums.append(jnp.broadcast_to(top + jnp.log(total), (block_rows, 128)))
    own_ref[...] = total_out[:half_rows].astype(jnp.bfloat16)
    other_ref[...] = total_out[half_rows:].astype(jnp.bfloat16)
    lane = lax.broadcasted_iota(jnp.int32, (block_rows, 128), 1)
    stacked = logsums[0]
    for head in range(1, len(logsums)):
        stacked = jnp.where(lane == head, logsums[head], stacked)
    logsum_ref[...] = stacked.T[: len(logsums), :]


def attend_forward(mixed, segment, place, head_width, block_rows):
    row_count = segment.shape[0]
    inner_width = mixed[0].shape[1] // 3
    head_count = inner_width // head_width
    whole = pl.BlockSpec(memory_space=pltpu.VMEM)
    half = jax.ShapeDtypeStruct((block_rows // 2, inner_width), jnp.bfloat16)
    return pl.pallas_call(
        functools.partial(attend_forward_kernel, head_width, place, len(mixed)),
        in_specs=[whole] * (2 + len(mixed)),
        out_specs=[whole] * 3,
        out_shape=[half, half, jax.ShapeDtypeStruct((head_count, block_rows), jnp.float32)],
        compiler_params=pltpu.CompilerParams(vmem_limit_bytes=kernel_vmem),
        cost_estimate=pl.CostEstimate(
            flops=4 * block_rows * row_count * inner_width * head_count,
            bytes_accessed=8 * row_count * inner_width,
            transcendentals=block_rows * row_count * head_count,
        ),
        name="attend_forward",
    )(
        segment.reshape(1, row_count),
        segment[place * block_rows : (place + 1) * block_rows].reshape(block_rows, 1),
        *mixed,
    )


def attend_backward_kernel(head_width, count, key_segment_ref, query_segment_ref, *refs):
    grad_refs, logsum_refs, refs = refs[:4], refs[4:6], refs[6:]
    mixed_refs, out_refs, refs = refs[:count], refs[count : count + 4], refs[count + 4 :]
    turned_ref, grad_ref, query_ref, bias_ref, query_grad_ref, key_total_ref, value_total_ref = refs
    row_count, inner_width = grad_ref.shape
    part_rows = row_count // 4
    block_rows = row_count // 2
    score_scale = head_width ** (-0.5)
    keys = joined_columns(mixed_refs, inner_width, 2 * inner_width)
    values = joined_columns(mixed_refs, 2 * inner_width, 3 * inner_width)
    turned_ref[...] = keys.astype(jnp.float32).T.astype(jnp.bfloat16)
    for k in range(4):
        grad_ref[k * part_rows : (k + 1) * part_rows, :] = grad_refs[k][...]
    query_ref[...] = joined_columns(mixed_refs, 0, inner_width)
    key_total_ref[...] = jnp.zeros_like(key_total_ref)
    value_total_ref[...] = jnp.zeros_like(value_total_ref)
    for block in range(2):
        bias_ref[block] = jnp.where(
            key_segment_ref[...]
            == query_segment_ref[:, block * block_rows : (block + 1) * block_rows],
            0.0,
            masked_score,
        )

    @pl.loop(0, 2)
    def _(block):
        rows = pl.ds(pl.multiple_of(block * block_rows, block_rows), block_rows)
        parts = []
        for head in range(inner_width // head_width):
            query = masked_rows(query_ref[rows, :], head, head_width)
            grad = masked_rows(grad_ref[rows, :], head, head_width)
            logsum = jnp.where(
                block == 0,
                logsum_refs[0][head : head + 1, :],
                logsum_refs[1][head : head + 1, :],
            )
            scores = last_dims(keys, query) * score_scale + bias_ref[block]
            attention = jnp.exp(scores - logsum)
            weighted = attention * last_dims(values, grad)
            row_dot = jnp.sum(weighted, axis=0, keepdims=True)
            score_grad = (weighted - attention * row_dot).astype(jnp.bfloat16)
            value_total_ref[...] += times(attention.astype(jnp.bfloat16), grad)
            key_total_ref[...] += times(score_grad, query)
            parts.append(
                times(turned_ref[head * head_width : (head + 1) * head_width, :], score_grad)
            )
        query_grad_ref[rows, :] = (jnp.concatenate(parts, axis=0) * score_scale).T

    for k, out_ref in enumerate(out_refs):
        rows = slice(k * part_rows, (k + 1) * part_rows)
        out_ref[:, :inner_width] = query_grad_ref[rows, :].astype(jnp.bfloat16)
        out_ref[:, inner_width : 2 * inner_width] = (key_total_ref[rows, :] * score_scale).astype(
            jnp.bfloat16
        )
        out_ref[:, 2 * inner_width :] = value_total_ref[rows, :].astype(jnp.bfloat16)


def attend_backward(heads_grads, mixed, logsums, segment, head_width):
    row_count = segment.shape[0]
    part_rows, inner_width = heads_grads[0].shape
    head_count = inner_width // head_width
    whole = pl.BlockSpec(memory_space=pltpu.VMEM)
    part = jax.ShapeDtypeStruct((part_rows, 3 * inner_width), jnp.bfloat16)
    return pl.pallas_call(
        functools.partial(attend_backward_kernel, head_width, len(mixed)),
        in_specs=[whole] * (8 + len(mixed)),
        out_specs=[whole] * 4,
        out_shape=[part] * 4,
        scratch_shapes=[
            pltpu.VMEM((inner_width, row_count), jnp.bfloat16),
            pltpu.VMEM((row_count, inner_width), jnp.bfloat16),
            pltpu.VMEM((row_count, inner_width), jnp.bfloat16),
            pltpu.VMEM((2, row_count, row_count // 2), jnp.float32),
            pltpu.VMEM((row_count, inner_width), jnp.float32),
            pltpu.VMEM((row_count, inner_width), jnp.float32),
            pltpu.VMEM((row_count, inner_width), jnp.float32),
        ],
        compiler_params=pltpu.CompilerParams(vmem_limit_bytes=kernel_vmem),
        cost_estimate=pl.CostEstimate(
            flops=10 * row_count * row_count * inner_width * head_count,
            bytes_accessed=14 * row_count * inner_width,
            transcendentals=row_count * row_count * head_count,
        ),
        name="attend_backward",
    )(
        segment.reshape(row_count, 1),
        segment.reshape(1, row_count),
        *heads_grads,
        *logsums,
        *mixed,
    )


def block_forward(own_chunks, rows, segment, pieces, norm_values, head_width, hook):
    qkv_proj, out_proj = pieces[:2]
    mixed = [times(part, qkv_proj).astype(jnp.bfloat16) for part in rows]
    block_rows = segment.shape[0] // len(own_chunks)
    heads, logsums, middles = [], [], []
    for place, own in enumerate(own_chunks):
        own_heads, other_heads, logsum = attend_forward(
            mixed, segment, place, head_width, block_rows
        )
        heads += [own_heads, other_heads]
        logsums.append(logsum)
        chip_term = chip_sum(
            times_turned(own_heads, out_proj), times_turned(other_heads, out_proj)
        )
        middles.append(own + far_sum(chip_term))
    middles = hook("middle", middles)
    up_proj, down_proj = pieces[2:4]
    seconds, chip_terms, ups, activated, slopes = [], [], [], [], []
    for middle in middles:
        normal, inverse = normalize(middle)
        parts = shared([(normal * norm_values[2] + norm_values[3]).astype(jnp.bfloat16)])
        partials = []
        for part in parts:
            value, slope = gelu_and_slope(times(part, up_proj))
            value = value.astype(jnp.bfloat16)
            partials.append(times_turned(value, down_proj))
            activated.append(value)
            slopes.append(slope)
        ups += parts
        chip_terms.append(chip_sum(*partials))
        seconds.append((normal, inverse))
    return middles, chip_terms, (rows, mixed, heads, logsums, seconds, ups, activated, slopes)


def block_backward(
    own_grads, half_rows, saved, firsts, pieces, norm_values, segment, head_width, hook
):
    rows, mixed, heads, logsums, seconds, ups, activated, slopes = saved
    qkv_proj, out_proj, up_proj, down_proj = pieces
    down_group = (half_rows, activated)
    half_rows = hook("start", half_rows, down_group)
    hidden_rows = [
        (times(half, down_proj) * slope).astype(jnp.bfloat16)
        for half, slope in zip(half_rows, slopes)
    ]
    chip_terms = [
        chip_sum(times_turned(own, up_proj), times_turned(other, up_proj))
        for own, other in paired(hidden_rows)
    ]
    up_group = (ups, hidden_rows)
    normed_grads = hook("sums", [far_sum(chip_term) for chip_term in chip_terms], up_group)
    middle_grads, gain_two, shift_two = [], 0.0, 0.0
    for own_grad, chip_term, normed_grad, (normal, inverse) in zip(
        own_grads, chip_terms, normed_grads, seconds
    ):
        gain_two = gain_two + jnp.sum(chip_term * normal, axis=0)
        shift_two = shift_two + jnp.sum(chip_term, axis=0)
        middle_grads.append(
            own_grad + normalize_back(normal, inverse, norm_values[2], normed_grad)
        )
    middle_rows = shared([grad.astype(jnp.bfloat16) for grad in middle_grads])
    out_group = (middle_rows, heads)
    middle_rows = hook("middle", middle_rows, out_group)
    heads_grads = [times(part, out_proj).astype(jnp.bfloat16) for part in middle_rows]
    heads_grads = hook("heads", heads_grads, None)
    mixed_grads = attend_backward(heads_grads, mixed, logsums, segment, head_width)
    qkv_group = (rows, mixed_grads)
    mixed_grads = hook("mixed", mixed_grads, qkv_group)
    chip_terms = [
        chip_sum(times_turned(own, qkv_proj), times_turned(other, qkv_proj))
        for own, other in paired(mixed_grads)
    ]
    gain_one, shift_one = 0.0, 0.0
    for chip_term, (normal, _) in zip(chip_terms, firsts):
        gain_one = gain_one + jnp.sum(chip_term * normal, axis=0)
        shift_one = shift_one + jnp.sum(chip_term, axis=0)
    norm_grads = jnp.stack([gain_one, shift_one, gain_two, shift_two])
    groups = [qkv_group, out_group, up_group, down_group]
    return chip_terms, middle_grads, groups, norm_grads


def block_input_grads(far_sums, middle_grads, firsts, norm_values):
    return [
        middle_grad + normalize_back(normal, inverse, norm_values[0], normed_grad)
        for middle_grad, normed_grad, (normal, inverse) in zip(middle_grads, far_sums, firsts)
    ]


def row_pieces(refs, count):
    if len(refs) == count:
        return [ref[...] for ref in refs]
    rows = refs[0].shape[0] // count
    return [refs[0][k * rows : (k + 1) * rows, :] for k in range(count)]


def weight_grads_kernel(counts, parity_ref, *refs):
    sent_ref, kept_ref = refs[-2:]
    even = parity_ref[0] == 0
    place, column = 0, 0
    for left_count, right_count in counts:
        count = max(left_count, right_count)
        lefts = row_pieces(refs[place : place + left_count], count)
        place += left_count
        rights = row_pieces(refs[place : place + right_count], count)
        place += right_count
        total = 0.0
        for left, right in zip(lefts, rights):
            total = total + lax.dot_general(
                left, right, (((0,), (0,)), ((), ())), preferred_element_type=jnp.float32
            )
        half = total.shape[0] // 2
        columns = slice(column, column + total.shape[1])
        upper, lower = total[:half], total[half:]
        sent_ref[:, columns] = jnp.where(even, lower, upper).astype(jnp.bfloat16)
        kept_ref[:, columns] = jnp.where(even, upper, lower).astype(jnp.bfloat16)
        column += total.shape[1]


def weight_grads(groups, parity):
    width = groups[0][0][0].shape[1]
    specs, operands, flops = [], [], 0
    for lefts, rights in groups:
        for left in lefts:
            specs.append(
                pl.BlockSpec((left.shape[0], width // 4), lambda i: (0, i % 2 * 2 + i // 2))
            )
            operands.append(left)
        for right in rights:
            specs.append(pl.BlockSpec(right.shape, lambda i: (0, 0)))
            operands.append(right)
            flops += 2 * width * right.shape[0] * right.shape[1]
    columns = sum(rights[0].shape[1] for _, rights in groups)
    half = jax.ShapeDtypeStruct((width // 2, columns), jnp.bfloat16)
    return pl.pallas_call(
        functools.partial(
            weight_grads_kernel, [(len(lefts), len(rights)) for lefts, rights in groups]
        ),
        grid=(4,),
        in_specs=[pl.BlockSpec(memory_space=pltpu.SMEM)] + specs,
        out_specs=[pl.BlockSpec((width // 8, columns), lambda i: (i, 0))] * 2,
        out_shape=[half, half],
        compiler_params=pltpu.CompilerParams(
            dimension_semantics=("arbitrary",), vmem_limit_bytes=grads_vmem
        ),
        cost_estimate=pl.CostEstimate(
            flops=flops,
            bytes_accessed=2 * sum(operand.size for operand in operands) + 2 * width * columns,
            transcendentals=0,
        ),
        name="weight_grads",
    )(parity.reshape(1), *operands)


low_set = ((0, 0), (0, 1), (0, 2), (0, 3), (1, 1))
high_set = ((2, 2), (2, 3), (3, 3), (1, 2), (1, 3))


def newton_kernel(
    enc_rows, dec_rows, paired_ref, low_ref, high_ref, own_ref, out_ref, gram_ref, total_ref,
    mix_ref, gram_half_ref, total_half_ref,
):
    size = gram_ref.shape[0]
    block = size // 4
    tile = size // 2

    def in_upper(axis, count, start):
        shape = (count, 1) if axis == 0 else (1, count)
        place = start + lax.broadcasted_iota(jnp.int32, shape, axis)
        return place % enc_rows < dec_rows

    row = lax.broadcasted_iota(jnp.int32, (block, block), 0)
    column = lax.broadcasted_iota(jnp.int32, (block, block), 1)
    upper_trace, whole_trace = 0.0, 0.0
    for places, blocks_ref in ((low_set, low_ref), (high_set, high_ref)):
        for k, (i, j) in enumerate(places):
            value = blocks_ref[k * block : (k + 1) * block, :]
            gram_ref[i * block : (i + 1) * block, j * block : (j + 1) * block] = value
            if i != j:
                gram_ref[j * block : (j + 1) * block, i * block : (i + 1) * block] = value.T
            else:
                diagonal = jnp.where(row == column, value, 0.0)
                whole_trace += jnp.sum(diagonal)
                upper_trace += jnp.sum(
                    jnp.where(in_upper(0, block, i * block), diagonal, 0.0)
                )
    paired = paired_ref[0] == 1
    upper_scale = 1.0 / (jnp.sqrt(jnp.where(paired, upper_trace, whole_trace)) + 1e-07)
    lower_scale = 1.0 / (
        jnp.sqrt(jnp.where(paired, whole_trace - upper_trace, whole_trace)) + 1e-07
    )
    column_scale = jnp.where(in_upper(1, size, 0), upper_scale, lower_scale)

    def rows_of(step):
        return slice(step * tile, (step + 1) * tile)

    for step in range(size // tile):
        rows = rows_of(step)
        row_scale = jnp.where(in_upper(0, tile, step * tile), upper_scale, lower_scale)
        scaled = gram_ref[rows, :] * row_scale * column_scale
        gram_ref[rows, :] = scaled
        gram_half_ref[0, rows, :] = scaled.astype(jnp.bfloat16)

    for newton_step in range(NS_STEPS):
        now, later = newton_step % 2, (newton_step + 1) % 2

        for step in range(size // tile):
            rows = rows_of(step)
            square = times(gram_half_ref[now, rows, :], gram_half_ref[now])
            mix = newton_second * gram_ref[rows, :] + newton_third * square
            mix_ref[rows, :] = mix.astype(jnp.bfloat16)
            if newton_step == 0:
                same = lax.broadcasted_iota(
                    jnp.int32, (tile, size), 0
                ) + step * tile == lax.broadcasted_iota(jnp.int32, (tile, size), 1)
                total = jnp.where(same, newton_first, 0.0) + mix
                total_ref[rows, :] = total
                total_half_ref[later, rows, :] = total.astype(jnp.bfloat16)

        for step in range(size // tile):
            rows = rows_of(step)
            mix = mix_ref[rows, :]
            if newton_step > 0:
                total = newton_first * total_ref[rows, :] + times(mix, total_half_ref[now])
                if newton_step == NS_STEPS - 1:
                    out_ref[rows, :] = times(
                        (total * column_scale).astype(jnp.bfloat16), own_ref[...]
                    ).astype(jnp.bfloat16)
                else:
                    total_ref[rows, :] = total
                    total_half_ref[later, rows, :] = total.astype(jnp.bfloat16)
            if newton_step < NS_STEPS - 1:
                left = newton_first * gram_ref[rows, :] + times(mix, gram_half_ref[now])
                gram = newton_first * left + times(left.astype(jnp.bfloat16), mix_ref[...])
                gram_ref[rows, :] = gram
                gram_half_ref[later, rows, :] = gram.astype(jnp.bfloat16)


def newton(low_blocks, high_blocks, own, paired, enc_rows, dec_rows):
    size, width = own.shape
    whole = pl.BlockSpec(memory_space=pltpu.VMEM)
    return pl.pallas_call(
        functools.partial(newton_kernel, enc_rows, dec_rows),
        in_specs=[pl.BlockSpec(memory_space=pltpu.SMEM)] + [whole] * 3,
        out_specs=whole,
        out_shape=jax.ShapeDtypeStruct((size, width), jnp.bfloat16),
        scratch_shapes=[
            pltpu.VMEM((size, size), jnp.float32),
            pltpu.VMEM((size, size), jnp.float32),
            pltpu.VMEM((size, size), jnp.bfloat16),
            pltpu.VMEM((2, size, size), jnp.bfloat16),
            pltpu.VMEM((2, size, size), jnp.bfloat16),
        ],
        compiler_params=pltpu.CompilerParams(vmem_limit_bytes=newton_vmem),
        cost_estimate=pl.CostEstimate(
            flops=36 * size * size * size, bytes_accessed=20 * size * size, transcendentals=0
        ),
        name="newton",
    )(paired.astype(jnp.int32).reshape(1), low_blocks, high_blocks, own)


def gram_sum(gram):
    size = gram.shape[0] // 4

    def packed(places):
        return jnp.concatenate(
            [gram[i * size : (i + 1) * size, j * size : (j + 1) * size] for i, j in places],
            axis=0,
        )

    lower_core = lax.axis_index("mp") % 2 == 0
    low_blocks, high_blocks = packed(low_set), packed(high_set)
    own = jnp.where(lower_core, low_blocks, high_blocks)
    own = own + core_swap(jnp.where(lower_core, high_blocks, low_blocks))
    own = own + far_swap(own)
    other = core_swap(own)
    return jnp.where(lower_core, own, other), jnp.where(lower_core, other, own)


enc_slots = (2, 5, 3, 4, 6)
dec_slots = (0, 7)


def slot_rows(enc_rows_half, dec_rows_half, enc_widths, dec_widths, slot_width, data_ranks):
    enc_parts = split_columns(enc_rows_half, enc_widths)
    dec_parts = split_columns(dec_rows_half, dec_widths)
    half_width = slot_width // 2

    def widened(part, width):
        return jnp.pad(part, ((0, 0), (0, width - part.shape[1])))

    empty = jnp.zeros((enc_rows_half.shape[0], slot_width), enc_rows_half.dtype)
    slots = [empty] * data_ranks
    for part, slot in zip(enc_parts, enc_slots):
        slots[slot] = widened(part, slot_width)
    for place, slot in enumerate(dec_slots):
        upper = jnp.pad(widened(dec_parts[2 * place], half_width), ((0, 0), (0, half_width)))
        lower = jnp.pad(widened(dec_parts[2 * place + 1], half_width), ((0, 0), (half_width, 0)))
        slots[slot] = jnp.concatenate([upper, lower], axis=0)
    return jnp.stack(slots)


def unslot(rows_back, enc_widths, dec_widths, dec_rows):
    slot_width = rows_back.shape[2]
    enc_results = [rows_back[slot][:, :width] for slot, width in zip(enc_slots, enc_widths)]
    dec_results = []
    for place, width in enumerate(dec_widths):
        slot = rows_back[dec_slots[place // 2]]
        odd = place % 2
        dec_results.append(
            slot[
                odd * dec_rows : (odd + 1) * dec_rows,
                odd * (slot_width // 2) : odd * (slot_width // 2) + width,
            ]
        )
    return enc_results, dec_results


def apply_step(master, ortho_rows, widths, model_width, rate, model_ranks):
    steps_all = [
        orthogonal * (0.2 * math.sqrt(max(model_width, piece_width * model_ranks)))
        for orthogonal, piece_width in zip(ortho_rows, widths)
    ]
    return master * (1.0 - rate * decay_rate) - rate * jnp.concatenate(steps_all, axis=1)


def local(
    patches,
    cotangent,
    item_lengths,
    enc_master,
    dec_master,
    enc_norms,
    dec_norms,
    enc_moment,
    dec_moment,
    enc_norm_moment,
    dec_norm_moment,
):
    model_ranks = lax.axis_size("mp")
    data_ranks = lax.axis_size("dp")
    enc_widths = [
        3 * D // model_ranks,
        D // model_ranks,
        FF // model_ranks,
        FF // model_ranks,
        DD // model_ranks,
    ]
    dec_widths = [3 * DD // model_ranks, DD // model_ranks, DFF // model_ranks, DFF // model_ranks]
    first_cols = enc_widths[0] + enc_widths[1]
    norm_parts = gather_small(
        jnp.concatenate([enc_norms, dec_norms], axis=1).astype(jnp.bfloat16)
    ).astype(jnp.float32)
    enc_share, dec_share = enc_norms.shape[1], dec_norms.shape[1]
    enc_norm_values = jnp.moveaxis(norm_parts[:, :, :enc_share], 0, 1).reshape(4, D)
    dec_norm_values = jnp.moveaxis(norm_parts[:, :, enc_share:], 0, 1).reshape(4, DD)
    enc_half = enc_master.astype(jnp.bfloat16)
    first_gather = Gather(enc_half[:, :first_cols])
    rest_low = lax.all_gather(
        after(enc_half[:, first_cols:], first_gather.lined), "dp", axis=0, tiled=True
    )
    dec_low = lax.all_gather(
        after(dec_master.astype(jnp.bfloat16), first_gather.lined), "dp", axis=0, tiled=True
    )
    enc_pieces = split_columns(first_gather.result(), enc_widths[:2])
    dec_pieces = split_columns(dec_low, dec_widths)
    model_rank = lax.axis_index("mp")
    core = model_rank % 2
    upper_chip = model_rank // 2
    row_count = patches.shape[0]
    enc_rows = enc_master.shape[0]
    dec_rows = dec_master.shape[0]
    chunk_count = 2
    chunk_rows = row_count // chunk_count
    own_count = chunk_rows // 2
    segment, live_mask = segments_of(item_lengths[0], row_count)
    segment = swap_halves(segment, chunk_rows, core)
    live_mask = swap_halves(live_mask, chunk_rows, core)
    inputs = swap_halves(patches, chunk_rows, core)
    upstream = swap_halves(cotangent, chunk_rows, core) * live_mask.astype(jnp.bfloat16)[:, None]

    slot_width = max(enc_widths)

    def to_owners(enc_part, dec_part):
        slots = slot_rows(
            enc_part.astype(jnp.bfloat16),
            dec_part.astype(jnp.bfloat16),
            enc_widths,
            dec_widths,
            slot_width,
            data_ranks,
        )
        moved = lax.all_to_all(slots, "dp", 0, 0)
        return moved.reshape(-1, slot_width)

    input_normal, input_inverse = normalize(inputs.astype(jnp.float32))
    own_places = [slice(k * chunk_rows, k * chunk_rows + own_count) for k in range(chunk_count)]
    enc_firsts = [(input_normal[place], input_inverse[place]) for place in own_places]
    enc_rows_in = [
        (input_normal * enc_norm_values[0] + enc_norm_values[1]).astype(jnp.bfloat16)
    ]
    late_pieces = {}

    def enc_forward_hook(name, values):
        if name == "middle":
            enc_pieces.extend(split_columns(rest_low, enc_widths[2:]))
            late_pieces["bridge"] = whole_bridge(enc_pieces[4])
        return values

    def whole_bridge(bridge):
        bridge_far = far_swap(bridge)
        bridge_pair = jnp.where(
            upper_chip == 0, jnp.stack([bridge, bridge_far]), jnp.stack([bridge_far, bridge])
        )
        pair_other = core_swap(bridge_pair)
        bridge_all = jnp.stack(
            [
                jnp.where(core == 0, bridge_pair, pair_other),
                jnp.where(core == 0, pair_other, bridge_pair),
            ],
            axis=1,
        )
        share_width = bridge.shape[1]
        return jnp.moveaxis(bridge_all.reshape(-1, D, share_width), 0, 1).reshape(D, DD)

    enc_middles, enc_terms, enc_saved = block_forward(
        [inputs[place].astype(jnp.float32) for place in own_places],
        enc_rows_in,
        segment,
        enc_pieces,
        enc_norm_values,
        HD,
        enc_forward_hook,
    )
    bridge_all = late_pieces["bridge"]
    encoded_own = [
        (middle + far_sum(term)).astype(jnp.bfloat16)
        for middle, term in zip(enc_middles, enc_terms)
    ]
    decoder_in = [
        times(chunk, bridge_all).astype(jnp.bfloat16).astype(jnp.float32) for chunk in encoded_own
    ]
    encoded_rows = shared(encoded_own)
    dec_firsts = [normalize(chunk) for chunk in decoder_in]
    dec_rows_in = shared(
        [
            (normal * dec_norm_values[0] + dec_norm_values[1]).astype(jnp.bfloat16)
            for normal, _ in dec_firsts
        ]
    )
    dec_outs, dec_out_terms, dec_saved = block_forward(
        decoder_in,
        dec_rows_in,
        segment,
        dec_pieces,
        dec_norm_values,
        DHD,
        lambda name, values: values,
    )
    old_enc, old_dec, _ = lax.optimization_barrier((enc_moment, dec_moment, encoded_own[0]))
    old_slots = to_owners(old_enc, old_dec)
    upstream_rows = [
        upstream[k * own_count : (k + 1) * own_count] for k in range(2 * chunk_count)
    ]
    dec_terms, dec_middles, dec_groups, dec_norm_grads = block_backward(
        [half.astype(jnp.float32) for half in upstream_rows[::2]],
        upstream_rows,
        dec_saved,
        dec_firsts,
        dec_pieces,
        dec_norm_values,
        segment,
        DHD,
        lambda name, values, group: values,
    )
    dec_scatter = Scatter(dec_groups)
    dec_far_sums, dec_scatter.sent = lax.optimization_barrier(
        ([far_sum(term) for term in dec_terms], dec_scatter.sent)
    )
    dec_scatter.send()
    dec_in_grads = block_input_grads(dec_far_sums, dec_middles, dec_firsts, dec_norm_values)
    bridge_rows_in = shared([grad.astype(jnp.bfloat16) for grad in dec_in_grads])
    bridge_rows_in, old_slots = lax.optimization_barrier((bridge_rows_in, old_slots))
    encoded_grads = [times_turned(part, bridge_all) for part in bridge_rows_in]
    share_width = enc_widths[4]
    bridge_in_grad = [
        lax.dynamic_slice_in_dim(part, model_rank * share_width, share_width, 1)
        for part in bridge_rows_in
    ]
    scatters = {}

    def joined(values, *background):
        values, received = lax.optimization_barrier(
            (values, [scatter.received for scatter in background])
        )
        for scatter, piece in zip(background, received):
            scatter.received = piece
            scatter.fold()
        return values

    def enc_hook(name, values, group):
        if name == "start":
            scatters["down"] = Scatter([group, (encoded_rows, bridge_in_grad)])
            scatters["down"].send()
        if name == "sums":
            values = joined(values, dec_scatter)
            dec_scatter.send()
            scatters["up"] = Scatter([group])
            values, scatters["up"].sent = lax.optimization_barrier((values, scatters["up"].sent))
            scatters["up"].send()
        if name == "middle":
            scatters["out"] = group
        if name == "heads":
            values = joined(values, scatters["down"])
            scatters["down"].send()
        if name == "mixed":
            late = scatters["late"] = Scatter([group, scatters["out"]])
            late.send()
            values = after(values, late.sent)
            values = joined(values, scatters["down"], scatters["up"], dec_scatter)
            for scatter in (scatters["up"], scatters["down"], dec_scatter):
                scatter.send()
        return values

    enc_back_terms, enc_middle_grads, _, enc_norm_grads = block_backward(
        encoded_grads[::2],
        [grad.astype(jnp.bfloat16) for grad in encoded_grads],
        enc_saved,
        enc_firsts,
        enc_pieces[:4],
        enc_norm_values,
        segment,
        HD,
        enc_hook,
    )
    late, up, down = (scatters[name] for name in ("late", "up", "down"))
    norm_hops = HopSum(jnp.concatenate([enc_norm_grads, dec_norm_grads], axis=1))
    norm_hops.step(2)
    enc_back_terms, norm_hops.value, down.received, dec_scatter.received = joined(
        (enc_back_terms, norm_hops.value, down.received, dec_scatter.received), late, up
    )
    late.send()
    up.send()
    norm_hops.step(1)
    dec_sum_rows = dec_scatter.result()
    down_rows, bridge_rows = split_columns(down.result(), enc_widths[3:])
    half_width = slot_width // 2
    half_rows = [
        jnp.pad(part, ((0, 0), (0, half_width - part.shape[1])))
        for part in split_columns(dec_sum_rows, dec_widths)
    ]
    narrow_rows = [
        jnp.concatenate(half_rows[:2], axis=0),
        jnp.concatenate(half_rows[2:], axis=0),
        bridge_rows,
    ]
    norm_hops.value, up.received = joined((norm_hops.value, up.received), late)
    up_rows = up.result()
    up_half, down_half = up_rows.astype(jnp.bfloat16), down_rows.astype(jnp.bfloat16)
    late.sent, up_half, down_half, narrow_rows = lax.optimization_barrier(
        (late.sent, up_half, down_half, narrow_rows)
    )
    narrow_all = lax.all_gather(
        jnp.concatenate(narrow_rows, axis=1).astype(jnp.bfloat16), "dp", axis=0, tiled=True
    )
    late.send()
    wide_crossed = cross_pair(down_half, up_half)
    norm_hops.step(1)
    late.received, wide_crossed, norm_hops.value = lax.optimization_barrier(
        (late.received, wide_crossed, norm_hops.value)
    )
    qkv_rows, out_rows = split_columns(late.result(), enc_widths[:2])
    out_padded = jnp.pad(out_rows, ((0, 0), (0, enc_widths[0] - enc_widths[1])))
    norm_sums = norm_hops.finish()
    data_rank = lax.axis_index("dp")
    enc_sum_rows = jnp.concatenate([qkv_rows, out_rows, up_rows, down_rows, bridge_rows], axis=1)
    local_sum = jnp.sum(enc_sum_rows * enc_sum_rows) + jnp.sum(dec_sum_rows * dec_sum_rows)
    square_hops = HopSum(jnp.full((8, 128), local_sum))
    square_hops.step(3)
    tail_rows = (qkv_rows.astype(jnp.bfloat16), out_padded.astype(jnp.bfloat16))
    square_hops.value, tail_rows = lax.optimization_barrier((square_hops.value, tail_rows))
    tail_crossed = cross_pair(*tail_rows)
    squares = square_hops.finish()[0, 0]
    tail_crossed, wide_crossed, squares, norm_sums = lax.optimization_barrier(
        (tail_crossed, wide_crossed, squares, norm_sums)
    )
    squares = squares + jnp.sum(norm_sums * norm_sums)
    tail_parts = line_pair(*tail_crossed, enc_slots[:2])
    wide_parts = line_pair(*wide_crossed, enc_slots[2:4])

    def owned(parts, place):
        whole = assemble(parts, place)
        return jnp.pad(whole, ((0, 0), (0, slot_width - whole.shape[1])))

    late_slots = owned(tail_parts, data_rank // 2)
    wide_slots = owned(wide_parts, data_rank // 2)
    dec_parts = [narrow_all[:, k * half_width : (k + 1) * half_width] for k in range(2)]
    bridge_part = jnp.pad(
        narrow_all[:, slot_width:], ((0, 0), (0, half_width - enc_widths[4]))
    )
    narrow_slots = jnp.where(
        data_rank == dec_slots[0],
        dec_parts[0],
        jnp.where(data_rank == dec_slots[1], dec_parts[1], bridge_part),
    )
    narrow_slots = jnp.pad(narrow_slots, ((0, 0), (0, slot_width - half_width)))
    enc_norm_rows = lax.dynamic_slice_in_dim(norm_sums[:, :D], data_rank * enc_share, enc_share, 1)
    dec_norm_rows = lax.dynamic_slice_in_dim(norm_sums[:, D:], data_rank * dec_share, dec_share, 1)
    def natural(own_chunks):
        return swap_halves(jnp.concatenate(shared(own_chunks), axis=0), chunk_rows, core)

    dec_out_terms, _ = lax.optimization_barrier((dec_out_terms, late.received))
    decoded = [middle + far_sum(term) for middle, term in zip(dec_outs, dec_out_terms)]
    decoded = natural(decoded)
    data_rank = lax.axis_index("dp")

    def is_rank(*slots):
        return functools.reduce(jnp.logical_or, [data_rank == slot for slot in slots])

    lower_row = (jnp.arange(wide_slots.shape[0], dtype=jnp.int32) % enc_rows >= dec_rows)[:, None]
    shifted = jnp.where(
        jnp.logical_and(lower_row, is_rank(*dec_slots)),
        jnp.roll(narrow_slots, half_width, axis=1),
        narrow_slots,
    )
    grad_slots = jnp.where(
        is_rank(*enc_slots[2:4]),
        wide_slots,
        jnp.where(is_rank(*enc_slots[:2]), late_slots, shifted),
    )
    grad_norm = jnp.sqrt(squares)
    factor = clip_bound * lax.rsqrt(squares + 1e-06)
    enc_grad = enc_sum_rows * factor
    dec_grad = dec_sum_rows * factor
    enc_norm_grad = enc_norm_rows * factor
    dec_norm_grad = dec_norm_rows * factor
    dec_shift_grad = dec_norm_grad[3]
    enc_moment_new = momentum_keep * enc_moment + enc_grad
    dec_moment_new = momentum_keep * dec_moment + dec_grad
    enc_norm_moment_new = momentum_keep * enc_norm_moment + enc_norm_grad
    dec_norm_moment_new = momentum_keep * dec_norm_moment + dec_norm_grad
    own = (
        momentum_keep * old_slots.astype(jnp.float32)
        + factor * grad_slots.astype(jnp.float32)
    ).astype(jnp.bfloat16)
    low_blocks, high_blocks = gram_sum(
        lax.dot_general(own, own, (((1,), (1,)), ((), ())), preferred_element_type=jnp.float32)
    )
    orthogonal = newton(low_blocks, high_blocks, own, is_rank(*dec_slots), enc_rows, dec_rows)
    enc_far_sums = [far_sum(term) for term in after(enc_back_terms, low_blocks)]
    enc_far_sums, orthogonal = lax.optimization_barrier((enc_far_sums, orthogonal))
    input_grad = natural(
        block_input_grads(enc_far_sums, enc_middle_grads, enc_firsts, enc_norm_values)
    )
    rows_back = lax.all_to_all(
        orthogonal.reshape(data_ranks, enc_rows, slot_width), "dp", 0, 0
    ).astype(jnp.float32)
    enc_results, dec_results = unslot(rows_back, enc_widths, dec_widths, dec_rows)
    enc_master_new = apply_step(enc_master, enc_results, enc_widths, D, rate_enc, model_ranks)
    dec_master_new = apply_step(dec_master, dec_results, dec_widths, DD, rate_dec, model_ranks)
    enc_norms_new = enc_norms - rate_norm * enc_norm_moment_new
    dec_norms_new = dec_norms - rate_norm * dec_norm_moment_new
    return (
        decoded,
        input_grad,
        enc_grad,
        dec_grad,
        enc_norm_grad,
        dec_norm_grad,
        dec_shift_grad,
        enc_moment_new,
        dec_moment_new,
        enc_norm_moment_new,
        dec_norm_moment_new,
        enc_master_new,
        dec_master_new,
        enc_norms_new,
        dec_norms_new,
        enc_master_new.astype(jnp.bfloat16),
        dec_master_new.astype(jnp.bfloat16),
        enc_norms_new.astype(jnp.bfloat16),
        dec_norms_new.astype(jnp.bfloat16),
        grad_norm,
    )


def solution(mesh):
    return jax.shard_map(
        local,
        mesh=mesh,
        in_specs=(
            P("dp", None),
            P("dp", None),
            P("dp", None),
            P("dp", "mp"),
            P("dp", "mp"),
            P(None, "dp"),
            P(None, "dp"),
            P("dp", "mp"),
            P("dp", "mp"),
            P(None, "dp"),
            P(None, "dp"),
        ),
        out_specs=(
            P("dp", None),
            P("dp", None),
            P("dp", "mp"),
            P("dp", "mp"),
            P(None, "dp"),
            P(None, "dp"),
            P("dp"),
            P("dp", "mp"),
            P("dp", "mp"),
            P(None, "dp"),
            P(None, "dp"),
            P("dp", "mp"),
            P("dp", "mp"),
            P(None, "dp"),
            P(None, "dp"),
            P("dp", "mp"),
            P("dp", "mp"),
            P(None, "dp"),
            P(None, "dp"),
            P(),
        ),
        check_vma=False,
    )
```

```python
import functools
import math

import jax
import jax.numpy as jnp
from jax import lax
from jax.experimental import pallas as pl
from jax.experimental.pallas import tpu as pltpu
from jax.sharding import PartitionSpec as P

D = 1024
HD = 64
FF = 4096
DD = 512
DHD = 32
DFF = 2048
NS_STEPS = 5


highest = lax.Precision.HIGHEST
ln_eps = 1e-06
masked_score = -1e30
newton_first = 3.4445
newton_second = -4.775
newton_third = 2.0315
momentum_keep = 0.5
clip_bound = 100.0
rate_enc = 0.2
rate_dec = 0.3
rate_norm = 1.0
decay_rate = 0.01
kernel_vmem = 32 * 1024 * 1024
newton_vmem = 48 * 1024 * 1024
grads_vmem = 58 * 1024 * 1024


def shortened(array):

    def short(part):
        return part.astype(jnp.bfloat16) if part.dtype == jnp.float32 else part

    return jax.tree.map(short, array)


def pair_swap(array, axis, bit):
    size = lax.axis_size(axis)
    return lax.ppermute(array, axis, [(rank, rank ^ bit) for rank in range(size)])


def core_swap(array):
    return pair_swap(array, "mp", 1)


def far_swap(array):
    return pair_swap(array, "mp", 2)


def far_sum(chip_term):
    half = chip_term.astype(jnp.bfloat16)
    return half.astype(jnp.float32) + far_swap(half).astype(jnp.float32)


def chip_sum(own_term, other_term):
    return own_term + core_swap(other_term.astype(jnp.bfloat16)).astype(jnp.float32)


def shared(own_parts):
    return [part for own in own_parts for part in (own, core_swap(own))]


def paired(parts):
    return list(zip(parts[::2], parts[1::2]))


def times(left, right):
    return jnp.dot(left, right, preferred_element_type=jnp.float32)


def times_turned(left, right):
    return jnp.einsum("tf,df->td", left, right, preferred_element_type=jnp.float32)


def gather_small(array):
    rank = lax.axis_index("dp")
    gathered = array[None]
    bit = 1
    while bit < lax.axis_size("dp"):
        other = pair_swap(gathered, "dp", bit)
        lower = (rank & bit) == 0
        gathered = jnp.concatenate(
            [jnp.where(lower, gathered, other), jnp.where(lower, other, gathered)], axis=0
        )
        bit *= 2
    return gathered


def assemble_kernel(rank_ref, *refs):
    whole_ref = refs[-1]
    rows = refs[0].shape[0]
    for bit, part_ref in enumerate(refs[:-1]):
        place = pl.multiple_of((rank_ref[0] ^ bit) * rows, rows)
        whole_ref[pl.ds(place, rows), :] = part_ref[...]


def assemble(parts, place):
    rows, columns = parts[0].shape
    spec = pl.BlockSpec(memory_space=pltpu.VMEM)
    return pl.pallas_call(
        assemble_kernel,
        in_specs=[pl.BlockSpec(memory_space=pltpu.SMEM)] + [spec] * len(parts),
        out_specs=spec,
        out_shape=jax.ShapeDtypeStruct((len(parts) * rows, columns), parts[0].dtype),
        compiler_params=pltpu.CompilerParams(vmem_limit_bytes=grads_vmem),
        cost_estimate=pl.CostEstimate(
            flops=0, bytes_accessed=4 * len(parts) * rows * columns, transcendentals=0
        ),
        name="assemble",
    )(place.reshape(1), *parts)


class Gather:
    def __init__(self, array):
        self.general = lax.axis_size("dp") != 8
        if self.general:
            self.whole = lax.all_gather(array, "dp", axis=0, tiled=True)
            self.lined = [array]
        else:
            self.lined = [array] + [pair_swap(array, "dp", 2 * bit) for bit in (1, 2, 3)]
            self.crossed = None

    def turn(self, values):
        if self.general:
            return values
        values, self.lined = lax.optimization_barrier((values, self.lined))
        self.cross()
        return values

    def cross(self):
        self.crossed = [pair_swap(part, "dp", 1) for part in self.lined]

    def result(self):
        if self.general:
            return self.whole
        if self.crossed is None:
            self.cross()
        parts = [part for pair in zip(self.lined, self.crossed) for part in pair]
        return assemble(parts, lax.axis_index("dp"))


def collect_values(slots):
    ranks = lax.axis_size("dp")
    rank = lax.axis_index("dp")
    width = max(rows.shape[1] for rows in slots.values())
    padded = {
        owner: jnp.pad(rows.astype(jnp.bfloat16), ((0, 0), (0, width - rows.shape[1])))
        for owner, rows in slots.items()
    }
    values = []
    for bit in range(ranks):
        value = None
        for owner, rows in padded.items():
            value = rows if value is None else jnp.where(rank ^ bit == owner, rows, value)
        values.append(value)
    return values


def collect_parts(values, owners):
    return values[:1] + [
        lax.ppermute(value, "dp", [(owner ^ bit, owner) for owner in owners])
        for bit, value in enumerate(values)
        if bit
    ]


def cross_pair(even_rows, odd_rows):
    even = lax.axis_index("dp") % 2 == 0
    kept = jnp.where(even, even_rows, odd_rows)
    return kept, pair_swap(jnp.where(even, odd_rows, even_rows), "dp", 1)


def line_pair(kept, crossed, owners):
    even = lax.axis_index("dp") % 2 == 0
    lined = jnp.concatenate(
        [jnp.where(even, kept, crossed), jnp.where(even, crossed, kept)], axis=0
    )
    return [lined] + [
        lax.ppermute(lined, "dp", [(owner ^ (2 * bit), owner) for owner in owners])
        for bit in range(1, lax.axis_size("dp") // 2)
    ]


def after(value, anchor):
    return lax.optimization_barrier((value, anchor))[0]


def fold(kept, received):
    return (kept.astype(jnp.float32) + received.astype(jnp.float32)).astype(jnp.bfloat16)


def split_rows(array, place):
    half = array.shape[0] // 2
    return (
        lax.dynamic_slice_in_dim(array, (1 - place) * half, half, 0),
        lax.dynamic_slice_in_dim(array, place * half, half, 0),
    )


class Scatter:
    def __init__(self, groups):
        self.phase = 0
        self.general = lax.axis_size("dp") != 8
        self.rank = lax.axis_index("dp")
        self.sent = self.kept = self.received = None
        if self.general:
            whole = jnp.concatenate(
                [
                    jnp.einsum(
                        "td,tf->df",
                        jnp.concatenate(lefts, axis=0),
                        jnp.concatenate(rights, axis=0),
                        preferred_element_type=jnp.float32,
                    ).astype(jnp.bfloat16)
                    for lefts, rights in groups
                ],
                axis=1,
            )
            self.total = lax.psum_scatter(whole, "dp", scatter_dimension=0, tiled=True)
        else:
            self.sent, self.kept = weight_grads(groups, self.rank % 2)

    def send(self):
        if not self.general:
            self.received = pair_swap(self.sent, "dp", 1 << self.phase)

    def fold(self):
        if not self.general:
            place = self.rank // 2 % 2 if self.phase == 0 else self.rank // 4
            self.sent, self.kept = split_rows(fold(self.kept, self.received), place)
            self.phase += 1

    def result(self):
        if self.general:
            return self.total.astype(jnp.float32)
        return self.kept.astype(jnp.float32) + self.received.astype(jnp.float32)


class HopSum:
    def __init__(self, value):
        self.value = value
        self.hops = [
            (axis, 1 << bit)
            for axis in ("mp", "dp")
            for bit in range(lax.axis_size(axis).bit_length() - 1)
        ]

    def step(self, count):
        for axis, bit in self.hops[:count]:
            self.value = self.value + pair_swap(self.value, axis, bit)
        self.hops = self.hops[count:]

    def finish(self):
        self.step(len(self.hops))
        return self.value


def normalize(values):
    center = values - jnp.mean(values, axis=-1, keepdims=True)
    inverse = lax.rsqrt(jnp.mean(center * center, axis=-1, keepdims=True) + ln_eps)
    return center * inverse, inverse


def normalize_back(normal, inverse, gain_row, out_grad):
    scaled = out_grad * gain_row
    mean_grad = jnp.mean(scaled, axis=-1, keepdims=True)
    mean_dot = jnp.mean(scaled * normal, axis=-1, keepdims=True)
    return inverse * (scaled - mean_grad - normal * mean_dot)


def gelu_and_slope(hidden):
    spread = 0.5 + 0.5 * lax.erf(hidden * math.sqrt(0.5))
    density = jnp.exp(-0.5 * hidden * hidden) * (1.0 / math.sqrt(2.0 * math.pi))
    return hidden * spread, spread + hidden * density


def swap_halves(array, chunk_rows, core):
    parts = array.reshape((-1, 2, chunk_rows // 2) + array.shape[1:])
    return jnp.where(core == 0, parts, parts[:, ::-1]).reshape(array.shape)


def segments_of(lengths, row_count):
    item_ends = jnp.cumsum(lengths)
    position = jnp.arange(row_count, dtype=jnp.int32)
    segment = jnp.sum((position[:, None] >= item_ends[None, :]).astype(jnp.int32), axis=1)
    live_mask = (position < item_ends[-1]).astype(jnp.float32)
    return (segment, live_mask)


def split_columns(whole_cols, widths):
    pieces = []
    start_col = 0
    for piece_width in widths:
        pieces.append(whole_cols[:, start_col : start_col + piece_width])
        start_col += piece_width
    return pieces


def head_mask(head, head_width, inner_width):
    lane = lax.broadcasted_iota(jnp.int32, (1, inner_width), 1)
    inside = jnp.logical_and(lane >= head * head_width, lane < (head + 1) * head_width)
    return jnp.where(inside, 1.0, 0.0)


def masked_rows(rows, head, head_width):
    mask = head_mask(head, head_width, rows.shape[1])
    return (rows.astype(jnp.float32) * mask).astype(jnp.bfloat16)


def last_dims(left, right):
    return lax.dot_general(
        left, right, (((1,), (1,)), ((), ())), preferred_element_type=jnp.float32
    )


def segment_bias(key_segment_ref, query_segment_ref):
    return jnp.where(key_segment_ref[...] == query_segment_ref[...], 0.0, masked_score)


def joined_columns(refs, first, last):
    return jnp.concatenate([ref[:, first:last] for ref in refs], axis=0)


def attend_forward_kernel(
    head_width, place, count, key_segment_ref, query_segment_ref, *refs
):
    mixed_refs, (own_ref, other_ref, logsum_ref) = refs[:count], refs[count:]
    block_rows = query_segment_ref.shape[0]
    half_rows, inner_width = own_ref.shape
    score_scale = head_width ** (-0.5)
    bias = segment_bias(key_segment_ref, query_segment_ref)
    if count == 1:
        rows = mixed_refs[0][place * block_rows : (place + 1) * block_rows, :inner_width]
    else:
        rows = joined_columns(mixed_refs[2 * place : 2 * place + 2], 0, inner_width)
    keys = joined_columns(mixed_refs, inner_width, 2 * inner_width)
    values = joined_columns(mixed_refs, 2 * inner_width, 3 * inner_width)
    total_out = jnp.zeros((block_rows, inner_width), jnp.float32)
    logsums = []
    for head in range(inner_width // head_width):
        scores = last_dims(masked_rows(rows, head, head_width), keys) * score_scale + bias
        top = jnp.max(scores, axis=1, keepdims=True)
        shifted = jnp.exp(scores - top)
        total = jnp.sum(shifted, axis=1, keepdims=True)
        part = times(shifted.astype(jnp.bfloat16), values)
        total_out += part * (head_mask(head, head_width, inner_width) / total)
        logsums.append(jnp.broadcast_to(top + jnp.log(total), (block_rows, 128)))
    own_ref[...] = total_out[:half_rows].astype(jnp.bfloat16)
    other_ref[...] = total_out[half_rows:].astype(jnp.bfloat16)
    lane = lax.broadcasted_iota(jnp.int32, (block_rows, 128), 1)
    stacked = logsums[0]
    for head in range(1, len(logsums)):
        stacked = jnp.where(lane == head, logsums[head], stacked)
    logsum_ref[...] = stacked.T[: len(logsums), :]


def attend_forward(mixed, segment, place, head_width, block_rows):
    row_count = segment.shape[0]
    inner_width = mixed[0].shape[1] // 3
    head_count = inner_width // head_width
    whole = pl.BlockSpec(memory_space=pltpu.VMEM)
    half = jax.ShapeDtypeStruct((block_rows // 2, inner_width), jnp.bfloat16)
    return pl.pallas_call(
        functools.partial(attend_forward_kernel, head_width, place, len(mixed)),
        in_specs=[whole] * (2 + len(mixed)),
        out_specs=[whole] * 3,
        out_shape=[half, half, jax.ShapeDtypeStruct((head_count, block_rows), jnp.float32)],
        compiler_params=pltpu.CompilerParams(vmem_limit_bytes=kernel_vmem),
        cost_estimate=pl.CostEstimate(
            flops=4 * block_rows * row_count * inner_width * head_count,
            bytes_accessed=8 * row_count * inner_width,
            transcendentals=block_rows * row_count * head_count,
        ),
        name="attend_forward",
    )(
        segment.reshape(1, row_count),
        segment[place * block_rows : (place + 1) * block_rows].reshape(block_rows, 1),
        *mixed,
    )


def attend_backward_kernel(head_width, count, key_segment_ref, query_segment_ref, *refs):
    grad_refs, logsum_refs, refs = refs[:4], refs[4:6], refs[6:]
    mixed_refs, out_refs, refs = refs[:count], refs[count : count + 4], refs[count + 4 :]
    turned_ref, grad_ref, query_ref, bias_ref, query_grad_ref, key_total_ref, value_total_ref = refs
    row_count, inner_width = grad_ref.shape
    part_rows = row_count // 4
    block_rows = row_count // 2
    score_scale = head_width ** (-0.5)
    keys = joined_columns(mixed_refs, inner_width, 2 * inner_width)
    values = joined_columns(mixed_refs, 2 * inner_width, 3 * inner_width)
    turned_ref[...] = keys.astype(jnp.float32).T.astype(jnp.bfloat16)
    for k in range(4):
        grad_ref[k * part_rows : (k + 1) * part_rows, :] = grad_refs[k][...]
    query_ref[...] = joined_columns(mixed_refs, 0, inner_width)
    key_total_ref[...] = jnp.zeros_like(key_total_ref)
    value_total_ref[...] = jnp.zeros_like(value_total_ref)
    for block in range(2):
        bias_ref[block] = jnp.where(
            key_segment_ref[...]
            == query_segment_ref[:, block * block_rows : (block + 1) * block_rows],
            0.0,
            masked_score,
        )

    @pl.loop(0, 2)
    def _(block):
        rows = pl.ds(pl.multiple_of(block * block_rows, block_rows), block_rows)
        parts, attentions, score_grads, grads, queries = [], [], [], [], []
        for head in range(inner_width // head_width):
            query = masked_rows(query_ref[rows, :], head, head_width)
            grad = masked_rows(grad_ref[rows, :], head, head_width)
            logsum = jnp.where(
                block == 0,
                logsum_refs[0][head : head + 1, :],
                logsum_refs[1][head : head + 1, :],
            )
            scores = last_dims(keys, query) * score_scale + bias_ref[block]
            attention = jnp.exp(scores - logsum)
            weighted = attention * last_dims(values, grad)
            row_dot = jnp.sum(weighted, axis=0, keepdims=True)
            score_grad = (weighted - attention * row_dot).astype(jnp.bfloat16)
            attentions.append(attention.astype(jnp.bfloat16))
            score_grads.append(score_grad)
            grads.append(grad)
            queries.append(query)
            parts.append(
                times(turned_ref[head * head_width : (head + 1) * head_width, :], score_grad)
            )
        value_total_ref[...] += times(
            jnp.concatenate(attentions, axis=1), jnp.concatenate(grads, axis=0)
        )
        key_total_ref[...] += times(
            jnp.concatenate(score_grads, axis=1), jnp.concatenate(queries, axis=0)
        )
        query_grad_ref[rows, :] = (jnp.concatenate(parts, axis=0) * score_scale).T

    for k, out_ref in enumerate(out_refs):
        rows = slice(k * part_rows, (k + 1) * part_rows)
        out_ref[:, :inner_width] = query_grad_ref[rows, :].astype(jnp.bfloat16)
        out_ref[:, inner_width : 2 * inner_width] = (key_total_ref[rows, :] * score_scale).astype(
            jnp.bfloat16
        )
        out_ref[:, 2 * inner_width :] = value_total_ref[rows, :].astype(jnp.bfloat16)


def attend_backward(heads_grads, mixed, logsums, segment, head_width):
    row_count = segment.shape[0]
    part_rows, inner_width = heads_grads[0].shape
    head_count = inner_width // head_width
    whole = pl.BlockSpec(memory_space=pltpu.VMEM)
    part = jax.ShapeDtypeStruct((part_rows, 3 * inner_width), jnp.bfloat16)
    return pl.pallas_call(
        functools.partial(attend_backward_kernel, head_width, len(mixed)),
        in_specs=[whole] * (8 + len(mixed)),
        out_specs=[whole] * 4,
        out_shape=[part] * 4,
        scratch_shapes=[
            pltpu.VMEM((inner_width, row_count), jnp.bfloat16),
            pltpu.VMEM((row_count, inner_width), jnp.bfloat16),
            pltpu.VMEM((row_count, inner_width), jnp.bfloat16),
            pltpu.VMEM((2, row_count, row_count // 2), jnp.float32),
            pltpu.VMEM((row_count, inner_width), jnp.float32),
            pltpu.VMEM((row_count, inner_width), jnp.float32),
            pltpu.VMEM((row_count, inner_width), jnp.float32),
        ],
        compiler_params=pltpu.CompilerParams(vmem_limit_bytes=kernel_vmem),
        cost_estimate=pl.CostEstimate(
            flops=10 * row_count * row_count * inner_width * head_count,
            bytes_accessed=14 * row_count * inner_width,
            transcendentals=row_count * row_count * head_count,
        ),
        name="attend_backward",
    )(
        segment.reshape(row_count, 1),
        segment.reshape(1, row_count),
        *heads_grads,
        *logsums,
        *mixed,
    )


def block_forward(own_chunks, rows, segment, pieces, norm_values, head_width, hook):
    qkv_proj, out_proj = pieces[:2]
    mixed = [times(part, qkv_proj).astype(jnp.bfloat16) for part in rows]
    block_rows = segment.shape[0] // len(own_chunks)
    heads, logsums, middles = [], [], []
    for place, own in enumerate(own_chunks):
        own_heads, other_heads, logsum = attend_forward(
            mixed, segment, place, head_width, block_rows
        )
        heads += [own_heads, other_heads]
        logsums.append(logsum)
        chip_term = chip_sum(
            times_turned(own_heads, out_proj), times_turned(other_heads, out_proj)
        )
        middles.append(own + far_sum(chip_term))
    middles = hook("middle", middles)
    up_proj, down_proj = pieces[2:4]
    seconds, chip_terms, ups, activated, slopes = [], [], [], [], []
    for middle in middles:
        normal, inverse = normalize(middle)
        parts = shared([(normal * norm_values[2] + norm_values[3]).astype(jnp.bfloat16)])
        partials = []
        for part in parts:
            value, slope = gelu_and_slope(times(part, up_proj))
            value = value.astype(jnp.bfloat16)
            partials.append(times_turned(value, down_proj))
            activated.append(value)
            slopes.append(slope)
        ups += parts
        chip_terms.append(chip_sum(*partials))
        seconds.append((normal, inverse))
    return middles, chip_terms, (rows, mixed, heads, logsums, seconds, ups, activated, slopes)


def block_backward(
    own_grads, half_rows, saved, firsts, pieces, norm_values, segment, head_width, hook
):
    rows, mixed, heads, logsums, seconds, ups, activated, slopes = saved
    qkv_proj, out_proj, up_proj, down_proj = pieces
    down_group = (half_rows, activated)
    half_rows = hook("start", half_rows, down_group)
    hidden_rows = [
        (times(half, down_proj) * slope).astype(jnp.bfloat16)
        for half, slope in zip(half_rows, slopes)
    ]
    chip_terms = [
        chip_sum(times_turned(own, up_proj), times_turned(other, up_proj))
        for own, other in paired(hidden_rows)
    ]
    up_group = (ups, hidden_rows)
    normed_grads = hook("sums", [far_sum(chip_term) for chip_term in chip_terms], up_group)
    middle_grads, gain_two, shift_two = [], 0.0, 0.0
    for own_grad, chip_term, normed_grad, (normal, inverse) in zip(
        own_grads, chip_terms, normed_grads, seconds
    ):
        gain_two = gain_two + jnp.sum(chip_term * normal, axis=0)
        shift_two = shift_two + jnp.sum(chip_term, axis=0)
        middle_grads.append(
            own_grad + normalize_back(normal, inverse, norm_values[2], normed_grad)
        )
    middle_rows = shared([grad.astype(jnp.bfloat16) for grad in middle_grads])
    out_group = (middle_rows, heads)
    middle_rows = hook("middle", middle_rows, out_group)
    heads_grads = [times(part, out_proj).astype(jnp.bfloat16) for part in middle_rows]
    heads_grads = hook("heads", heads_grads, None)
    mixed_grads = attend_backward(heads_grads, mixed, logsums, segment, head_width)
    qkv_group = (rows, mixed_grads)
    mixed_grads = hook("mixed", mixed_grads, qkv_group)
    chip_terms = [
        chip_sum(times_turned(own, qkv_proj), times_turned(other, qkv_proj))
        for own, other in paired(mixed_grads)
    ]
    gain_one, shift_one = 0.0, 0.0
    for chip_term, (normal, _) in zip(chip_terms, firsts):
        gain_one = gain_one + jnp.sum(chip_term * normal, axis=0)
        shift_one = shift_one + jnp.sum(chip_term, axis=0)
    norm_grads = jnp.stack([gain_one, shift_one, gain_two, shift_two])
    groups = [qkv_group, out_group, up_group, down_group]
    return chip_terms, middle_grads, groups, norm_grads


def block_input_grads(far_sums, middle_grads, firsts, norm_values):
    return [
        middle_grad + normalize_back(normal, inverse, norm_values[0], normed_grad)
        for middle_grad, normed_grad, (normal, inverse) in zip(middle_grads, far_sums, firsts)
    ]


def row_pieces(refs, count):
    if len(refs) == count:
        return [ref[...] for ref in refs]
    rows = refs[0].shape[0] // count
    return [refs[0][k * rows : (k + 1) * rows, :] for k in range(count)]


def weight_grads_kernel(counts, parity_ref, *refs):
    sent_ref, kept_ref = refs[-2:]
    even = parity_ref[0] == 0
    place, column = 0, 0
    for left_count, right_count in counts:
        count = max(left_count, right_count)
        lefts = row_pieces(refs[place : place + left_count], count)
        place += left_count
        rights = row_pieces(refs[place : place + right_count], count)
        place += right_count
        total = 0.0
        for left, right in zip(lefts, rights):
            total = total + lax.dot_general(
                left, right, (((0,), (0,)), ((), ())), preferred_element_type=jnp.float32
            )
        half = total.shape[0] // 2
        columns = slice(column, column + total.shape[1])
        upper, lower = total[:half], total[half:]
        sent_ref[:, columns] = jnp.where(even, lower, upper).astype(jnp.bfloat16)
        kept_ref[:, columns] = jnp.where(even, upper, lower).astype(jnp.bfloat16)
        column += total.shape[1]


def weight_grads(groups, parity):
    width = groups[0][0][0].shape[1]
    specs, operands, flops = [], [], 0
    for lefts, rights in groups:
        for left in lefts:
            specs.append(
                pl.BlockSpec((left.shape[0], width // 4), lambda i: (0, i % 2 * 2 + i // 2))
            )
            operands.append(left)
        for right in rights:
            specs.append(pl.BlockSpec(right.shape, lambda i: (0, 0)))
            operands.append(right)
            flops += 2 * width * right.shape[0] * right.shape[1]
    columns = sum(rights[0].shape[1] for _, rights in groups)
    half = jax.ShapeDtypeStruct((width // 2, columns), jnp.bfloat16)
    return pl.pallas_call(
        functools.partial(
            weight_grads_kernel, [(len(lefts), len(rights)) for lefts, rights in groups]
        ),
        grid=(4,),
        in_specs=[pl.BlockSpec(memory_space=pltpu.SMEM)] + specs,
        out_specs=[pl.BlockSpec((width // 8, columns), lambda i: (i, 0))] * 2,
        out_shape=[half, half],
        compiler_params=pltpu.CompilerParams(
            dimension_semantics=("arbitrary",), vmem_limit_bytes=grads_vmem
        ),
        cost_estimate=pl.CostEstimate(
            flops=flops,
            bytes_accessed=2 * sum(operand.size for operand in operands) + 2 * width * columns,
            transcendentals=0,
        ),
        name="weight_grads",
    )(parity.reshape(1), *operands)


low_set = ((0, 0), (0, 1), (0, 2), (0, 3), (1, 1))
high_set = ((2, 2), (2, 3), (3, 3), (1, 2), (1, 3))


def newton_kernel(
    enc_rows, dec_rows, paired_ref, low_ref, high_ref, own_ref, out_ref, gram_ref, total_ref,
    mix_ref, gram_half_ref, total_half_ref,
):
    size = gram_ref.shape[0]
    block = size // 4
    tile = size // 2

    def in_upper(axis, count, start):
        shape = (count, 1) if axis == 0 else (1, count)
        place = start + lax.broadcasted_iota(jnp.int32, shape, axis)
        return place % enc_rows < dec_rows

    row = lax.broadcasted_iota(jnp.int32, (block, block), 0)
    column = lax.broadcasted_iota(jnp.int32, (block, block), 1)
    upper_trace, whole_trace = 0.0, 0.0
    for places, blocks_ref in ((low_set, low_ref), (high_set, high_ref)):
        for k, (i, j) in enumerate(places):
            value = blocks_ref[k * block : (k + 1) * block, :]
            gram_ref[i * block : (i + 1) * block, j * block : (j + 1) * block] = value
            if i != j:
                gram_ref[j * block : (j + 1) * block, i * block : (i + 1) * block] = value.T
            else:
                diagonal = jnp.where(row == column, value, 0.0)
                whole_trace += jnp.sum(diagonal)
                upper_trace += jnp.sum(
                    jnp.where(in_upper(0, block, i * block), diagonal, 0.0)
                )
    paired = paired_ref[0] == 1
    upper_scale = 1.0 / (jnp.sqrt(jnp.where(paired, upper_trace, whole_trace)) + 1e-07)
    lower_scale = 1.0 / (
        jnp.sqrt(jnp.where(paired, whole_trace - upper_trace, whole_trace)) + 1e-07
    )
    column_scale = jnp.where(in_upper(1, size, 0), upper_scale, lower_scale)

    def rows_of(step):
        return slice(step * tile, (step + 1) * tile)

    for step in range(size // tile):
        rows = rows_of(step)
        row_scale = jnp.where(in_upper(0, tile, step * tile), upper_scale, lower_scale)
        scaled = gram_ref[rows, :] * row_scale * column_scale
        gram_ref[rows, :] = scaled
        gram_half_ref[0, rows, :] = scaled.astype(jnp.bfloat16)

    for newton_step in range(NS_STEPS):
        now, later = newton_step % 2, (newton_step + 1) % 2

        for step in range(size // tile):
            rows = rows_of(step)
            square = times(gram_half_ref[now, rows, :], gram_half_ref[now])
            mix = newton_second * gram_ref[rows, :] + newton_third * square
            mix_ref[rows, :] = mix.astype(jnp.bfloat16)
            if newton_step == 0:
                same = lax.broadcasted_iota(
                    jnp.int32, (tile, size), 0
                ) + step * tile == lax.broadcasted_iota(jnp.int32, (tile, size), 1)
                total = jnp.where(same, newton_first, 0.0) + mix
                total_ref[rows, :] = total
                total_half_ref[later, rows, :] = total.astype(jnp.bfloat16)

        for step in range(size // tile):
            rows = rows_of(step)
            mix = mix_ref[rows, :]
            if newton_step > 0:
                total = newton_first * total_ref[rows, :] + times(mix, total_half_ref[now])
                if newton_step == NS_STEPS - 1:
                    out_ref[rows, :] = times(
                        (total * column_scale).astype(jnp.bfloat16), own_ref[...]
                    ).astype(jnp.bfloat16)
                else:
                    total_ref[rows, :] = total
                    total_half_ref[later, rows, :] = total.astype(jnp.bfloat16)
            if newton_step < NS_STEPS - 1:
                left = newton_first * gram_ref[rows, :] + times(mix, gram_half_ref[now])
                gram = newton_first * left + times(left.astype(jnp.bfloat16), mix_ref[...])
                gram_ref[rows, :] = gram
                gram_half_ref[later, rows, :] = gram.astype(jnp.bfloat16)


def newton(low_blocks, high_blocks, own, paired, enc_rows, dec_rows):
    size, width = own.shape
    whole = pl.BlockSpec(memory_space=pltpu.VMEM)
    return pl.pallas_call(
        functools.partial(newton_kernel, enc_rows, dec_rows),
        in_specs=[pl.BlockSpec(memory_space=pltpu.SMEM)] + [whole] * 3,
        out_specs=whole,
        out_shape=jax.ShapeDtypeStruct((size, width), jnp.bfloat16),
        scratch_shapes=[
            pltpu.VMEM((size, size), jnp.float32),
            pltpu.VMEM((size, size), jnp.float32),
            pltpu.VMEM((size, size), jnp.bfloat16),
            pltpu.VMEM((2, size, size), jnp.bfloat16),
            pltpu.VMEM((2, size, size), jnp.bfloat16),
        ],
        compiler_params=pltpu.CompilerParams(vmem_limit_bytes=newton_vmem),
        cost_estimate=pl.CostEstimate(
            flops=36 * size * size * size, bytes_accessed=20 * size * size, transcendentals=0
        ),
        name="newton",
    )(paired.astype(jnp.int32).reshape(1), low_blocks, high_blocks, own)


def gram_sum(gram):
    size = gram.shape[0] // 4

    def packed(places):
        return jnp.concatenate(
            [gram[i * size : (i + 1) * size, j * size : (j + 1) * size] for i, j in places],
            axis=0,
        )

    lower_core = lax.axis_index("mp") % 2 == 0
    low_blocks, high_blocks = packed(low_set), packed(high_set)
    own = jnp.where(lower_core, low_blocks, high_blocks)
    own = own + core_swap(jnp.where(lower_core, high_blocks, low_blocks))
    own = own + far_swap(own)
    other = core_swap(own)
    return jnp.where(lower_core, own, other), jnp.where(lower_core, other, own)


enc_slots = (2, 5, 3, 4, 6)
dec_slots = (0, 7)


def slot_rows(enc_rows_half, dec_rows_half, enc_widths, dec_widths, slot_width, data_ranks):
    enc_parts = split_columns(enc_rows_half, enc_widths)
    dec_parts = split_columns(dec_rows_half, dec_widths)
    half_width = slot_width // 2

    def widened(part, width):
        return jnp.pad(part, ((0, 0), (0, width - part.shape[1])))

    empty = jnp.zeros((enc_rows_half.shape[0], slot_width), enc_rows_half.dtype)
    slots = [empty] * data_ranks
    for part, slot in zip(enc_parts, enc_slots):
        slots[slot] = widened(part, slot_width)
    for place, slot in enumerate(dec_slots):
        upper = jnp.pad(widened(dec_parts[2 * place], half_width), ((0, 0), (0, half_width)))
        lower = jnp.pad(widened(dec_parts[2 * place + 1], half_width), ((0, 0), (half_width, 0)))
        slots[slot] = jnp.concatenate([upper, lower], axis=0)
    return jnp.stack(slots)


def unslot(rows_back, enc_widths, dec_widths, dec_rows):
    slot_width = rows_back.shape[2]
    enc_results = [rows_back[slot][:, :width] for slot, width in zip(enc_slots, enc_widths)]
    dec_results = []
    for place, width in enumerate(dec_widths):
        slot = rows_back[dec_slots[place // 2]]
        odd = place % 2
        dec_results.append(
            slot[
                odd * dec_rows : (odd + 1) * dec_rows,
                odd * (slot_width // 2) : odd * (slot_width // 2) + width,
            ]
        )
    return enc_results, dec_results


def apply_step(master, ortho_rows, widths, model_width, rate, model_ranks):
    steps_all = [
        orthogonal * (0.2 * math.sqrt(max(model_width, piece_width * model_ranks)))
        for orthogonal, piece_width in zip(ortho_rows, widths)
    ]
    return master * (1.0 - rate * decay_rate) - rate * jnp.concatenate(steps_all, axis=1)


def local(
    patches,
    cotangent,
    item_lengths,
    enc_master,
    dec_master,
    enc_norms,
    dec_norms,
    enc_moment,
    dec_moment,
    enc_norm_moment,
    dec_norm_moment,
):
    model_ranks = lax.axis_size("mp")
    data_ranks = lax.axis_size("dp")
    enc_widths = [
        3 * D // model_ranks,
        D // model_ranks,
        FF // model_ranks,
        FF // model_ranks,
        DD // model_ranks,
    ]
    dec_widths = [3 * DD // model_ranks, DD // model_ranks, DFF // model_ranks, DFF // model_ranks]
    first_cols = enc_widths[0] + enc_widths[1]
    norm_parts = gather_small(
        jnp.concatenate([enc_norms, dec_norms], axis=1).astype(jnp.bfloat16)
    ).astype(jnp.float32)
    enc_share, dec_share = enc_norms.shape[1], dec_norms.shape[1]
    enc_norm_values = jnp.moveaxis(norm_parts[:, :, :enc_share], 0, 1).reshape(4, D)
    dec_norm_values = jnp.moveaxis(norm_parts[:, :, enc_share:], 0, 1).reshape(4, DD)
    enc_half = enc_master.astype(jnp.bfloat16)
    first_gather = Gather(enc_half[:, :first_cols])
    rest_low = lax.all_gather(
        after(enc_half[:, first_cols:], first_gather.lined), "dp", axis=0, tiled=True
    )
    dec_low = lax.all_gather(
        after(dec_master.astype(jnp.bfloat16), first_gather.lined), "dp", axis=0, tiled=True
    )
    enc_pieces = split_columns(first_gather.result(), enc_widths[:2])
    dec_pieces = split_columns(dec_low, dec_widths)
    model_rank = lax.axis_index("mp")
    core = model_rank % 2
    upper_chip = model_rank // 2
    row_count = patches.shape[0]
    enc_rows = enc_master.shape[0]
    dec_rows = dec_master.shape[0]
    chunk_count = 2
    chunk_rows = row_count // chunk_count
    own_count = chunk_rows // 2
    segment, live_mask = segments_of(item_lengths[0], row_count)
    segment = swap_halves(segment, chunk_rows, core)
    live_mask = swap_halves(live_mask, chunk_rows, core)
    inputs = swap_halves(patches, chunk_rows, core)
    upstream = swap_halves(cotangent, chunk_rows, core) * live_mask.astype(jnp.bfloat16)[:, None]

    slot_width = max(enc_widths)

    def to_owners(enc_part, dec_part):
        slots = slot_rows(
            enc_part.astype(jnp.bfloat16),
            dec_part.astype(jnp.bfloat16),
            enc_widths,
            dec_widths,
            slot_width,
            data_ranks,
        )
        moved = lax.all_to_all(slots, "dp", 0, 0)
        return moved.reshape(-1, slot_width)

    input_normal, input_inverse = normalize(inputs.astype(jnp.float32))
    own_places = [slice(k * chunk_rows, k * chunk_rows + own_count) for k in range(chunk_count)]
    enc_firsts = [(input_normal[place], input_inverse[place]) for place in own_places]
    enc_rows_in = [
        (input_normal * enc_norm_values[0] + enc_norm_values[1]).astype(jnp.bfloat16)
    ]
    late_pieces = {}

    def enc_forward_hook(name, values):
        if name == "middle":
            enc_pieces.extend(split_columns(rest_low, enc_widths[2:]))
            late_pieces["bridge"] = whole_bridge(enc_pieces[4])
        return values

    def whole_bridge(bridge):
        bridge_far = far_swap(bridge)
        bridge_pair = jnp.where(
            upper_chip == 0, jnp.stack([bridge, bridge_far]), jnp.stack([bridge_far, bridge])
        )
        pair_other = core_swap(bridge_pair)
        bridge_all = jnp.stack(
            [
                jnp.where(core == 0, bridge_pair, pair_other),
                jnp.where(core == 0, pair_other, bridge_pair),
            ],
            axis=1,
        )
        share_width = bridge.shape[1]
        return jnp.moveaxis(bridge_all.reshape(-1, D, share_width), 0, 1).reshape(D, DD)

    enc_middles, enc_terms, enc_saved = block_forward(
        [inputs[place].astype(jnp.float32) for place in own_places],
        enc_rows_in,
        segment,
        enc_pieces,
        enc_norm_values,
        HD,
        enc_forward_hook,
    )
    bridge_all = late_pieces["bridge"]
    encoded_own = [
        (middle + far_sum(term)).astype(jnp.bfloat16)
        for middle, term in zip(enc_middles, enc_terms)
    ]
    decoder_in = [
        times(chunk, bridge_all).astype(jnp.bfloat16).astype(jnp.float32) for chunk in encoded_own
    ]
    encoded_rows = shared(encoded_own)
    dec_firsts = [normalize(chunk) for chunk in decoder_in]
    dec_rows_in = shared(
        [
            (normal * dec_norm_values[0] + dec_norm_values[1]).astype(jnp.bfloat16)
            for normal, _ in dec_firsts
        ]
    )
    dec_outs, dec_out_terms, dec_saved = block_forward(
        decoder_in,
        dec_rows_in,
        segment,
        dec_pieces,
        dec_norm_values,
        DHD,
        lambda name, values: values,
    )
    old_enc, old_dec, _ = lax.optimization_barrier((enc_moment, dec_moment, encoded_own[0]))
    old_slots = to_owners(old_enc, old_dec)
    upstream_rows = [
        upstream[k * own_count : (k + 1) * own_count] for k in range(2 * chunk_count)
    ]
    dec_terms, dec_middles, dec_groups, dec_norm_grads = block_backward(
        [half.astype(jnp.float32) for half in upstream_rows[::2]],
        upstream_rows,
        dec_saved,
        dec_firsts,
        dec_pieces,
        dec_norm_values,
        segment,
        DHD,
        lambda name, values, group: values,
    )
    dec_scatter = Scatter(dec_groups)
    dec_far_sums, dec_scatter.sent = lax.optimization_barrier(
        ([far_sum(term) for term in dec_terms], dec_scatter.sent)
    )
    dec_scatter.send()
    dec_in_grads = block_input_grads(dec_far_sums, dec_middles, dec_firsts, dec_norm_values)
    bridge_rows_in = shared([grad.astype(jnp.bfloat16) for grad in dec_in_grads])
    bridge_rows_in, old_slots = lax.optimization_barrier((bridge_rows_in, old_slots))
    encoded_grads = [times_turned(part, bridge_all) for part in bridge_rows_in]
    share_width = enc_widths[4]
    bridge_in_grad = [
        lax.dynamic_slice_in_dim(part, model_rank * share_width, share_width, 1)
        for part in bridge_rows_in
    ]
    scatters = {}

    def joined(values, *background):
        values, received = lax.optimization_barrier(
            (values, [scatter.received for scatter in background])
        )
        for scatter, piece in zip(background, received):
            scatter.received = piece
            scatter.fold()
        return values

    def enc_hook(name, values, group):
        if name == "start":
            scatters["down"] = Scatter([group, (encoded_rows, bridge_in_grad)])
            scatters["down"].send()
        if name == "sums":
            values = joined(values, dec_scatter)
            dec_scatter.send()
            scatters["up"] = Scatter([group])
            values, scatters["up"].sent = lax.optimization_barrier((values, scatters["up"].sent))
            scatters["up"].send()
        if name == "middle":
            scatters["out"] = group
        if name == "heads":
            values = joined(values, scatters["down"])
            scatters["down"].send()
        if name == "mixed":
            late = scatters["late"] = Scatter([group, scatters["out"]])
            late.send()
            values = after(values, late.sent)
            values = joined(values, scatters["down"], scatters["up"], dec_scatter)
            for scatter in (scatters["up"], scatters["down"], dec_scatter):
                scatter.send()
        return values

    enc_back_terms, enc_middle_grads, _, enc_norm_grads = block_backward(
        encoded_grads[::2],
        [grad.astype(jnp.bfloat16) for grad in encoded_grads],
        enc_saved,
        enc_firsts,
        enc_pieces[:4],
        enc_norm_values,
        segment,
        HD,
        enc_hook,
    )
    late, up, down = (scatters[name] for name in ("late", "up", "down"))
    norm_hops = HopSum(jnp.concatenate([enc_norm_grads, dec_norm_grads], axis=1))
    norm_hops.step(2)
    enc_back_terms, norm_hops.value, down.received, dec_scatter.received = joined(
        (enc_back_terms, norm_hops.value, down.received, dec_scatter.received), late, up
    )
    late.send()
    up.send()
    norm_hops.step(1)
    dec_sum_rows = dec_scatter.result()
    down_rows, bridge_rows = split_columns(down.result(), enc_widths[3:])
    half_width = slot_width // 2
    half_rows = [
        jnp.pad(part, ((0, 0), (0, half_width - part.shape[1])))
        for part in split_columns(dec_sum_rows, dec_widths)
    ]
    narrow_rows = [
        jnp.concatenate(half_rows[:2], axis=0),
        jnp.concatenate(half_rows[2:], axis=0),
        bridge_rows,
    ]
    norm_hops.value, up.received = joined((norm_hops.value, up.received), late)
    up_rows = up.result()
    up_half, down_half = up_rows.astype(jnp.bfloat16), down_rows.astype(jnp.bfloat16)
    late.sent, up_half, down_half, narrow_rows = lax.optimization_barrier(
        (late.sent, up_half, down_half, narrow_rows)
    )
    narrow_all = lax.all_gather(
        jnp.concatenate(narrow_rows, axis=1).astype(jnp.bfloat16), "dp", axis=0, tiled=True
    )
    late.send()
    wide_crossed = cross_pair(down_half, up_half)
    norm_hops.step(1)
    late.received, wide_crossed, norm_hops.value = lax.optimization_barrier(
        (late.received, wide_crossed, norm_hops.value)
    )
    qkv_rows, out_rows = split_columns(late.result(), enc_widths[:2])
    out_padded = jnp.pad(out_rows, ((0, 0), (0, enc_widths[0] - enc_widths[1])))
    norm_sums = norm_hops.finish()
    data_rank = lax.axis_index("dp")
    enc_sum_rows = jnp.concatenate([qkv_rows, out_rows, up_rows, down_rows, bridge_rows], axis=1)
    local_sum = jnp.sum(enc_sum_rows * enc_sum_rows) + jnp.sum(dec_sum_rows * dec_sum_rows)
    square_hops = HopSum(jnp.full((8, 128), local_sum))
    square_hops.step(3)
    tail_rows = (qkv_rows.astype(jnp.bfloat16), out_padded.astype(jnp.bfloat16))
    square_hops.value, tail_rows = lax.optimization_barrier((square_hops.value, tail_rows))
    tail_crossed = cross_pair(*tail_rows)
    squares = square_hops.finish()[0, 0]
    tail_crossed, wide_crossed, squares, norm_sums = lax.optimization_barrier(
        (tail_crossed, wide_crossed, squares, norm_sums)
    )
    squares = squares + jnp.sum(norm_sums * norm_sums)
    tail_parts = line_pair(*tail_crossed, enc_slots[:2])
    wide_parts = line_pair(*wide_crossed, enc_slots[2:4])

    def owned(parts, place):
        whole = assemble(parts, place)
        return jnp.pad(whole, ((0, 0), (0, slot_width - whole.shape[1])))

    late_slots = owned(tail_parts, data_rank // 2)
    wide_slots = owned(wide_parts, data_rank // 2)
    dec_parts = [narrow_all[:, k * half_width : (k + 1) * half_width] for k in range(2)]
    bridge_part = jnp.pad(
        narrow_all[:, slot_width:], ((0, 0), (0, half_width - enc_widths[4]))
    )
    narrow_slots = jnp.where(
        data_rank == dec_slots[0],
        dec_parts[0],
        jnp.where(data_rank == dec_slots[1], dec_parts[1], bridge_part),
    )
    narrow_slots = jnp.pad(narrow_slots, ((0, 0), (0, slot_width - half_width)))
    enc_norm_rows = lax.dynamic_slice_in_dim(norm_sums[:, :D], data_rank * enc_share, enc_share, 1)
    dec_norm_rows = lax.dynamic_slice_in_dim(norm_sums[:, D:], data_rank * dec_share, dec_share, 1)
    def natural(own_chunks):
        return swap_halves(jnp.concatenate(shared(own_chunks), axis=0), chunk_rows, core)

    dec_out_terms, _ = lax.optimization_barrier((dec_out_terms, late.received))
    decoded = [middle + far_sum(term) for middle, term in zip(dec_outs, dec_out_terms)]
    decoded = natural(decoded)
    data_rank = lax.axis_index("dp")

    def is_rank(*slots):
        return functools.reduce(jnp.logical_or, [data_rank == slot for slot in slots])

    lower_row = (jnp.arange(wide_slots.shape[0], dtype=jnp.int32) % enc_rows >= dec_rows)[:, None]
    shifted = jnp.where(
        jnp.logical_and(lower_row, is_rank(*dec_slots)),
        jnp.roll(narrow_slots, half_width, axis=1),
        narrow_slots,
    )
    grad_slots = jnp.where(
        is_rank(*enc_slots[2:4]),
        wide_slots,
        jnp.where(is_rank(*enc_slots[:2]), late_slots, shifted),
    )
    grad_norm = jnp.sqrt(squares)
    factor = clip_bound * lax.rsqrt(squares + 1e-06)
    enc_grad = enc_sum_rows * factor
    dec_grad = dec_sum_rows * factor
    enc_norm_grad = enc_norm_rows * factor
    dec_norm_grad = dec_norm_rows * factor
    dec_shift_grad = dec_norm_grad[3]
    enc_moment_new = momentum_keep * enc_moment + enc_grad
    dec_moment_new = momentum_keep * dec_moment + dec_grad
    enc_norm_moment_new = momentum_keep * enc_norm_moment + enc_norm_grad
    dec_norm_moment_new = momentum_keep * dec_norm_moment + dec_norm_grad
    own = (
        momentum_keep * old_slots.astype(jnp.float32)
        + factor * grad_slots.astype(jnp.float32)
    ).astype(jnp.bfloat16)
    low_blocks, high_blocks = gram_sum(
        lax.dot_general(own, own, (((1,), (1,)), ((), ())), preferred_element_type=jnp.float32)
    )
    orthogonal = newton(low_blocks, high_blocks, own, is_rank(*dec_slots), enc_rows, dec_rows)
    enc_far_sums = [far_sum(term) for term in after(enc_back_terms, low_blocks)]
    enc_far_sums, orthogonal = lax.optimization_barrier((enc_far_sums, orthogonal))
    input_grad = natural(
        block_input_grads(enc_far_sums, enc_middle_grads, enc_firsts, enc_norm_values)
    )
    rows_back = lax.all_to_all(
        orthogonal.reshape(data_ranks, enc_rows, slot_width), "dp", 0, 0
    ).astype(jnp.float32)
    enc_results, dec_results = unslot(rows_back, enc_widths, dec_widths, dec_rows)
    enc_master_new = apply_step(enc_master, enc_results, enc_widths, D, rate_enc, model_ranks)
    dec_master_new = apply_step(dec_master, dec_results, dec_widths, DD, rate_dec, model_ranks)
    enc_norms_new = enc_norms - rate_norm * enc_norm_moment_new
    dec_norms_new = dec_norms - rate_norm * dec_norm_moment_new
    return (
        decoded,
        input_grad,
        enc_grad,
        dec_grad,
        enc_norm_grad,
        dec_norm_grad,
        dec_shift_grad,
        enc_moment_new,
        dec_moment_new,
        enc_norm_moment_new,
        dec_norm_moment_new,
        enc_master_new,
        dec_master_new,
        enc_norms_new,
        dec_norms_new,
        enc_master_new.astype(jnp.bfloat16),
        dec_master_new.astype(jnp.bfloat16),
        enc_norms_new.astype(jnp.bfloat16),
        dec_norms_new.astype(jnp.bfloat16),
        grad_norm,
    )


def solution(mesh):
    return jax.shard_map(
        local,
        mesh=mesh,
        in_specs=(
            P("dp", None),
            P("dp", None),
            P("dp", None),
            P("dp", "mp"),
            P("dp", "mp"),
            P(None, "dp"),
            P(None, "dp"),
            P("dp", "mp"),
            P("dp", "mp"),
            P(None, "dp"),
            P(None, "dp"),
        ),
        out_specs=(
            P("dp", None),
            P("dp", None),
            P("dp", "mp"),
            P("dp", "mp"),
            P(None, "dp"),
            P(None, "dp"),
            P("dp"),
            P("dp", "mp"),
            P("dp", "mp"),
            P(None, "dp"),
            P(None, "dp"),
            P("dp", "mp"),
            P("dp", "mp"),
            P(None, "dp"),
            P(None, "dp"),
            P("dp", "mp"),
            P("dp", "mp"),
            P(None, "dp"),
            P(None, "dp"),
            P(),
        ),
        check_vma=False,
    )
```
